32 devices in a mesh: dp: 4 (over y, x), ctx: 4 (over z), tp: 2 (over core).
Axes of the slice: x: 2, y: 2, z: 4, core: 2. Of those that a mesh axis runs over, the one named last changes fastest.
Arguments:
- query_rows: bfloat16 [32768, 4096], P(('dp', 'ctx'), 'tp'), parts along dimension 0, may hold values from -6 to 6
- key_rows: bfloat16 [32768, 4096], P(('dp', 'ctx'), 'tp'), parts along dimension 0, may hold values from -16 to 16
- value_rows: bfloat16 [32768, 4096], P(('dp', 'ctx'), 'tp'), parts along dimension 0, may hold values from -72 to 72
- gate_rows: bfloat16 [32768, 4096], P(('dp', 'ctx'), 'tp'), parts along dimension 0, may hold values from -8 to 8
- decay_log: float32 [32, 32768], P('tp', ('dp', 'ctx')), parts along dimension 1, may hold values from -1 to 0
- norm_gain: float32 [4096], replicated, may hold values from 0.1 to 1.9
- doc_lengths: int32 [64], P('dp'), parts along dimension 0, may hold values from 1 to 4096, 8192 in all
- block_shard: int32 [128], P('dp'), parts along dimension 0, may hold values from 0 to 3, as said below
Outputs:
- placed: bfloat16 [32768, 4096], P(('dp', 'ctx', 'tp')), parts along dimension 0
The draws below stay inside these ranges and needn't reach their ends.
There are 4 independent parts, one for each index of `dp`. The reference program is written for one: setup_inputs(seed, part) draws one part's arguments, and reference() takes and returns one part's arrays. A program takes and returns all parts, laid end to end along the dimension named above; an argument that names none is the same for every part. Nothing has to cross between parts.
Inputs may be any that keep to these rules, and one draw needn't show every extreme that they name: `doc_lengths`: the 16 lengths sum to 8192; the longest is exactly 4096. `block_shard`: of the 8 blocks of each index of ctx, exactly 2 go to each of the 4 shards.
All inputs are finite; a program needn't handle non-finite values.
Results may differ from the reference program's by a relative error of at most 0.0057.
Values may be sent and summed in bfloat16 or wider, within the bound.
No kernel may reach another device: no remote copies, remote signals or barrier semaphores. Data moves between devices by JAX's collectives and lax.ppermute only.
A program may use at most 192 MiB of HBM per device.

```python
import math
import jax
import jax.numpy as jnp
import numpy as np
from jax import lax

HEADS = 32
HD = 128
F = 4096
BLK = 256
TOKENS = 8192
NBLK = 32
SHARDS = 4
PER_PEER = 2
CB = 512
DOCS = 16
MAXDOC = 4096


def draw_key_rows(key, part):
    base = jax.random.fold_in(key, 11)
    first, second = jax.random.split(base, 2)
    row_scale = jnp.exp(jax.random.uniform(first, (TOKENS, 1), jnp.float32, math.log(0.5), math.log(5.0)))
    entries = jax.random.truncated_normal(second, -4.0, 4.0, (TOKENS, F), jnp.float32) * 0.5
    return (entries * row_scale).astype(jnp.bfloat16)


def draw_value_rows(key, part):
    base = jax.random.fold_in(key, 23)
    first, second = jax.random.split(base, 2)
    head_pos = (jnp.arange(F) // HD).astype(jnp.float32) / max(HEADS - 1, 1)
    head_rise = jnp.exp(0.5 * math.log(3.0) * head_pos)
    column = jnp.exp(jax.random.uniform(first, (1, F), jnp.float32, 0.0, math.log(10.0))) * head_rise[None, :]
    entries = jax.random.truncated_normal(second, -4.0, 4.0, (TOKENS, F), jnp.float32)
    return (entries * column).astype(jnp.bfloat16)


def draw_decay_log(key, part):
    base = jax.random.fold_in(key, 37)
    pick, fast_key, slow_key, rough_key, spot_key, depth_key = jax.random.split(base, 6)
    slow_share = 0.5
    slow = jax.random.uniform(pick, (HEADS, 1), jnp.float32) < slow_share
    fast_rate = jnp.exp(jax.random.uniform(fast_key, (HEADS, 1), jnp.float32, math.log(1.0 / 400.0), math.log(1.0 / 30.0)))
    slow_rate = jnp.exp(jax.random.uniform(slow_key, (HEADS, 1), jnp.float32, math.log(0.05), math.log(0.5))) / TOKENS
    rate = jnp.where(slow, slow_rate, fast_rate)
    rough = jnp.exp(jax.random.uniform(rough_key, (HEADS, TOKENS), jnp.float32, -0.7, 0.7))
    spots = jax.random.randint(spot_key, (HEADS, 2, 1), 0, TOKENS)
    hit = jnp.any(spots == jnp.arange(TOKENS, dtype=jnp.int32)[None, None, :], axis=1)
    depth = jnp.log(jax.random.uniform(depth_key, (HEADS, TOKENS), jnp.float32, 0.5, 0.8))
    return (-rate * rough + jnp.where(hit, depth, 0.0)).astype(jnp.float32)


def shuffle_one(one_key):
    pattern = jnp.repeat(jnp.arange(SHARDS, dtype=jnp.int32), PER_PEER)
    return jax.random.permutation(one_key, pattern)


def draw_block_shard(key, part):
    base = jax.random.fold_in(key, 53)
    source_keys = jax.random.split(base, SHARDS)
    listed = jax.vmap(shuffle_one)(source_keys)
    return listed.reshape(NBLK).astype(jnp.int32)


def steps_of(stream_key, extent, cuts, smallest, high):
    factor_of = 1.0
    for dim, parts in cuts:
        steps = jax.random.uniform(jax.random.fold_in(jax.random.fold_in(stream_key, 6), dim), (parts,), jnp.float32, smallest / len(cuts), high / len(cuts))
        factor_of = factor_of * jnp.repeat(jnp.exp(steps), extent[dim] // parts).reshape((-1,) + (1,) * (len(extent) - 1 - dim))
    return factor_of


def split_up(amount, total, most, lean):
    weights = [(1 << 20) // math.isqrt(grade ** lean) + 1 for grade in range(2, amount + 1)]
    spare, counts = total - most - (amount - 1), [1] * (amount - 1)
    while spare > 0:
        candidates = [i for i in range(amount - 1) if counts[i] < most]
        whole, left = sum([weights[i] for i in candidates]), spare
        for i in candidates:
            extra = min(most - counts[i], max(1, left * weights[i] // whole), spare)
            counts[i] = counts[i] + extra
            spare = spare - extra
    return np.array([most] + counts)


def uneven_parts(rng, count, total, reach, slope):
    if count == 2:
        one = jax.random.randint(rng, (), max(1, total - reach), min(reach, total - 1) + 1)
        return jnp.stack([one, total - one])
    tallies = jnp.asarray(split_up(count, total, reach, slope), jnp.int32)
    twos = (count - 1) // 2
    donor, sink = tallies[1:1 + 2 * twos:2], tallies[2:2 + 2 * twos:2]
    slack = jnp.minimum(donor - 1, reach - sink)
    moved = jax.random.randint(jax.random.fold_in(rng, 1), (twos,), 0, 1 << 20) % (slack + 1)
    tallies = tallies.at[1:1 + 2 * twos:2].set(donor - moved).at[2:2 + 2 * twos:2].set(sink + moved)
    return tallies[jax.random.permutation(jax.random.fold_in(rng, 2), count)]


def centred(key, extent, spread, limit, pieces=(), held_as=jnp.bfloat16):
    values = jax.random.normal(key, extent, jnp.float32) * spread
    if len(pieces) > 0:
        values = steps_of(key, extent, pieces, -0.22, 0.18) * values
    return jnp.clip(values, min=-limit, max=limit).astype(held_as)


def setup_inputs(seed: int = 0, part: int = 0) -> dict:
    arg_keys = jax.random.split(jax.random.key(seed), 9)
    own_keys = jax.random.split(jax.random.fold_in(arg_keys[8], part), 9)
    return {
        "query_rows": centred(own_keys[0], (TOKENS, F), 0.5, 6.0, ((0, 4), (1, 2))),
        "key_rows": draw_key_rows(jax.random.fold_in(jax.random.fold_in(arg_keys[8], part), 71), part),
        "value_rows": draw_value_rows(jax.random.fold_in(jax.random.fold_in(arg_keys[8], part), 71), part),
        "gate_rows": centred(own_keys[3], (TOKENS, F), 2.0, 8.0, ((0, 4), (1, 2))),
        "decay_log": draw_decay_log(jax.random.fold_in(jax.random.fold_in(arg_keys[8], part), 71), part),
        "norm_gain": jnp.clip(1.0 + 0.18 * jax.random.normal(arg_keys[5], (F,), jnp.float32), 0.1, 1.9),
        "doc_lengths": uneven_parts(own_keys[6], DOCS, TOKENS, MAXDOC, 2).astype(jnp.int32),
        "block_shard": draw_block_shard(jax.random.fold_in(jax.random.fold_in(arg_keys[8], part), 71), part),
    }


norm_eps = 1e-05

def doc_positions(doc_lengths, first, length):
    starts = (jnp.cumsum(doc_lengths) - doc_lengths).astype(jnp.int32)
    position = (first + jnp.arange(length, dtype=jnp.int32)).astype(jnp.int32)
    found = lax.optimization_barrier(jnp.sum((position[:, None] >= starts[None, :]).astype(jnp.int32), axis=1))
    return (found - 1).astype(jnp.int32)

def block_terms(query_blk, key_blk, value_blk, decay_blk, doc_blk, doc_before):
    block_len = doc_blk.shape[0]
    cum_decay = jnp.cumsum(decay_blk, axis=1)
    later = jnp.arange(block_len)[:, None] >= jnp.arange(block_len)[None, :]
    allowed = (later & (doc_blk[:, None] == doc_blk[None, :]))[None]
    log_gap = cum_decay[:, :, None] - cum_decay[:, None, :]
    weight = jnp.where(allowed, jnp.exp(jnp.where(allowed, log_gap, 0.0)), 0.0)
    scores = jnp.einsum('thd,jhd->htj', query_blk.astype(jnp.float32), key_blk.astype(jnp.float32))
    weights_low = (scores * weight).astype(jnp.bfloat16)
    intra_sum = jnp.einsum('htj,jhd->thd', weights_low.astype(jnp.float32), value_blk.astype(jnp.float32))
    same_last = (doc_blk == doc_blk[-1])[None, :]
    tail_gate = jnp.where(same_last, jnp.exp(cum_decay[:, -1:] - cum_decay), 0.0)
    scaled_keys = (key_blk.astype(jnp.float32) * tail_gate.T[:, :, None]).astype(jnp.bfloat16)
    update = jnp.einsum('jhd,jhe->hde', scaled_keys.astype(jnp.float32), value_blk.astype(jnp.float32))
    carry_gate = jnp.where(doc_blk[-1] == doc_before, jnp.exp(cum_decay[:, -1]), 0.0)
    entry_gate = jnp.where((doc_blk == doc_before)[None, :], jnp.exp(cum_decay), 0.0)
    return (intra_sum, update, carry_gate, entry_gate)

def reference(query_rows, key_rows, value_rows, gate_rows, decay_log, norm_gain, doc_lengths, block_shard):
    block_count = TOKENS // CB
    doc_ids = doc_positions(doc_lengths, 0, TOKENS)
    doc_shifted = jnp.concatenate([jnp.array([-1], dtype=jnp.int32), doc_ids[:-1]])
    doc_before = doc_shifted.reshape(block_count, CB)[:, 0]
    query_blocks = query_rows.reshape(block_count, CB, HEADS, HD)
    key_blocks = key_rows.reshape(block_count, CB, HEADS, HD)
    value_blocks = value_rows.reshape(block_count, CB, HEADS, HD)
    decay_blocks = decay_log.reshape(HEADS, block_count, CB).transpose(1, 0, 2)
    doc_blocks = doc_ids.reshape(block_count, CB)

    def advance(kv_state, element):
        query_blk, key_blk, value_blk, decay_blk, doc_blk, doc_first = element
        intra_sum, update, carry_gate, entry_gate = block_terms(query_blk, key_blk, value_blk, decay_blk, doc_blk, doc_first)
        reached = jnp.einsum('thd,hde->the', query_blk.astype(jnp.float32), kv_state, precision=lax.Precision.HIGHEST)
        attended = (intra_sum + entry_gate.T[:, :, None] * reached).astype(jnp.bfloat16)
        return (carry_gate[:, None, None] * kv_state + update, attended)
    zero_state = jnp.zeros((HEADS, HD, HD), dtype=jnp.float32)
    final_state, attended = lax.scan(advance, zero_state, (query_blocks, key_blocks, value_blocks, decay_blocks, doc_blocks, doc_before))
    attended_full = attended.reshape(TOKENS, F).astype(jnp.float32)
    mean_square = lax.optimization_barrier(jnp.mean(attended_full * attended_full, axis=1, keepdims=True))
    normed = (attended_full * lax.rsqrt(mean_square + norm_eps) * norm_gain[None, :] * jax.nn.sigmoid(gate_rows.astype(jnp.float32))).astype(jnp.bfloat16)
    block_order = jnp.argsort(block_shard, stable=True)
    return normed.reshape(NBLK, BLK, F)[block_order].reshape(TOKENS, F)
```

```python
import functools

import jax
import jax.numpy as jnp
from jax import lax
from jax.experimental import pallas as pl
from jax.experimental.pallas import tpu as pltpu
from jax.sharding import PartitionSpec as P

BLK = 256
norm_eps = 1e-05
VMEM_LIMIT = 56 * 2**20
F32 = jnp.float32
BF16 = jnp.bfloat16


def params():
    return pltpu.CompilerParams(vmem_limit_bytes=VMEM_LIMIT)


def whole(shape):
    return pl.BlockSpec(shape, lambda *_: (0,) * len(shape))


def pad8(count):
    return -(-count // 8) * 8


def gates_kernel(base_ref, len_ref, decay_ref, rows_ref, cols_ref, docs_ref, total_ref, scr):
    heads, tokens = decay_ref.shape
    hp = pad8(heads)
    chunks = tokens // BLK
    base = base_ref[0]
    starts, run = [], jnp.int32(0)
    for i in range(len_ref.shape[0]):
        starts.append(run)
        run = run + len_ref[i]

    def doc_at(position):
        found = jnp.int32(0)
        for start in starts:
            found = found + (position >= start).astype(jnp.int32)
        return found - 1

    position = base + lax.broadcasted_iota(jnp.int32, (8, tokens), 1)
    doc = jnp.zeros((8, tokens), jnp.int32) - 1
    for start in starts:
        doc = doc + (position >= start).astype(jnp.int32)
    docs_ref[...] = doc.astype(F32)
    edges = [doc_at(base - 1)] + [doc_at(base + (c + 1) * BLK - 1) for c in range(chunks)]

    first = lax.broadcasted_iota(jnp.int32, (BLK, BLK), 0)
    second = lax.broadcasted_iota(jnp.int32, (BLK, BLK), 1)
    upto = jnp.where(first <= second, 1.0, 0.0).astype(F32)
    every = jnp.ones((BLK, BLK), F32)
    scr[...] = jnp.zeros_like(scr)
    cums, sums = [], []
    for c in range(chunks):
        part = decay_ref[:, c * BLK : (c + 1) * BLK]
        cums.append(jnp.dot(part, upto, precision=lax.Precision.HIGHEST, preferred_element_type=F32))
        sums.append(jnp.dot(part, every, precision=lax.Precision.HIGHEST, preferred_element_type=F32))
    after = [None] * chunks
    run = jnp.zeros_like(sums[0])
    for c in reversed(range(chunks)):
        after[c] = run
        run = run + sums[c]
    for c in range(chunks):
        span = slice(c * BLK, (c + 1) * BLK)
        doc_c = doc[:1, span]
        cum, total = cums[c], sums[c]
        rows_ref[0:heads, span] = cum
        rows_ref[hp : hp + heads, span] = jnp.where(doc_c == edges[c + 1], jnp.exp(total - cum), 0.0)
        rows_ref[2 * hp : 2 * hp + heads, span] = jnp.where(
            doc_c == edges[-1], jnp.exp(total - cum + after[c]), 0.0
        )
        rows_ref[3 * hp : 3 * hp + heads, span] = jnp.where(
            edges[c + 1] == edges[c], jnp.exp(total), 0.0
        )
        scr[0:heads, span] = cum
        scr[hp : hp + heads, span] = jnp.where(doc_c == edges[c], jnp.exp(cum), 0.0)
    scr[2 * hp : 2 * hp + 8, :] = doc.astype(F32)
    cols_ref[...] = scr[...].T
    total_ref[...] = jnp.where(edges[-1] == edges[0], jnp.exp(run[:, :128]), 0.0)


def gates(base, doc_lengths, decay):
    heads, tokens = decay.shape
    hp = pad8(heads)
    smem = pl.BlockSpec(memory_space=pltpu.SMEM)
    vmem = pl.BlockSpec(memory_space=pltpu.VMEM)
    return pl.pallas_call(
        gates_kernel,
        in_specs=[smem, smem, vmem],
        out_specs=[vmem] * 4,
        out_shape=[
            jax.ShapeDtypeStruct((4 * hp, tokens), F32),
            jax.ShapeDtypeStruct((tokens, 128), F32),
            jax.ShapeDtypeStruct((8, tokens), F32),
            jax.ShapeDtypeStruct((heads, 128), F32),
        ],
        scratch_shapes=[pltpu.VMEM((128, tokens), F32)],
        compiler_params=params(),
        name="gates",
    )(base, doc_lengths, decay)


def totals_kernel(lo, hp, count, key_ref, value_ref, rows_ref, low_ref, full_ref, acc):
    step = pl.program_id(0)

    @pl.when(step == 0)
    def _():
        acc[...] = jnp.zeros_like(acc)

    for h in range(count):
        cols = slice(h * 128, (h + 1) * 128)
        tail = rows_ref[2 * hp + lo + h : 2 * hp + lo + h + 1, :]
        key_t = key_ref[:, cols].T.astype(F32)
        acc[h] += jnp.dot((key_t * tail).astype(BF16), value_ref[:, cols], preferred_element_type=F32)

    @pl.when(step == pl.num_programs(0) - 1)
    def _():
        low_ref[...] = acc[...].astype(BF16)
        full_ref[...] = acc[...]


def totals(key_rows, value_rows, rows, lo, count):
    tokens = key_rows.shape[0]
    hp = rows.shape[0] // 4
    tile = 2 * BLK
    width = count * 128
    at = lo * 128 // width
    return pl.pallas_call(
        functools.partial(totals_kernel, lo, hp, count),
        grid=(tokens // tile,),
        in_specs=[
            pl.BlockSpec((tile, width), lambda c: (c, at)),
            pl.BlockSpec((tile, width), lambda c: (c, at)),
            pl.BlockSpec((rows.shape[0], tile), lambda c: (0, c)),
        ],
        out_specs=[whole((count, 128, 128))] * 2,
        out_shape=[
            jax.ShapeDtypeStruct((count, 128, 128), BF16),
            jax.ShapeDtypeStruct((count, 128, 128), F32),
        ],
        scratch_shapes=[pltpu.VMEM((count, 128, 128), F32)],
        compiler_params=params(),
        cost_estimate=pl.CostEstimate(
            flops=2 * tokens * 128 * width, bytes_accessed=4 * tokens * width, transcendentals=0
        ),
        name="totals",
    )(key_rows, value_rows, rows)


def attend_kernel(lo, hp, count, ops, *refs):
    (which_ref, _, _, query_ref, key_ref, value_ref, gate_ref, gain_ref, rows_ref, cols_ref, docs_ref, state_ref) = refs[:12]
    outs = refs[12 : 12 + ops]
    square_ref, state, gated, squares = refs[12 + ops :]
    step = pl.program_id(0)

    @pl.when(step == 0)
    def _():
        state[...] = state_ref[...].astype(F32)

    first = lax.broadcasted_iota(jnp.int32, (BLK, BLK), 0)
    second = lax.broadcasted_iota(jnp.int32, (BLK, BLK), 1)
    same = cols_ref[:, 2 * hp : 2 * hp + 1] == docs_ref[0:1, :]
    barred = jnp.where((first >= second) & same, 0.0, -1e30).astype(F32)
    square = jnp.zeros((BLK, 128), F32)
    for h in range(count):
        head = lo + h
        cols = slice(h * 128, (h + 1) * 128)
        query, value = query_ref[:, cols], value_ref[:, cols]
        key_t = key_ref[:, cols].T
        scores = jnp.dot(query, key_t, preferred_element_type=F32)
        gap = cols_ref[:, head : head + 1] - rows_ref[head : head + 1, :] + barred
        weights = (scores * jnp.exp(gap)).astype(BF16)
        intra = jnp.dot(weights, value, preferred_element_type=F32)
        reached = jnp.dot(query, state[h].astype(BF16), preferred_element_type=F32)
        attended = (intra + cols_ref[:, hp + head : hp + head + 1] * reached).astype(BF16).astype(F32)
        scaled = (key_t.astype(F32) * rows_ref[hp + head : hp + head + 1, :]).astype(BF16)
        carry = rows_ref[3 * hp + head : 3 * hp + head + 1, :128]
        state[h] = carry * state[h] + jnp.dot(scaled, value, preferred_element_type=F32)
        square = square + attended * attended
        gated[:, cols] = (
            attended * gain_ref[0:1, cols] * jax.nn.sigmoid(gate_ref[:, cols].astype(F32))
        ).astype(BF16)
    square_ref[0] = jnp.sum(square.T, axis=0, keepdims=True)
    for op in range(ops):

        @pl.when(which_ref[step] == op)
        def _():
            outs[op][0] = gated[...]


def attend(tables, query, key, value, gate, gain, rows, cols, docs, entering, lo, count):
    tokens = query.shape[0]
    chunks = tokens // BLK
    hp = rows.shape[0] // 4
    width = count * 128
    at = lo * 128 // width
    which, place, slot = tables
    ops = place.shape[0] // chunks
    per = chunks // ops
    wide = pl.BlockSpec((BLK, width), lambda c, *_: (c, at))

    def out_map(op, c, which_ref, place_ref, slot_ref):
        return (place_ref[op * chunks + c], 0, 0)

    out = pl.pallas_call(
        functools.partial(attend_kernel, lo, hp, count, ops),
        grid_spec=pltpu.PrefetchScalarGridSpec(
            num_scalar_prefetch=3,
            grid=(chunks,),
            in_specs=[
                wide,
                wide,
                wide,
                wide,
                pl.BlockSpec((1, width), lambda c, *_: (0, at)),
                pl.BlockSpec((rows.shape[0], BLK), lambda c, *_: (0, c)),
                pl.BlockSpec((BLK, 128), lambda c, *_: (c, 0)),
                pl.BlockSpec((8, BLK), lambda c, *_: (0, c)),
                whole((count, 128, 128)),
            ],
            out_specs=[
                pl.BlockSpec((1, BLK, width), functools.partial(out_map, op)) for op in range(ops)
            ]
            + [pl.BlockSpec((1, 1, BLK), lambda c, which_ref, place_ref, slot_ref: (slot_ref[c], 0, 0))],
            scratch_shapes=[
                pltpu.VMEM((count, 128, 128), F32),
                pltpu.VMEM((BLK, width), BF16),
                pltpu.VMEM((8, 128), F32),
            ],
        ),
        out_shape=[jax.ShapeDtypeStruct((per, BLK, width), BF16)] * ops
        + [jax.ShapeDtypeStruct((chunks, 1, BLK), F32)],
        compiler_params=params(),
        cost_estimate=pl.CostEstimate(
            flops=2 * tokens * width * (2 * BLK + 256),
            bytes_accessed=10 * tokens * width,
            transcendentals=tokens * count * (BLK + 128),
        ),
        name="attend",
    )(which, place, slot, query, key, value, gate, gain, rows, cols, docs, entering)
    return out[:ops], out[ops]


def place_kernel(features, pos_ref, piece_ref, square_ref, *refs):
    out_ref = refs[-1]
    scale = lax.rsqrt(square_ref[0] / features + norm_eps)
    scale = jnp.broadcast_to(scale, (128, BLK)).T
    for c in range(out_ref.shape[1] // 128):
        cols = slice(c * 128, (c + 1) * 128)
        out_ref[:, cols] = (piece_ref[0, :, cols].astype(F32) * scale).astype(BF16)


def place(position, piece, square, out, shape, features, unit):
    per, _, width = piece.shape
    in_specs = [
        pl.BlockSpec((1, BLK, unit), lambda k, j, pos: (k, 0, j)),
        pl.BlockSpec((1, 1, BLK), lambda k, j, pos: (k, 0, 0)),
    ]
    operands = [position, piece, square]
    aliases = {}
    if out is not None:
        in_specs.append(pl.BlockSpec(memory_space=pl.ANY))
        operands.append(out)
        aliases = {3: 0}
    return pl.pallas_call(
        functools.partial(place_kernel, features),
        grid_spec=pltpu.PrefetchScalarGridSpec(
            num_scalar_prefetch=1,
            grid=(per, width // unit),
            in_specs=in_specs,
            out_specs=pl.BlockSpec((BLK, unit), lambda k, j, pos: (pos[0] + k, pos[1] + j)),
        ),
        out_shape=jax.ShapeDtypeStruct(shape, BF16),
        input_output_aliases=aliases,
        compiler_params=params(),
        cost_estimate=pl.CostEstimate(
            flops=per * BLK * width, bytes_accessed=4 * per * BLK * width, transcendentals=0
        ),
        name="place",
    )(*operands)


def local(query_rows, key_rows, value_rows, gate_rows, decay_log, norm_gain, doc_lengths, block_shard):
    tokens, width = query_rows.shape
    heads = decay_log.shape[0]
    chunks = tokens // BLK
    features = norm_gain.shape[0]
    n, t = lax.axis_size("ctx"), lax.axis_size("tp")
    stride = n // t
    per = chunks // n
    ctx, tp = lax.axis_index("ctx"), lax.axis_index("tp")
    quarter = max(1, heads // 4)
    groups = [(lo, quarter) for lo in range(0, heads, quarter)]

    base = (ctx * tokens).astype(jnp.int32).reshape(1)
    rows, cols, docs, total_gate = gates(base, doc_lengths, decay_log)

    shards = lax.dynamic_slice_in_dim(block_shard, ctx * chunks, chunks)
    which = jnp.mod(shards - ctx - tp * stride, n).astype(jnp.int32)
    index = jnp.arange(chunks)
    earlier = index[None, :] < index[:, None]
    ranks = jnp.sum((earlier & (which[None, :] == which[:, None])).astype(jnp.int32), axis=1)
    seen = jnp.sum(
        (earlier[None] & (which[None, None, :] == jnp.arange(n)[:, None, None])).astype(jnp.int32), axis=2
    )
    tables = (which, jnp.minimum(seen, per - 1).reshape(-1), which * per + jnp.minimum(ranks, per - 1))
    gain = lax.dynamic_slice_in_dim(norm_gain, tp * width, width).reshape(1, width)

    hop = [(i, i + 1) for i in range(n - 1)]

    def route(op):
        return [
            (d * t + k, (d + op + k * stride) % n * t + d // stride) for d in range(n) for k in range(t)
        ]

    pieces, squares = [], None
    for lo, count in groups:
        low, full = totals(key_rows, value_rows, rows, lo, count)
        carry = total_gate[lo : lo + count, :1, None]
        entering = lax.ppermute(low, "ctx", hop)
        for _ in range(max(1, n // 2) - 1):
            entering = lax.ppermute((carry * entering.astype(F32) + full).astype(BF16), "ctx", hop)
        outs, square = attend(
            tables, query_rows, key_rows, value_rows, gate_rows, gain, rows, cols, docs, entering, lo, count
        )
        squares = square if squares is None else squares + square
        pieces.append([lax.ppermute(outs[op], ("ctx", "tp"), route(op)) for op in range(n)])

    halves = [
        lax.ppermute(squares[op * per : (op + 1) * per], ("ctx", "tp"), route(op)) for op in range(n)
    ]
    joined = [sum(halves[op + k * stride] for k in range(t)) for op in range(stride)]

    unit = quarter * 128
    shape = (tokens // t, features)
    out = None
    for (lo, count), received in zip(groups, pieces):
        for op in range(n):
            lane = jnp.mod(ctx - op, stride)
            source = tp * stride + lane
            half = jnp.mod(ctx - op - source, n) // stride
            position = jnp.stack([lane * per, (half * width + lo * 128) // unit]).astype(jnp.int32)
            out = place(position, received[op], joined[op % stride], out, shape, features, unit)
    return out


def solution(mesh):
    return jax.shard_map(
        local,
        mesh=mesh,
        in_specs=(
            P(("dp", "ctx"), "tp"),
            P(("dp", "ctx"), "tp"),
            P(("dp", "ctx"), "tp"),
            P(("dp", "ctx"), "tp"),
            P("tp", ("dp", "ctx")),
            P(),
            P("dp"),
            P("dp"),
        ),
        out_specs=P(("dp", "ctx", "tp"), None),
        check_vma=False,
    )
```

```python
import functools

import jax
import jax.numpy as jnp
from jax import lax
from jax.experimental import pallas as pl
from jax.experimental.pallas import tpu as pltpu
from jax.sharding import PartitionSpec as P

BLK = 256
norm_eps = 1e-05
VMEM_LIMIT = 56 * 2**20
F32 = jnp.float32
BF16 = jnp.bfloat16


def params():
    return pltpu.CompilerParams(vmem_limit_bytes=VMEM_LIMIT)


def whole(shape):
    return pl.BlockSpec(shape, lambda *_: (0,) * len(shape))


def pad8(count):
    return -(-count // 8) * 8


class Table:
    def __init__(self, n, t, chunks):
        self.n, self.t, self.chunks = n, t, chunks
        self.stride, self.per = n // t, chunks // n
        self.half = 0
        self.which = 1
        self.slot = self.which + chunks
        self.place = self.slot + chunks
        self.row = self.place + n * chunks
        self.side = self.row + n
        self.source = self.side + n
        self.square = self.source + n
        self.size = self.square + n * t


def fill_table(tab, shard_ref, table_ref):
    n, t, per, chunks = tab.n, tab.t, tab.per, tab.chunks
    ctx, tp = lax.axis_index("ctx"), lax.axis_index("tp")
    table_ref[tab.half] = tp
    seen = [jnp.int32(0)] * n
    for c in range(chunks):
        shard = shard_ref[ctx * chunks + c]
        op = lax.rem(shard - ctx - tp * tab.stride + 2 * n, n)
        table_ref[tab.which + c] = op
        rank = jnp.int32(0)
        for k in range(n):
            table_ref[tab.place + k * chunks + c] = jnp.minimum(seen[k], per - 1)
            here = (op == k).astype(jnp.int32)
            rank = rank + here * seen[k]
            seen[k] = seen[k] + here
        table_ref[tab.slot + c] = op * per + jnp.minimum(rank, per - 1)
    for op in range(n):
        lane = lax.rem(ctx - op + n, tab.stride)
        source = tp * tab.stride + lane
        table_ref[tab.row + op] = lane * per
        table_ref[tab.side + op] = lax.rem(ctx - op - source + 2 * n, n) // tab.stride
        table_ref[tab.source + op] = source
        for k in range(t):
            table_ref[tab.square + op * t + k] = lax.rem(ctx - source - k * tab.stride + 2 * n, n) * per


def gates_kernel(tab, len_ref, shard_ref, decay_ref, rows_ref, cols_ref, docs_ref, total_ref, table_ref, scr):
    fill_table(tab, shard_ref, table_ref)
    heads, tokens = decay_ref.shape
    hp = pad8(heads)
    chunks = tokens // BLK
    base = lax.axis_index("ctx") * tokens
    starts, run = [], jnp.int32(0)
    for i in range(len_ref.shape[0]):
        starts.append(run)
        run = run + len_ref[i]

    def doc_at(position):
        found = jnp.int32(0)
        for start in starts:
            found = found + (position >= start).astype(jnp.int32)
        return found - 1

    position = base + lax.broadcasted_iota(jnp.int32, (8, tokens), 1)
    doc = jnp.zeros((8, tokens), jnp.int32) - 1
    for start in starts:
        doc = doc + (position >= start).astype(jnp.int32)
    docs_ref[...] = doc.astype(F32)
    edges = [doc_at(base - 1)] + [doc_at(base + (c + 1) * BLK - 1) for c in range(chunks)]

    first = lax.broadcasted_iota(jnp.int32, (BLK, BLK), 0)
    second = lax.broadcasted_iota(jnp.int32, (BLK, BLK), 1)
    upto = jnp.where(first <= second, 1.0, 0.0).astype(F32)
    every = jnp.ones((BLK, BLK), F32)
    scr[...] = jnp.zeros_like(scr)
    cums, sums = [], []
    for c in range(chunks):
        part = decay_ref[:, c * BLK : (c + 1) * BLK]
        cums.append(jnp.dot(part, upto, precision=lax.Precision.HIGHEST, preferred_element_type=F32))
        sums.append(jnp.dot(part, every, precision=lax.Precision.HIGHEST, preferred_element_type=F32))
    after = [None] * chunks
    run = jnp.zeros_like(sums[0])
    for c in reversed(range(chunks)):
        after[c] = run
        run = run + sums[c]
    for c in range(chunks):
        span = slice(c * BLK, (c + 1) * BLK)
        doc_c = doc[:1, span]
        cum, total = cums[c], sums[c]
        rows_ref[0:heads, span] = cum
        rows_ref[hp : hp + heads, span] = jnp.where(doc_c == edges[c + 1], jnp.exp(total - cum), 0.0)
        rows_ref[2 * hp : 2 * hp + heads, span] = jnp.where(
            doc_c == edges[-1], jnp.exp(total - cum + after[c]), 0.0
        )
        rows_ref[3 * hp : 3 * hp + heads, span] = jnp.where(
            edges[c + 1] == edges[c], jnp.exp(total), 0.0
        )
        scr[0:heads, span] = cum
        scr[hp : hp + heads, span] = jnp.where(doc_c == edges[c], jnp.exp(cum), 0.0)
    scr[2 * hp : 2 * hp + 8, :] = doc.astype(F32)
    cols_ref[...] = scr[...].T
    total_ref[...] = jnp.where(edges[-1] == edges[0], jnp.exp(run[:, :128]), 0.0)


def gates(tab, doc_lengths, block_shard, decay):
    heads, tokens = decay.shape
    hp = pad8(heads)
    smem = pl.BlockSpec(memory_space=pltpu.SMEM)
    vmem = pl.BlockSpec(memory_space=pltpu.VMEM)
    return pl.pallas_call(
        functools.partial(gates_kernel, tab),
        in_specs=[smem, smem, vmem],
        out_specs=[vmem] * 4 + [smem],
        out_shape=[
            jax.ShapeDtypeStruct((4 * hp, tokens), F32),
            jax.ShapeDtypeStruct((tokens, 128), F32),
            jax.ShapeDtypeStruct((8, tokens), F32),
            jax.ShapeDtypeStruct((heads, 128), F32),
            jax.ShapeDtypeStruct((tab.size,), jnp.int32),
        ],
        scratch_shapes=[pltpu.VMEM((128, tokens), F32)],
        compiler_params=params(),
        name="gates",
    )(doc_lengths, block_shard, decay)


def totals_kernel(lo, hp, count, key_ref, value_ref, rows_ref, low_ref, full_ref, acc):
    step = pl.program_id(0)

    @pl.when(step == 0)
    def _():
        acc[...] = jnp.zeros_like(acc)

    for h in range(count):
        cols = slice(h * 128, (h + 1) * 128)
        tail = rows_ref[2 * hp + lo + h : 2 * hp + lo + h + 1, :]
        key_t = key_ref[:, cols].T.astype(F32)
        acc[h] += jnp.dot((key_t * tail).astype(BF16), value_ref[:, cols], preferred_element_type=F32)

    @pl.when(step == pl.num_programs(0) - 1)
    def _():
        low_ref[...] = acc[...].astype(BF16)
        full_ref[...] = acc[...]


def totals(key_rows, value_rows, rows, lo, count):
    tokens = key_rows.shape[0]
    hp = rows.shape[0] // 4
    tile = 2 * BLK
    width = count * 128
    at = lo * 128 // width
    return pl.pallas_call(
        functools.partial(totals_kernel, lo, hp, count),
        grid=(tokens // tile,),
        in_specs=[
            pl.BlockSpec((tile, width), lambda c: (c, at)),
            pl.BlockSpec((tile, width), lambda c: (c, at)),
            pl.BlockSpec((rows.shape[0], tile), lambda c: (0, c)),
        ],
        out_specs=[whole((count, 128, 128))] * 2,
        out_shape=[
            jax.ShapeDtypeStruct((count, 128, 128), BF16),
            jax.ShapeDtypeStruct((count, 128, 128), F32),
        ],
        scratch_shapes=[pltpu.VMEM((count, 128, 128), F32)],
        compiler_params=params(),
        cost_estimate=pl.CostEstimate(
            flops=2 * tokens * 128 * width, bytes_accessed=4 * tokens * width, transcendentals=0
        ),
        name="totals",
    )(key_rows, value_rows, rows)


def attend_kernel(tab, lo, hp, count, chain, *refs):
    ops = tab.n
    (table_ref, query_ref, key_ref, value_ref, gate_ref, gain_ref, rows_ref, cols_ref, docs_ref, state_ref) = refs[:10]
    outs = refs[10 + chain : 10 + chain + ops]
    square_ref, state, gated = refs[10 + chain + ops :]
    step = pl.program_id(0)

    @pl.when(step == 0)
    def _():
        state[...] = state_ref[...].astype(F32)

    first = lax.broadcasted_iota(jnp.int32, (BLK, BLK), 0)
    second = lax.broadcasted_iota(jnp.int32, (BLK, BLK), 1)
    same = cols_ref[:, 2 * hp : 2 * hp + 1] == docs_ref[0:1, :]
    barred = jnp.where((first >= second) & same, 0.0, -1e30).astype(F32)
    square = jnp.zeros((BLK, 128), F32)
    for h in range(count):
        head = lo + h
        cols = slice(h * 128, (h + 1) * 128)
        query, value = query_ref[:, cols], value_ref[:, cols]
        key_t = key_ref[:, cols].T
        scores = jnp.dot(query, key_t, preferred_element_type=F32)
        gap = cols_ref[:, head : head + 1] - rows_ref[head : head + 1, :] + barred
        weights = (scores * jnp.exp(gap)).astype(BF16)
        intra = jnp.dot(weights, value, preferred_element_type=F32)
        reached = jnp.dot(query, state[h].astype(BF16), preferred_element_type=F32)
        attended = (intra + cols_ref[:, hp + head : hp + head + 1] * reached).astype(BF16).astype(F32)
        scaled = (key_t.astype(F32) * rows_ref[hp + head : hp + head + 1, :]).astype(BF16)
        carry = rows_ref[3 * hp + head : 3 * hp + head + 1, :128]
        state[h] = carry * state[h] + jnp.dot(scaled, value, preferred_element_type=F32)
        square = square + attended * attended
        gated[:, cols] = (
            attended * gain_ref[0:1, cols] * jax.nn.sigmoid(gate_ref[:, cols].astype(F32))
        ).astype(BF16)
    total = jnp.sum(square.T, axis=0, keepdims=True)
    square_ref[0] = total + refs[10][0] if chain else total
    which = table_ref[tab.which + step]
    for op in range(ops):

        @pl.when(which == op)
        def _():
            outs[op][0] = gated[...]


def attend(tab, table, query, key, value, gate, gain, rows, cols, docs, entering, base, lo, count, squares):
    tokens, local_width = query.shape
    chunks, ops, per = tab.chunks, tab.n, tab.per
    hp = rows.shape[0] // 4
    width = count * 128
    at = lo * 128 // width
    chain = squares is not None
    wide = pl.BlockSpec((BLK, width), lambda c, tbl: (c, at))
    square_spec = pl.BlockSpec((1, 1, BLK), lambda c, tbl: (tbl[tab.slot + c], 0, 0))

    def out_map(op, c, tbl):
        return (tbl[tab.place + op * chunks + c], 0, 0)

    out = pl.pallas_call(
        functools.partial(attend_kernel, tab, lo, hp, count, int(chain)),
        grid_spec=pltpu.PrefetchScalarGridSpec(
            num_scalar_prefetch=1,
            grid=(chunks,),
            in_specs=[
                wide,
                wide,
                wide,
                wide,
                pl.BlockSpec((1, width), lambda c, tbl: (0, tbl[tab.half] * (local_width // width) + at)),
                pl.BlockSpec((rows.shape[0], BLK), lambda c, tbl: (0, c)),
                pl.BlockSpec((BLK, 128), lambda c, tbl: (c, 0)),
                pl.BlockSpec((8, BLK), lambda c, tbl: (0, c)),
                pl.BlockSpec((count, 128, 128), lambda c, tbl: ((lo - base) // count, 0, 0)),
            ]
            + [square_spec] * chain,
            out_specs=[
                pl.BlockSpec((1, BLK, width), functools.partial(out_map, op)) for op in range(ops)
            ]
            + [square_spec],
            scratch_shapes=[
                pltpu.VMEM((count, 128, 128), F32),
                pltpu.VMEM((BLK, width), BF16),
            ],
        ),
        out_shape=[jax.ShapeDtypeStruct((per, BLK, width), BF16)] * ops
        + [jax.ShapeDtypeStruct((chunks, 1, BLK), F32)],
        compiler_params=params(),
        cost_estimate=pl.CostEstimate(
            flops=2 * tokens * width * (2 * BLK + 256),
            bytes_accessed=10 * tokens * width,
            transcendentals=tokens * count * (BLK + 128),
        ),
        name="attend",
    )(table, query, key, value, gate, gain, rows, cols, docs, entering, *([squares] if chain else []))
    return out[:ops], out[ops]


def place_kernel(features, t, table_ref, piece_ref, *refs):
    out_ref = refs[-1]
    square = refs[0][0, 0]
    for k in range(1, t):
        square = square + refs[k][0, 0]
    scale = lax.rsqrt(square / features + norm_eps)
    scale = jnp.broadcast_to(scale, (128, BLK)).T
    for c in range(out_ref.shape[1] // 128):
        cols = slice(c * 128, (c + 1) * 128)
        out_ref[:, cols] = (piece_ref[0, :, cols].astype(F32) * scale).astype(BF16)


def place(tab, table, op, lo, piece, squares, out, shape, local_width, features, unit):
    per, _, width = piece.shape
    t = tab.t

    def square_map(k, c, j, tbl):
        return (tbl[tab.source + op] * t + k, tbl[tab.square + op * t + k] + c, 0, 0)

    def out_map(c, j, tbl):
        return (tbl[tab.row + op] + c, (tbl[tab.side + op] * local_width + lo * 128) // unit + j)

    in_specs = [pl.BlockSpec((1, BLK, unit), lambda c, j, tbl: (c, 0, j))]
    in_specs += [pl.BlockSpec((1, 1, 1, BLK), functools.partial(square_map, k)) for k in range(t)]
    operands = [table, piece] + [squares] * t
    aliases = {}
    if out is not None:
        in_specs.append(pl.BlockSpec(memory_space=pl.ANY))
        operands.append(out)
        aliases = {len(operands) - 1: 0}
    return pl.pallas_call(
        functools.partial(place_kernel, features, t),
        grid_spec=pltpu.PrefetchScalarGridSpec(
            num_scalar_prefetch=1,
            grid=(per, width // unit),
            in_specs=in_specs,
            out_specs=pl.BlockSpec((BLK, unit), out_map),
        ),
        out_shape=jax.ShapeDtypeStruct(shape, BF16),
        input_output_aliases=aliases,
        compiler_params=params(),
        cost_estimate=pl.CostEstimate(
            flops=per * BLK * width, bytes_accessed=4 * per * BLK * width, transcendentals=0
        ),
        name="place",
    )(*operands)


def local(query_rows, key_rows, value_rows, gate_rows, decay_log, norm_gain, doc_lengths, block_shard):
    tokens, width = query_rows.shape
    heads = decay_log.shape[0]
    features = norm_gain.shape[0]
    n, t = lax.axis_size("ctx"), lax.axis_size("tp")
    tab = Table(n, t, tokens // BLK)
    quarter = max(1, heads // 4)

    rows, cols, docs, total_gate, table = gates(tab, doc_lengths, block_shard, decay_log)
    gain = norm_gain.reshape(1, features)
    hop = [(i, i + 1) for i in range(n - 1)]

    def route(op):
        return [
            (d * t + k, (d + op + k * tab.stride) % n * t + d // tab.stride)
            for d in range(n)
            for k in range(t)
        ]

    def enter(lo, count):
        low, full = totals(key_rows, value_rows, rows, lo, count)
        carry = total_gate[lo : lo + count, :1, None]
        entering = lax.ppermute(low, "ctx", hop)
        for _ in range(max(1, n // 2) - 1):
            entering = lax.ppermute((carry * entering.astype(F32) + full).astype(BF16), "ctx", hop)
        return entering

    rest = heads - quarter
    entering = {rest: enter(rest, quarter), 0: enter(0, rest)}
    groups = [(rest, quarter, rest), (0, 2 * quarter, 0), (2 * quarter, quarter, 0)]
    gated, squares = [], None
    for lo, count, base in groups:
        outs, squares = attend(
            tab, table, query_rows, key_rows, value_rows, gate_rows, gain, rows, cols, docs,
            entering[base], base, lo, count, squares,
        )
        gated.append(outs)
    squares = lax.all_gather(squares, ("ctx", "tp"))

    unit = quarter * 128
    shape = (tokens // t, features)
    out = None
    pieces = [[lax.ppermute(gated[g][op], ("ctx", "tp"), route(op)) for op in range(n)] for g in range(2)]
    for g in range(3):
        if g == 1:
            sent = []
            for op in range(n):
                ready, out = lax.optimization_barrier((gated[2][op], out))
                sent.append(lax.ppermute(ready, ("ctx", "tp"), route(op)))
            pieces.append(sent)
        for op in range(n):
            out = place(tab, table, op, groups[g][0], pieces[g][op], squares, out, shape, width, features, unit)
    return out


def solution(mesh):
    return jax.shard_map(
        local,
        mesh=mesh,
        in_specs=(
            P(("dp", "ctx"), "tp"),
            P(("dp", "ctx"), "tp"),
            P(("dp", "ctx"), "tp"),
            P(("dp", "ctx"), "tp"),
            P("tp", ("dp", "ctx")),
            P(),
            P("dp"),
            P("dp"),
        ),
        out_specs=P(("dp", "ctx", "tp"), None),
        check_vma=False,
    )
```

```python
import functools

import jax
import jax.numpy as jnp
from jax import lax
from jax.experimental import pallas as pl
from jax.experimental.pallas import tpu as pltpu
from jax.sharding import PartitionSpec as P

BLK = 256
norm_eps = 1e-05
VMEM_LIMIT = 56 * 2**20
F32 = jnp.float32
BF16 = jnp.bfloat16


def params(limit=VMEM_LIMIT):
    return pltpu.CompilerParams(vmem_limit_bytes=limit)


def whole(shape):
    return pl.BlockSpec(shape, lambda *_: (0,) * len(shape))


def extra_rows(width):
    lanes = min(width, BLK)
    return lanes, BLK // lanes


def pad8(count):
    return -(-count // 8) * 8


class Table:
    def __init__(self, n, t, chunks):
        self.n, self.t, self.chunks = n, t, chunks
        self.stride, self.per = n // t, chunks // n
        self.half = 0
        self.which = 1
        self.slot = self.which + chunks
        self.place = self.slot + chunks
        self.row = self.place + n * chunks
        self.side = self.row + n
        self.shard = self.side + n
        self.size = self.shard + chunks


def fill_table(tab, shard_ref, table_ref):
    n, per, chunks = tab.n, tab.per, tab.chunks
    ctx, tp = lax.axis_index("ctx"), lax.axis_index("tp")
    table_ref[tab.half] = tp
    seen = [jnp.int32(0)] * n
    for c in range(chunks):
        shard = shard_ref[ctx * chunks + c]
        op = lax.rem(shard - ctx - tp * tab.stride + 2 * n, n)
        table_ref[tab.which + c] = op
        rank = jnp.int32(0)
        for k in range(n):
            table_ref[tab.place + k * chunks + c] = jnp.minimum(seen[k], per - 1)
            here = (op == k).astype(jnp.int32)
            rank = rank + here * seen[k]
            seen[k] = seen[k] + here
        table_ref[tab.slot + c] = op * per + jnp.minimum(rank, per - 1)
        table_ref[tab.shard + c] = shard * per + jnp.minimum(rank, per - 1)
    for op in range(n):
        lane = lax.rem(ctx - op + n, tab.stride)
        source = tp * tab.stride + lane
        table_ref[tab.row + op] = lane * per
        table_ref[tab.side + op] = lax.rem(ctx - op - source + 2 * n, n) // tab.stride


def fill_gates(len_ref, decay_ref, rows_ref, cols_ref, docs_ref, total_ref, tail_ref, scr):
    heads, tokens = decay_ref.shape
    hp = pad8(heads)
    chunks = tokens // BLK
    base = lax.axis_index("ctx") * tokens
    starts, run = [], jnp.int32(0)
    for i in range(len_ref.shape[0]):
        starts.append(run)
        run = run + len_ref[i]

    def doc_at(position):
        found = jnp.int32(0)
        for start in starts:
            found = found + (position >= start).astype(jnp.int32)
        return found - 1

    position = base + lax.broadcasted_iota(jnp.int32, (8, tokens), 1)
    doc = jnp.zeros((8, tokens), jnp.int32) - 1
    for start in starts:
        doc = doc + (position >= start).astype(jnp.int32)
    docs_ref[...] = doc.astype(F32)
    edges = [doc_at(base - 1)] + [doc_at(base + (c + 1) * BLK - 1) for c in range(chunks)]

    first = lax.broadcasted_iota(jnp.int32, (BLK, BLK), 0)
    second = lax.broadcasted_iota(jnp.int32, (BLK, BLK), 1)
    upto = jnp.where(first <= second, 1.0, 0.0).astype(F32)
    every = jnp.ones((BLK, BLK), F32)
    scr[...] = jnp.zeros_like(scr)
    cums, sums = [], []
    for c in range(chunks):
        part = decay_ref[:, c * BLK : (c + 1) * BLK]
        cums.append(jnp.dot(part, upto, precision=lax.Precision.HIGHEST, preferred_element_type=F32))
        sums.append(jnp.dot(part, every, precision=lax.Precision.HIGHEST, preferred_element_type=F32))
    before, after = [], [None] * chunks
    run = jnp.zeros_like(sums[0])
    for c in range(chunks):
        before.append(run)
        run = run + sums[c]
    run = jnp.zeros_like(sums[0])
    for c in reversed(range(chunks)):
        after[c] = run
        run = run + sums[c]
    for c in range(chunks):
        span = slice(c * BLK, (c + 1) * BLK)
        doc_c = doc[:1, span]
        cum, total = cums[c], sums[c]
        rows_ref[0:heads, span] = cum
        rows_ref[hp : hp + heads, span] = jnp.where(doc_c == edges[c + 1], jnp.exp(total - cum), 0.0)
        tail_ref[0:heads, span] = jnp.where(doc_c == edges[-1], jnp.exp(total - cum + after[c]), 0.0)
        rows_ref[2 * hp : 2 * hp + heads, span] = jnp.where(
            edges[c + 1] == edges[c], jnp.exp(total), 0.0
        )
        scr[0:heads, span] = cum
        scr[hp : hp + heads, span] = jnp.where(doc_c == edges[c], jnp.exp(cum), 0.0)
        scr[2 * hp + 8 : 2 * hp + 8 + heads, span] = jnp.where(
            doc_c == edges[0], jnp.exp(before[c] + cum), 0.0
        )
    scr[2 * hp : 2 * hp + 8, :] = doc.astype(F32)
    cols_ref[...] = scr[...].T
    total_ref[...] = jnp.where(edges[-1] == edges[0], jnp.exp(run[:, :128]), 0.0)


def prelude_kernel(tab, splits, len_ref, shard_ref, decay_ref, key_ref, value_ref, *refs):
    rows_ref, cols_ref, docs_ref, total_ref, table_ref = refs[:5]
    lows, fulls = refs[5 : 5 + len(splits)], refs[5 + len(splits) : 5 + 2 * len(splits)]
    tail_ref, scr, acc = refs[5 + 2 * len(splits) :]
    step = pl.program_id(0)
    tile = key_ref.shape[0]

    @pl.when(step == 0)
    def _():
        fill_table(tab, shard_ref, table_ref)
        fill_gates(len_ref, decay_ref, rows_ref, cols_ref, docs_ref, total_ref, tail_ref, scr)
        acc[...] = jnp.zeros_like(acc)

    tails = tail_ref[:, pl.ds(pl.multiple_of(step * tile, tile), tile)]
    for h in range(acc.shape[0]):
        cols = slice(h * 128, (h + 1) * 128)
        scaled = (key_ref[:, cols].T.astype(F32) * tails[h : h + 1, :]).astype(BF16)
        acc[h] += jnp.dot(scaled, value_ref[:, cols], preferred_element_type=F32)

    @pl.when(step == pl.num_programs(0) - 1)
    def _():
        for (lo, count), low_ref, full_ref in zip(splits, lows, fulls):
            low_ref[...] = acc[lo : lo + count].astype(BF16)
            full_ref[...] = acc[lo : lo + count]


def prelude(tab, splits, doc_lengths, block_shard, decay, key, value):
    heads, tokens = decay.shape
    hp = pad8(heads)
    tile = 2 * BLK
    smem = pl.BlockSpec(memory_space=pltpu.SMEM)
    shapes = [(3 * hp, tokens), (tokens, 128), (8, tokens), (heads, 128)]
    states = [(count, 128, 128) for _, count in splits]
    wide = pl.BlockSpec((tile, key.shape[1]), lambda c: (c, 0))
    return pl.pallas_call(
        functools.partial(prelude_kernel, tab, splits),
        grid=(tokens // tile,),
        in_specs=[smem, smem, whole(decay.shape), wide, wide],
        out_specs=[whole(shape) for shape in shapes] + [smem] + [whole(shape) for shape in states * 2],
        out_shape=[jax.ShapeDtypeStruct(shape, F32) for shape in shapes]
        + [jax.ShapeDtypeStruct((tab.size,), jnp.int32)]
        + [jax.ShapeDtypeStruct(shape, BF16) for shape in states]
        + [jax.ShapeDtypeStruct(shape, F32) for shape in states],
        scratch_shapes=[
            pltpu.VMEM((hp, tokens), F32),
            pltpu.VMEM((128, tokens), F32),
            pltpu.VMEM((heads, 128, 128), F32),
        ],
        compiler_params=params(),
        name="prelude",
    )(doc_lengths, block_shard, decay, key, value)


def barred_pairs(hp, cols_ref, docs_ref):
    first = lax.broadcasted_iota(jnp.int32, (BLK, BLK), 0)
    second = lax.broadcasted_iota(jnp.int32, (BLK, BLK), 1)
    same = cols_ref[:, 2 * hp : 2 * hp + 1] == docs_ref[0:1, :]
    return jnp.where((first >= second) & same, 0.0, -1e30).astype(F32)


def chunk_of_head(h, head, hp, barred, query_ref, key_ref, value_ref, rows_ref, cols_ref, state):
    cols = slice(h * 128, (h + 1) * 128)
    query, value = query_ref[:, cols], value_ref[:, cols]
    key_t = key_ref[:, cols].T
    scores = jnp.dot(query, key_t, preferred_element_type=F32)
    gap = cols_ref[:, head : head + 1] - rows_ref[head : head + 1, :] + barred
    weights = (scores * jnp.exp(gap)).astype(BF16)
    intra = jnp.dot(weights, value, preferred_element_type=F32)
    reached = jnp.dot(query, state[h].astype(BF16), preferred_element_type=F32)
    scaled = (key_t.astype(F32) * rows_ref[hp + head : hp + head + 1, :]).astype(BF16)
    carry = rows_ref[2 * hp + head : 2 * hp + head + 1, :128]
    state[h] = carry * state[h] + jnp.dot(scaled, value, preferred_element_type=F32)
    return intra + cols_ref[:, hp + head : hp + head + 1] * reached


def gate_head(h, attended, square, gain_ref, gate_ref, gated):
    cols = slice(h * 128, (h + 1) * 128)
    attended = attended.astype(BF16).astype(F32)
    gated[:BLK, cols] = (
        attended * gain_ref[0:1, cols] * jax.nn.sigmoid(gate_ref[:, cols].astype(F32))
    ).astype(BF16)
    return square + attended * attended


def own_kernel(lo, hp, count, query_ref, key_ref, value_ref, rows_ref, cols_ref, docs_ref, own_ref, state):
    @pl.when(pl.program_id(0) == 0)
    def _():
        state[...] = jnp.zeros_like(state)

    barred = barred_pairs(hp, cols_ref, docs_ref)
    for h in range(count):
        own_ref[:, h * 128 : (h + 1) * 128] = chunk_of_head(
            h, lo + h, hp, barred, query_ref, key_ref, value_ref, rows_ref, cols_ref, state
        )


def attend_own(query, key, value, rows, cols, docs, lo, count):
    tokens = query.shape[0]
    hp = rows.shape[0] // 3
    width = count * 128
    at = lo * 128 // width
    wide = pl.BlockSpec((BLK, width), lambda c: (c, at))
    return pl.pallas_call(
        functools.partial(own_kernel, lo, hp, count),
        grid=(tokens // BLK,),
        in_specs=[
            wide,
            wide,
            wide,
            pl.BlockSpec((rows.shape[0], BLK), lambda c: (0, c)),
            pl.BlockSpec((BLK, 128), lambda c: (c, 0)),
            pl.BlockSpec((8, BLK), lambda c: (0, c)),
        ],
        out_specs=pl.BlockSpec((BLK, width), lambda c: (c, 0)),
        out_shape=jax.ShapeDtypeStruct((tokens, width), F32),
        scratch_shapes=[pltpu.VMEM((count, 128, 128), F32)],
        compiler_params=params(),
        cost_estimate=pl.CostEstimate(
            flops=8 * tokens * width * BLK, bytes_accessed=10 * tokens * width, transcendentals=0
        ),
        name="attend_own",
    )(query, key, value, rows, cols, docs)


def enter_kernel(tab, lo, hp, count, table_ref, query_ref, own_ref, gate_ref, gain_ref, cols_ref, state_ref, out_ref, square_ref):
    square = jnp.zeros((BLK, 128), F32)
    for h in range(count):
        cols = slice(h * 128, (h + 1) * 128)
        reached = jnp.dot(query_ref[:, cols], state_ref[h], preferred_element_type=F32)
        column = 2 * hp + 8 + lo + h
        attended = own_ref[:, cols] + cols_ref[:, column : column + 1] * reached
        square = gate_head(h, attended, square, gain_ref, gate_ref, out_ref.at[0])
    square_ref[0] = jnp.sum(square.T, axis=0, keepdims=True)


def attend_entered(tab, table, query, own, gate, gain, cols, entering, lo, count, hp):
    tokens, local_width = query.shape
    width = count * 128
    at = lo * 128 // width
    wide = pl.BlockSpec((BLK, width), lambda c, tbl: (c, at))
    return pl.pallas_call(
        functools.partial(enter_kernel, tab, lo, hp, count),
        grid_spec=pltpu.PrefetchScalarGridSpec(
            num_scalar_prefetch=1,
            grid=(tab.chunks,),
            in_specs=[
                wide,
                pl.BlockSpec((BLK, width), lambda c, tbl: (c, 0)),
                wide,
                pl.BlockSpec((1, width), lambda c, tbl: (0, tbl[tab.half] * (local_width // width) + at)),
                pl.BlockSpec((BLK, 128), lambda c, tbl: (c, 0)),
                whole((count, 128, 128)),
            ],
            out_specs=[
                pl.BlockSpec((1, BLK, width), lambda c, tbl: (tbl[tab.shard + c], 0, 0)),
                pl.BlockSpec((1, 1, BLK), lambda c, tbl: (tbl[tab.slot + c], 0, 0)),
            ],
        ),
        out_shape=[
            jax.ShapeDtypeStruct((tab.chunks, BLK, width), BF16),
            jax.ShapeDtypeStruct((tab.chunks, 1, BLK), F32),
        ],
        compiler_params=params(),
        cost_estimate=pl.CostEstimate(flops=width, bytes_accessed=width, transcendentals=0),
        name="attend_entered",
    )(table, query, own, gate, gain, cols, entering)


def attend_kernel(tab, lo, hp, count, last, *refs):
    ops = tab.n
    (table_ref, query_ref, key_ref, value_ref, gate_ref, gain_ref, rows_ref, cols_ref, docs_ref, state_ref, squares_ref) = refs[:11]
    outs = refs[11 : 11 + ops]
    state, gated = refs[-2:]
    step = pl.program_id(0)

    @pl.when(step == 0)
    def _():
        state[...] = state_ref[...].astype(F32)
        if last:
            gated[BLK:, :] = jnp.zeros((16, gated.shape[1]), BF16)

    barred = barred_pairs(hp, cols_ref, docs_ref)
    square = jnp.zeros((BLK, 128), F32)
    for h in range(count):
        attended = chunk_of_head(
            h, lo + h, hp, barred, query_ref, key_ref, value_ref, rows_ref, cols_ref, state
        )
        square = gate_head(h, attended, square, gain_ref, gate_ref, gated)
    total = jnp.sum(square.T, axis=0, keepdims=True) + squares_ref[0]
    if last:
        lanes, lines = extra_rows(gated.shape[1])
        row = lax.broadcasted_iota(jnp.int32, (16, lanes), 0)
        extra, left = jnp.zeros((16, lanes), F32), total
        for term in range(3):
            part = left.astype(BF16).astype(F32)
            left = left - part
            for line in range(lines):
                piece = part[:, line * lanes : (line + 1) * lanes]
                extra = jnp.where(row == term * lines + line, piece, extra)
        gated[BLK:, :lanes] = extra.astype(BF16)
    else:
        refs[11 + ops][0] = total
    which = table_ref[tab.which + step]
    for op in range(ops):

        @pl.when(which == op)
        def _():
            outs[op][0] = gated[...]


def attend(tab, table, query, key, value, gate, gain, rows, cols, docs, entering, base, lo, count, squares, last):
    tokens, local_width = query.shape
    chunks, per = tab.chunks, tab.per
    ops = tab.n
    hp = rows.shape[0] // 3
    width = count * 128
    at = lo * 128 // width
    height = BLK + 16 * last
    wide = pl.BlockSpec((BLK, width), lambda c, tbl: (c, at))
    square_spec = pl.BlockSpec((1, 1, BLK), lambda c, tbl: (tbl[tab.slot + c], 0, 0))

    def out_map(op, c, tbl):
        return (tbl[tab.place + op * chunks + c], 0, 0)

    out = pl.pallas_call(
        functools.partial(attend_kernel, tab, lo, hp, count, last),
        grid_spec=pltpu.PrefetchScalarGridSpec(
            num_scalar_prefetch=1,
            grid=(chunks,),
            in_specs=[
                wide,
                wide,
                wide,
                wide,
                pl.BlockSpec((1, width), lambda c, tbl: (0, tbl[tab.half] * (local_width // width) + at)),
                pl.BlockSpec((rows.shape[0], BLK), lambda c, tbl: (0, c)),
                pl.BlockSpec((BLK, 128), lambda c, tbl: (c, 0)),
                pl.BlockSpec((8, BLK), lambda c, tbl: (0, c)),
                pl.BlockSpec((count, 128, 128), lambda c, tbl: ((lo - base) // count, 0, 0)),
            ]
            + [square_spec],
            out_specs=[
                pl.BlockSpec((1, height, width), functools.partial(out_map, op)) for op in range(ops)
            ]
            + [square_spec] * (not last),
            scratch_shapes=[
                pltpu.VMEM((count, 128, 128), F32),
                pltpu.VMEM((height, width), BF16),
            ],
        ),
        out_shape=[jax.ShapeDtypeStruct((chunks // ops, height, width), BF16)] * ops
        + [jax.ShapeDtypeStruct((chunks, 1, BLK), F32)] * (not last),
        compiler_params=params(),
        cost_estimate=pl.CostEstimate(flops=width, bytes_accessed=width, transcendentals=0),
        name="attend",
    )(table, query, key, value, gate, gain, rows, cols, docs, entering, squares)
    return out[:ops], None if last else out[ops]


def place_kernel(features, t, count, lanes, lines, table_ref, *refs):
    out_ref = refs[-1]
    square = []
    for line in range(lines):
        parts = [refs[k][0, term * lines + line : term * lines + line + 1, :] for k in range(t) for term in range(3)]
        square.append(sum(part.astype(F32) for part in parts))
    scale = [lax.rsqrt(row / features + norm_eps) for row in square]
    scale = jnp.concatenate([jnp.broadcast_to(row, (128, lanes)).T for row in scale], axis=0)
    done = 0
    for piece_ref in refs[t : t + count]:
        for c in range(piece_ref.shape[2] // 128):
            piece = piece_ref[0, :BLK, c * 128 : (c + 1) * 128].astype(F32)
            out_ref[:, done : done + 128] = (piece * scale).astype(BF16)
            done += 128


def place(tab, table, op, lo, pieces, extras, out, shape, local_width, features):
    def piece_map(all_blocks, c, tbl):
        block = tbl[tab.side + op] * tab.stride * tab.per + tbl[tab.row + op] if all_blocks else 0
        return (block + c, 0, 0)

    lanes, lines = extra_rows(extras[0].shape[2])
    unit = sum(piece.shape[2] for piece in pieces)

    def out_map(c, tbl):
        return (tbl[tab.row + op] + c, tbl[tab.side + op] * (local_width // unit) + lo * 128 // unit)

    in_specs = [pl.BlockSpec((1, 16, lanes), lambda c, tbl: (c, BLK // 16, 0))] * tab.t
    in_specs += [
        pl.BlockSpec((1, *piece.shape[1:]), functools.partial(piece_map, piece.shape[0] > tab.per))
        for piece in pieces
    ]
    operands = [table, *extras, *pieces]
    aliases = {}
    if out is not None:
        in_specs.append(pl.BlockSpec(memory_space=pl.ANY))
        operands.append(out)
        aliases = {len(operands) - 1: 0}
    return pl.pallas_call(
        functools.partial(place_kernel, features, tab.t, len(pieces), lanes, lines),
        grid_spec=pltpu.PrefetchScalarGridSpec(
            num_scalar_prefetch=1,
            grid=(tab.per,),
            in_specs=in_specs,
            out_specs=pl.BlockSpec((BLK, unit), out_map),
        ),
        out_shape=jax.ShapeDtypeStruct(shape, BF16),
        input_output_aliases=aliases,
        compiler_params=params(63 * 2**20),
        cost_estimate=pl.CostEstimate(flops=unit, bytes_accessed=unit, transcendentals=0),
        name="place",
    )(*operands)


def local(query_rows, key_rows, value_rows, gate_rows, decay_log, norm_gain, doc_lengths, block_shard):
    tokens, width = query_rows.shape
    heads = decay_log.shape[0]
    features = norm_gain.shape[0]
    n, t = lax.axis_size("ctx"), lax.axis_size("tp")
    tab = Table(n, t, tokens // BLK)
    quarter = max(1, heads // 4)

    rest = heads - quarter
    splits = ((rest, quarter), (0, rest))
    (rows, cols, docs, total_gate, table, *states) = prelude(
        tab, splits, doc_lengths, block_shard, decay_log, key_rows, value_rows
    )
    gain = norm_gain.reshape(1, features)
    hop = [(i, i + 1) for i in range(n - 1)]

    def route(op):
        return [
            (d * t + k, (d + op + k * tab.stride) % n * t + d // tab.stride)
            for d in range(n)
            for k in range(t)
        ]

    def relay(lo, count, low, full):
        carry = total_gate[lo : lo + count, :1, None]
        for _ in range(max(1, n // 2) - 1):
            low = (carry * lax.ppermute(low, "ctx", hop).astype(F32) + full).astype(BF16)
        return low

    early, later = (relay(*split, low, full) for split, low, full in zip(splits, states[:2], states[2:]))
    own = attend_own(query_rows, key_rows, value_rows, rows, cols, docs, rest, quarter)
    early, own = lax.optimization_barrier((early, own))
    early = lax.ppermute(early, "ctx", hop)
    early, later = lax.optimization_barrier((early, later))
    entering = lax.ppermute(later, "ctx", hop)
    ready, squares = attend_entered(
        tab, table, query_rows, own, gate_rows, gain, cols, early, rest, quarter, rows.shape[0] // 3
    )
    ready, entering = lax.optimization_barrier((ready, entering))
    gated = [None]
    for lo, count in ((0, 2 * quarter), (2 * quarter, quarter)):
        outs, squares = attend(
            tab, table, query_rows, key_rows, value_rows, gate_rows, gain, rows, cols, docs,
            entering, 0, lo, count, squares, lo > 0,
        )
        gated.append(outs)
    head = lax.all_to_all(ready, "ctx", split_axis=0, concat_axis=0, tiled=True)
    head = lax.all_to_all(head, "tp", split_axis=0, concat_axis=0, tiled=True)
    tail = [lax.ppermute(gated[2][op], ("ctx", "tp"), route(op)) for op in range(n)]
    middle = []
    for op in range(n):
        ready = gated[1][op]
        for before in ([], [0, n - 1])[op] if op < 2 else [op - 1]:
            ready, tail[before] = lax.optimization_barrier((ready, tail[before]))
        middle.append(lax.ppermute(ready, ("ctx", "tp"), route(op)))

    shape = (tokens // t, features)
    out = None
    for pieces, lo in ((lambda op: [tail[op], head], 2 * quarter), (lambda op: [middle[op]], 0)):
        for op in range(n):
            extras = [tail[(op + k * tab.stride) % n] for k in range(t)]
            out = place(tab, table, op, lo, pieces(op), extras, out, shape, width, features)
    return out


def solution(mesh):
    return jax.shard_map(
        local,
        mesh=mesh,
        in_specs=(
            P(("dp", "ctx"), "tp"),
            P(("dp", "ctx"), "tp"),
            P(("dp", "ctx"), "tp"),
            P(("dp", "ctx"), "tp"),
            P("tp", ("dp", "ctx")),
            P(),
            P("dp"),
            P("dp"),
        ),
        out_specs=P(("dp", "ctx", "tp"), None),
        check_vma=False,
    )
```

```python
import functools

import jax
import jax.numpy as jnp
from jax import lax
from jax.experimental import pallas as pl
from jax.experimental.pallas import tpu as pltpu
from jax.sharding import PartitionSpec as P

BLK = 256
norm_eps = 1e-05
VMEM_LIMIT = 56 * 2**20
F32 = jnp.float32
BF16 = jnp.bfloat16


def params(limit=VMEM_LIMIT):
    return pltpu.CompilerParams(vmem_limit_bytes=limit)


def in_hbm(array):
    return pltpu.with_memory_space_constraint(array, pltpu.HBM)


def whole(shape):
    return pl.BlockSpec(shape, lambda *_: (0,) * len(shape))


def extra_rows(width):
    lanes = min(width, BLK)
    return lanes, BLK // lanes


def pad8(count):
    return -(-count // 8) * 8


class Table:
    def __init__(self, n, t, chunks):
        self.n, self.t, self.chunks = n, t, chunks
        self.stride, self.per = n // t, chunks // n
        self.half = 0
        self.which = 1
        self.slot = self.which + chunks
        self.place = self.slot + chunks
        self.row = self.place + n * chunks
        self.side = self.row + n
        self.shard = self.side + n
        self.size = self.shard + chunks


def fill_table(tab, shard_ref, table_ref):
    n, per, chunks = tab.n, tab.per, tab.chunks
    ctx, tp = lax.axis_index("ctx"), lax.axis_index("tp")
    table_ref[tab.half] = tp
    seen = [jnp.int32(0)] * n
    for c in range(chunks):
        shard = shard_ref[ctx * chunks + c]
        op = lax.rem(shard - ctx - tp * tab.stride + 2 * n, n)
        table_ref[tab.which + c] = op
        rank = jnp.int32(0)
        for k in range(n):
            table_ref[tab.place + k * chunks + c] = jnp.minimum(seen[k], per - 1)
            here = (op == k).astype(jnp.int32)
            rank = rank + here * seen[k]
            seen[k] = seen[k] + here
        table_ref[tab.slot + c] = op * per + jnp.minimum(rank, per - 1)
        table_ref[tab.shard + c] = shard * per + jnp.minimum(rank, per - 1)
    for op in range(n):
        lane = lax.rem(ctx - op + n, tab.stride)
        source = tp * tab.stride + lane
        table_ref[tab.row + op] = lane * per
        table_ref[tab.side + op] = lax.rem(ctx - op - source + 2 * n, n) // tab.stride


def fill_gates(len_ref, decay_ref, rows_ref, cols_ref, docs_ref, total_ref, tail_ref, scr):
    heads, tokens = decay_ref.shape
    hp = pad8(heads)
    chunks = tokens // BLK
    base = lax.axis_index("ctx") * tokens
    starts, run = [], jnp.int32(0)
    for i in range(len_ref.shape[0]):
        starts.append(run)
        run = run + len_ref[i]

    def doc_at(position):
        found = jnp.int32(0)
        for start in starts:
            found = found + (position >= start).astype(jnp.int32)
        return found - 1

    position = base + lax.broadcasted_iota(jnp.int32, (8, tokens), 1)
    doc = jnp.zeros((8, tokens), jnp.int32) - 1
    for start in starts:
        doc = doc + (position >= start).astype(jnp.int32)
    docs_ref[...] = doc.astype(F32)
    edges = [doc_at(base - 1)] + [doc_at(base + (c + 1) * BLK - 1) for c in range(chunks)]

    first = lax.broadcasted_iota(jnp.int32, (BLK, BLK), 0)
    second = lax.broadcasted_iota(jnp.int32, (BLK, BLK), 1)
    upto = jnp.where(first <= second, 1.0, 0.0).astype(F32)
    every = jnp.ones((BLK, BLK), F32)
    scr[...] = jnp.zeros_like(scr)
    cums, sums = [], []
    for c in range(chunks):
        part = decay_ref[:, c * BLK : (c + 1) * BLK]
        cums.append(jnp.dot(part, upto, precision=lax.Precision.HIGHEST, preferred_element_type=F32))
        sums.append(jnp.dot(part, every, precision=lax.Precision.HIGHEST, preferred_element_type=F32))
    before, after = [], [None] * chunks
    run = jnp.zeros_like(sums[0])
    for c in range(chunks):
        before.append(run)
        run = run + sums[c]
    run = jnp.zeros_like(sums[0])
    for c in reversed(range(chunks)):
        after[c] = run
        run = run + sums[c]
    for c in range(chunks):
        span = slice(c * BLK, (c + 1) * BLK)
        doc_c = doc[:1, span]
        cum, total = cums[c], sums[c]
        rows_ref[0:heads, span] = cum
        rows_ref[hp : hp + heads, span] = jnp.where(doc_c == edges[c + 1], jnp.exp(total - cum), 0.0)
        tail_ref[0:heads, span] = jnp.where(doc_c == edges[-1], jnp.exp(total - cum + after[c]), 0.0)
        rows_ref[2 * hp : 2 * hp + heads, span] = jnp.where(
            edges[c + 1] == edges[c], jnp.exp(total), 0.0
        )
        scr[0:heads, span] = cum
        scr[hp : hp + heads, span] = jnp.where(doc_c == edges[c], jnp.exp(cum), 0.0)
        scr[2 * hp + 8 : 2 * hp + 8 + heads, span] = jnp.where(
            doc_c == edges[0], jnp.exp(before[c] + cum), 0.0
        )
    scr[2 * hp : 2 * hp + 8, :] = doc.astype(F32)
    cols_ref[...] = scr[...].T
    total_ref[...] = jnp.where(edges[-1] == edges[0], jnp.exp(run[:, :128]), 0.0)


def prelude_kernel(tab, splits, len_ref, shard_ref, decay_ref, key_ref, value_ref, *refs):
    rows_ref, cols_ref, docs_ref, total_ref, table_ref = refs[:5]
    lows, fulls = refs[5 : 5 + len(splits)], refs[5 + len(splits) : 5 + 2 * len(splits)]
    tail_ref, scr, acc = refs[5 + 2 * len(splits) :]
    step = pl.program_id(0)
    tile = key_ref.shape[0]

    @pl.when(step == 0)
    def _():
        fill_table(tab, shard_ref, table_ref)
        fill_gates(len_ref, decay_ref, rows_ref, cols_ref, docs_ref, total_ref, tail_ref, scr)
        acc[...] = jnp.zeros_like(acc)

    tails = tail_ref[:, pl.ds(pl.multiple_of(step * tile, tile), tile)]
    for h in range(acc.shape[0]):
        cols = slice(h * 128, (h + 1) * 128)
        scaled = (key_ref[:, cols].T.astype(F32) * tails[h : h + 1, :]).astype(BF16)
        acc[h] += jnp.dot(scaled, value_ref[:, cols], preferred_element_type=F32)

    @pl.when(step == pl.num_programs(0) - 1)
    def _():
        for (lo, count), low_ref, full_ref in zip(splits, lows, fulls):
            low_ref[...] = acc[lo : lo + count].astype(BF16)
            full_ref[...] = acc[lo : lo + count]


def prelude(tab, splits, doc_lengths, block_shard, decay, key, value):
    heads, tokens = decay.shape
    hp = pad8(heads)
    tile = 2 * BLK
    smem = pl.BlockSpec(memory_space=pltpu.SMEM)
    shapes = [(3 * hp, tokens), (tokens, 128), (8, tokens), (heads, 128)]
    states = [(count, 128, 128) for _, count in splits]
    wide = pl.BlockSpec((tile, key.shape[1]), lambda c: (c, 0))
    return pl.pallas_call(
        functools.partial(prelude_kernel, tab, splits),
        grid=(tokens // tile,),
        in_specs=[smem, smem, whole(decay.shape), wide, wide],
        out_specs=[whole(shape) for shape in shapes] + [smem] + [whole(shape) for shape in states * 2],
        out_shape=[jax.ShapeDtypeStruct(shape, F32) for shape in shapes]
        + [jax.ShapeDtypeStruct((tab.size,), jnp.int32)]
        + [jax.ShapeDtypeStruct(shape, BF16) for shape in states]
        + [jax.ShapeDtypeStruct(shape, F32) for shape in states],
        scratch_shapes=[
            pltpu.VMEM((hp, tokens), F32),
            pltpu.VMEM((128, tokens), F32),
            pltpu.VMEM((heads, 128, 128), F32),
        ],
        compiler_params=params(24 * 2**20),
        name="prelude",
    )(doc_lengths, block_shard, decay, in_hbm(key), in_hbm(value))


def barred_pairs(hp, cols_ref, docs_ref):
    first = lax.broadcasted_iota(jnp.int32, (BLK, BLK), 0)
    second = lax.broadcasted_iota(jnp.int32, (BLK, BLK), 1)
    same = cols_ref[:, 2 * hp : 2 * hp + 1] == docs_ref[0:1, :]
    return jnp.where((first >= second) & same, 0.0, -1e30).astype(F32)


def chunk_of_head(h, head, hp, barred, query_ref, key_ref, value_ref, rows_ref, cols_ref, state):
    cols = slice(h * 128, (h + 1) * 128)
    query, value = query_ref[:, cols], value_ref[:, cols]
    key_t = key_ref[:, cols].T
    scores = jnp.dot(query, key_t, preferred_element_type=F32)
    gap = cols_ref[:, head : head + 1] - rows_ref[head : head + 1, :] + barred
    weights = (scores * jnp.exp(gap)).astype(BF16)
    intra = jnp.dot(weights, value, preferred_element_type=F32)
    reached = jnp.dot(query, state[h].astype(BF16), preferred_element_type=F32)
    scaled = (key_t.astype(F32) * rows_ref[hp + head : hp + head + 1, :]).astype(BF16)
    carry = rows_ref[2 * hp + head : 2 * hp + head + 1, :128]
    state[h] = carry * state[h] + jnp.dot(scaled, value, preferred_element_type=F32)
    return intra + cols_ref[:, hp + head : hp + head + 1] * reached


def gate_head(h, attended, square, gain_ref, gate_ref, gated):
    cols = slice(h * 128, (h + 1) * 128)
    attended = attended.astype(BF16).astype(F32)
    gated[:BLK, cols] = (
        attended * gain_ref[0:1, cols] * jax.nn.sigmoid(gate_ref[:, cols].astype(F32))
    ).astype(BF16)
    return square + attended * attended


def own_kernel(lo, hp, count, *refs):
    (_, query_ref, key_ref, value_ref, gate_ref, gain_ref, rows_ref, cols_ref, docs_ref) = refs[:9]
    own_ref, same_ref, factor_ref, state = refs[9:]

    @pl.when(pl.program_id(0) == 0)
    def _():
        state[...] = jnp.zeros_like(state)

    barred = barred_pairs(hp, cols_ref, docs_ref)
    for h in range(count):
        own_ref[:, h * 128 : (h + 1) * 128] = chunk_of_head(
            h, lo + h, hp, barred, query_ref, key_ref, value_ref, rows_ref, cols_ref, state
        )
    same_ref[...] = query_ref[...]
    factor_ref[...] = gain_ref[0:1, :] * jax.nn.sigmoid(gate_ref[...].astype(F32))


def attend_own(tab, table, query, key, value, gate, gain, rows, cols, docs, lo, count):
    tokens, local_width = query.shape
    hp = rows.shape[0] // 3
    width = count * 128
    at = lo * 128 // width
    wide = pl.BlockSpec((BLK, width), lambda c, tbl: (c, at))
    narrow = pl.BlockSpec((BLK, width), lambda c, tbl: (c, 0))
    return pl.pallas_call(
        functools.partial(own_kernel, lo, hp, count),
        grid_spec=pltpu.PrefetchScalarGridSpec(
            num_scalar_prefetch=1,
            grid=(tokens // BLK,),
            in_specs=[
                wide,
                wide,
                wide,
                wide,
                pl.BlockSpec((1, width), lambda c, tbl: (0, tbl[tab.half] * (local_width // width) + at)),
                pl.BlockSpec((rows.shape[0], BLK), lambda c, tbl: (0, c)),
                pl.BlockSpec((BLK, 128), lambda c, tbl: (c, 0)),
                pl.BlockSpec((8, BLK), lambda c, tbl: (0, c)),
            ],
            out_specs=[narrow] * 3,
            scratch_shapes=[pltpu.VMEM((count, 128, 128), F32)],
        ),
        out_shape=[jax.ShapeDtypeStruct((tokens, width), kind) for kind in (F32, BF16, F32)],
        compiler_params=params(24 * 2**20),
        cost_estimate=pl.CostEstimate(
            flops=8 * tokens * width * BLK, bytes_accessed=10 * tokens * width, transcendentals=0
        ),
        name="attend_own",
    )(table, *map(in_hbm, (query, key, value, gate)), gain, rows, cols, docs)


def enter_kernel(tab, lo, hp, count, table_ref, own_ref, query_ref, factor_ref, cols_ref, state_ref, out_ref, square_ref):
    for c in range(tab.chunks):
        span = slice(c * BLK, (c + 1) * BLK)
        place, slot = table_ref[tab.shard + c], table_ref[tab.slot + c]
        square = jnp.zeros((BLK, 128), F32)
        for h in range(count):
            cols = slice(h * 128, (h + 1) * 128)
            reached = jnp.dot(query_ref[span, cols], state_ref[h], preferred_element_type=F32)
            column = 2 * hp + 8 + lo + h
            attended = own_ref[span, cols] + cols_ref[span, column : column + 1] * reached
            attended = attended.astype(BF16).astype(F32)
            out_ref[place, :, cols] = (attended * factor_ref[span, cols]).astype(BF16)
            square = square + attended * attended
        square_ref[slot] = jnp.sum(square.T, axis=0, keepdims=True)


def attend_entered(tab, table, own, cols, entering, lo, count, hp):
    width = count * 128
    vmem = pl.BlockSpec(memory_space=pltpu.VMEM)
    return pl.pallas_call(
        functools.partial(enter_kernel, tab, lo, hp, count),
        in_specs=[pl.BlockSpec(memory_space=pltpu.SMEM)] + [vmem] * 5,
        out_specs=[vmem] * 2,
        out_shape=[
            jax.ShapeDtypeStruct((tab.chunks, BLK, width), BF16),
            jax.ShapeDtypeStruct((tab.chunks, 1, BLK), F32),
        ],
        compiler_params=params(24 * 2**20),
        cost_estimate=pl.CostEstimate(flops=width, bytes_accessed=width, transcendentals=0),
        name="attend_entered",
    )(table, *own, cols, entering)


def attend_kernel(tab, lo, hp, count, last, *refs):
    ops = tab.n
    (table_ref, query_ref, key_ref, value_ref, gate_ref, gain_ref, rows_ref, cols_ref, docs_ref, state_ref, squares_ref) = refs[:11]
    outs = refs[11 : 11 + ops]
    state, gated = refs[-2:]
    step = pl.program_id(0)

    @pl.when(step == 0)
    def _():
        state[...] = state_ref[...].astype(F32)
        if last:
            gated[BLK:, :] = jnp.zeros((16, gated.shape[1]), BF16)

    barred = barred_pairs(hp, cols_ref, docs_ref)
    square = jnp.zeros((BLK, 128), F32)
    for h in range(count):
        attended = chunk_of_head(
            h, lo + h, hp, barred, query_ref, key_ref, value_ref, rows_ref, cols_ref, state
        )
        square = gate_head(h, attended, square, gain_ref, gate_ref, gated)
    total = jnp.sum(square.T, axis=0, keepdims=True) + squares_ref[0]
    if last:
        lanes, lines = extra_rows(gated.shape[1])
        row = lax.broadcasted_iota(jnp.int32, (16, lanes), 0)
        extra, left = jnp.zeros((16, lanes), F32), total
        for term in range(3):
            part = left.astype(BF16).astype(F32)
            left = left - part
            for line in range(lines):
                piece = part[:, line * lanes : (line + 1) * lanes]
                extra = jnp.where(row == term * lines + line, piece, extra)
        gated[BLK:, :lanes] = extra.astype(BF16)
    else:
        refs[11 + ops][0] = total
    which = table_ref[tab.which + step]
    for op in range(ops):

        @pl.when(which == op)
        def _():
            outs[op][0] = gated[...]


def attend(tab, table, query, key, value, gate, gain, rows, cols, docs, entering, base, lo, count, squares, last):
    tokens, local_width = query.shape
    chunks, per = tab.chunks, tab.per
    ops = tab.n
    hp = rows.shape[0] // 3
    width = count * 128
    at = lo * 128 // width
    height = BLK + 16 * last
    wide = pl.BlockSpec((BLK, width), lambda c, tbl: (c, at))
    square_spec = pl.BlockSpec((1, 1, BLK), lambda c, tbl: (tbl[tab.slot + c], 0, 0))

    def out_map(op, c, tbl):
        return (tbl[tab.place + op * chunks + c], 0, 0)

    out = pl.pallas_call(
        functools.partial(attend_kernel, tab, lo, hp, count, last),
        grid_spec=pltpu.PrefetchScalarGridSpec(
            num_scalar_prefetch=1,
            grid=(chunks,),
            in_specs=[
                wide,
                wide,
                wide,
                wide,
                pl.BlockSpec((1, width), lambda c, tbl: (0, tbl[tab.half] * (local_width // width) + at)),
                pl.BlockSpec((rows.shape[0], BLK), lambda c, tbl: (0, c)),
                pl.BlockSpec((BLK, 128), lambda c, tbl: (c, 0)),
                pl.BlockSpec((8, BLK), lambda c, tbl: (0, c)),
                pl.BlockSpec((count, 128, 128), lambda c, tbl: ((lo - base) // count, 0, 0)),
            ]
            + [square_spec],
            out_specs=[
                pl.BlockSpec((1, height, width), functools.partial(out_map, op)) for op in range(ops)
            ]
            + [square_spec] * (not last),
            scratch_shapes=[
                pltpu.VMEM((count, 128, 128), F32),
                pltpu.VMEM((height, width), BF16),
            ],
        ),
        out_shape=[jax.ShapeDtypeStruct((chunks // ops, height, width), BF16)] * ops
        + [jax.ShapeDtypeStruct((chunks, 1, BLK), F32)] * (not last),
        compiler_params=params(),
        cost_estimate=pl.CostEstimate(flops=16 * tokens * width * BLK, bytes_accessed=10 * tokens * width, transcendentals=tokens * width),
        name="attend",
    )(table, query, key, value, gate, gain, rows, cols, docs, entering, squares)
    return out[:ops], None if last else out[ops]


def place_kernel(features, t, count, lanes, lines, table_ref, *refs):
    out_ref = refs[-1]
    square = []
    for line in range(lines):
        parts = [refs[k][0, term * lines + line : term * lines + line + 1, :] for k in range(t) for term in range(3)]
        square.append(sum(part.astype(F32) for part in parts))
    scale = [lax.rsqrt(row / features + norm_eps) for row in square]
    scale = jnp.concatenate([jnp.broadcast_to(row, (128, lanes)).T for row in scale], axis=0)
    done = 0
    for piece_ref in refs[t : t + count]:
        for c in range(piece_ref.shape[2] // 128):
            piece = piece_ref[0, :BLK, c * 128 : (c + 1) * 128].astype(F32)
            out_ref[:, done : done + 128] = (piece * scale).astype(BF16)
            done += 128


def place(tab, table, op, lo, pieces, extras, out, shape, local_width, features):
    def piece_map(all_blocks, c, tbl):
        block = tbl[tab.side + op] * tab.stride * tab.per + tbl[tab.row + op] if all_blocks else 0
        return (block + c, 0, 0)

    lanes, lines = extra_rows(extras[0].shape[2])
    unit = sum(piece.shape[2] for piece in pieces)

    def out_map(c, tbl):
        return (tbl[tab.row + op] + c, tbl[tab.side + op] * (local_width // unit) + lo * 128 // unit)

    in_specs = [pl.BlockSpec((1, 16, lanes), lambda c, tbl: (c, BLK // 16, 0))] * tab.t
    in_specs += [
        pl.BlockSpec((1, *piece.shape[1:]), functools.partial(piece_map, piece.shape[0] > tab.per))
        for piece in pieces
    ]
    operands = [table, *extras, *pieces]
    aliases = {}
    if out is not None:
        in_specs.append(pl.BlockSpec(memory_space=pl.ANY))
        operands.append(out)
        aliases = {len(operands) - 1: 0}
    return pl.pallas_call(
        functools.partial(place_kernel, features, tab.t, len(pieces), lanes, lines),
        grid_spec=pltpu.PrefetchScalarGridSpec(
            num_scalar_prefetch=1,
            grid=(tab.per,),
            in_specs=in_specs,
            out_specs=pl.BlockSpec((BLK, unit), out_map),
        ),
        out_shape=jax.ShapeDtypeStruct(shape, BF16),
        input_output_aliases=aliases,
        compiler_params=params(63 * 2**20),
        cost_estimate=pl.CostEstimate(flops=unit, bytes_accessed=unit, transcendentals=0),
        name="place",
    )(*operands)


def local(query_rows, key_rows, value_rows, gate_rows, decay_log, norm_gain, doc_lengths, block_shard):
    tokens, width = query_rows.shape
    heads = decay_log.shape[0]
    features = norm_gain.shape[0]
    n, t = lax.axis_size("ctx"), lax.axis_size("tp")
    tab = Table(n, t, tokens // BLK)
    quarter = max(1, heads // 4)

    rest = heads - quarter
    splits = ((0, heads),)
    (rows, cols, docs, total_gate, table, *states) = prelude(
        tab, splits, doc_lengths, block_shard, decay_log, key_rows, value_rows
    )
    gain = norm_gain.reshape(1, features)
    hop = [(i, i + 1) for i in range(n - 1)]

    def route(op):
        return [
            (d * t + k, (d + op + k * tab.stride) % n * t + d // tab.stride)
            for d in range(n)
            for k in range(t)
        ]

    low, full = states
    carry = total_gate[:, :1, None]

    def merge(arrived, part):
        return (carry[part] * arrived[part].astype(F32) + full[part]).astype(BF16)

    first, others = slice(rest, heads), slice(0, rest)
    for _ in range(max(1, n // 2) - 2):
        low = merge(lax.ppermute(low, "ctx", hop), slice(0, heads))
    parts = [low[first], low[others]]
    if n // 2 > 1:
        arrived = lax.ppermute(low, "ctx", hop)
        parts = [merge(arrived, first), merge(arrived, others)]
    own = attend_own(
        tab, table, query_rows, key_rows, value_rows, gate_rows, gain, rows, cols, docs, rest, quarter
    )
    parts, own = lax.optimization_barrier((parts, own))
    early, entering = (lax.ppermute(part, "ctx", hop) for part in parts)
    ready, squares = attend_entered(tab, table, own, cols, early, rest, quarter, rows.shape[0] // 3)
    gated = [None]
    for lo, count in ((0, 2 * quarter), (2 * quarter, quarter)):
        outs, squares = attend(
            tab, table, query_rows, key_rows, value_rows, gate_rows, gain, rows, cols, docs,
            entering, 0, lo, count, squares, lo > 0,
        )
        gated.append(outs)
    head = lax.all_to_all(ready, "ctx", split_axis=0, concat_axis=0, tiled=True)
    head = lax.all_to_all(head, "tp", split_axis=0, concat_axis=0, tiled=True)
    tail = [lax.ppermute(gated[2][op], ("ctx", "tp"), route(op)) for op in range(n)]
    middle = []
    for op in range(n):
        ready = gated[1][op]
        for before in ([], [0, n - 1])[op] if op < 2 else [op - 1]:
            ready, tail[before] = lax.optimization_barrier((ready, tail[before]))
        middle.append(lax.ppermute(ready, ("ctx", "tp"), route(op)))

    shape = (tokens // t, features)
    out = None
    for pieces, lo in ((lambda op: [tail[op], head], 2 * quarter), (lambda op: [middle[op]], 0)):
        for op in range(n):
            extras = [tail[(op + k * tab.stride) % n] for k in range(t)]
            out = place(tab, table, op, lo, pieces(op), extras, out, shape, width, features)
    return out


def solution(mesh):
    return jax.shard_map(
        local,
        mesh=mesh,
        in_specs=(
            P(("dp", "ctx"), "tp"),
            P(("dp", "ctx"), "tp"),
            P(("dp", "ctx"), "tp"),
            P(("dp", "ctx"), "tp"),
            P("tp", ("dp", "ctx")),
            P(),
            P("dp"),
            P("dp"),
        ),
        out_specs=P(("dp", "ctx", "tp"), None),
        check_vma=False,
    )
```

```python
import functools

import jax
import jax.numpy as jnp
from jax import lax
from jax.experimental import pallas as pl
from jax.experimental.pallas import tpu as pltpu
from jax.sharding import PartitionSpec as P

BLK = 256
norm_eps = 1e-05
VMEM_LIMIT = 56 * 2**20
F32 = jnp.float32
BF16 = jnp.bfloat16


def params(limit=VMEM_LIMIT):
    return pltpu.CompilerParams(vmem_limit_bytes=limit)


def in_hbm(array):
    return pltpu.with_memory_space_constraint(array, pltpu.HBM)


def whole(shape):
    return pl.BlockSpec(shape, lambda *_: (0,) * len(shape))


def extra_rows(width):
    lanes = min(width, BLK)
    return lanes, BLK // lanes


def pad8(count):
    return -(-count // 8) * 8


class Table:
    def __init__(self, n, t, chunks):
        self.n, self.t, self.chunks = n, t, chunks
        self.stride, self.per = n // t, chunks // n
        self.half = 0
        self.which = 1
        self.slot = self.which + chunks
        self.place = self.slot + chunks
        self.row = self.place + n * chunks
        self.side = self.row + n
        self.shard = self.side + n
        self.size = self.shard + chunks


def fill_table(tab, shard_ref, table_ref):
    n, per, chunks = tab.n, tab.per, tab.chunks
    ctx, tp = lax.axis_index("ctx"), lax.axis_index("tp")
    table_ref[tab.half] = tp
    seen = [jnp.int32(0)] * n
    for c in range(chunks):
        shard = shard_ref[ctx * chunks + c]
        op = lax.rem(shard - ctx - tp * tab.stride + 2 * n, n)
        table_ref[tab.which + c] = op
        rank = jnp.int32(0)
        for k in range(n):
            table_ref[tab.place + k * chunks + c] = jnp.minimum(seen[k], per - 1)
            here = (op == k).astype(jnp.int32)
            rank = rank + here * seen[k]
            seen[k] = seen[k] + here
        table_ref[tab.slot + c] = op * per + jnp.minimum(rank, per - 1)
        table_ref[tab.shard + c] = shard * per + jnp.minimum(rank, per - 1)
    for op in range(n):
        lane = lax.rem(ctx - op + n, tab.stride)
        source = tp * tab.stride + lane
        table_ref[tab.row + op] = lane * per
        table_ref[tab.side + op] = lax.rem(ctx - op - source + 2 * n, n) // tab.stride


def fill_gates(len_ref, decay_ref, rows_ref, cols_ref, docs_ref, total_ref, tail_ref, scr, stack):
    heads, tokens = decay_ref.shape
    hp = pad8(heads)
    chunks = tokens // BLK
    base = lax.axis_index("ctx") * tokens
    starts, run = [], jnp.int32(0)
    for i in range(len_ref.shape[0]):
        starts.append(run)
        run = run + len_ref[i]

    def doc_at(position):
        found = jnp.int32(0)
        for start in starts:
            found = found + (position >= start).astype(jnp.int32)
        return found - 1

    position = base + lax.broadcasted_iota(jnp.int32, (8, tokens), 1)
    doc = jnp.zeros((8, tokens), jnp.int32) - 1
    for start in starts:
        doc = doc + (position >= start).astype(jnp.int32)
    docs_ref[...] = doc.astype(F32)
    edges = [doc_at(base - 1)] + [doc_at(base + (c + 1) * BLK - 1) for c in range(chunks)]

    first = lax.broadcasted_iota(jnp.int32, (BLK, BLK), 0)
    second = lax.broadcasted_iota(jnp.int32, (BLK, BLK), 1)
    upto = jnp.where(first <= second, 1.0, 0.0).astype(BF16)
    stack[...] = jnp.zeros_like(stack)
    for c in range(chunks):
        stack[c * hp : c * hp + heads, :] = decay_ref[:, c * BLK : (c + 1) * BLK]
    left, terms = stack[...], []
    for _ in range(3):
        terms.append(left.astype(BF16))
        left = left - terms[-1].astype(F32)
    high, middle, low = (jnp.dot(term, upto, preferred_element_type=F32) for term in terms)
    stack[...] = high + (middle + low)
    scr[...] = jnp.zeros_like(scr)
    cums = [stack[c * hp : c * hp + heads, :] for c in range(chunks)]
    sums = [jnp.broadcast_to(cum[:, BLK - 1 :], cum.shape) for cum in cums]
    before, after = [], [None] * chunks
    run = jnp.zeros_like(sums[0])
    for c in range(chunks):
        before.append(run)
        run = run + sums[c]
    run = jnp.zeros_like(sums[0])
    for c in reversed(range(chunks)):
        after[c] = run
        run = run + sums[c]
    for c in range(chunks):
        span = slice(c * BLK, (c + 1) * BLK)
        doc_c = doc[:1, span]
        cum, total = cums[c], sums[c]
        rows_ref[0:heads, span] = cum
        rows_ref[hp : hp + heads, span] = jnp.where(doc_c == edges[c + 1], jnp.exp(total - cum), 0.0)
        tail_ref[0:heads, span] = jnp.where(doc_c == edges[-1], jnp.exp(total - cum + after[c]), 0.0)
        rows_ref[2 * hp : 2 * hp + heads, span] = jnp.where(
            edges[c + 1] == edges[c], jnp.exp(total), 0.0
        )
        scr[0:heads, span] = cum
        scr[hp : hp + heads, span] = jnp.where(doc_c == edges[c], jnp.exp(cum), 0.0)
        scr[2 * hp + 8 : 2 * hp + 8 + heads, span] = jnp.where(
            doc_c == edges[0], jnp.exp(before[c] + cum), 0.0
        )
    scr[2 * hp : 2 * hp + 8, :] = doc.astype(F32)
    cols_ref[...] = scr[...].T
    total_ref[...] = jnp.where(edges[-1] == edges[0], jnp.exp(run[:, :128]), 0.0)


def prelude_kernel(tab, tile, len_ref, shard_ref, decay_ref, key_hbm, value_hbm, *refs):
    rows_ref, cols_ref, docs_ref, total_ref, table_ref, low_ref, full_ref = refs[:7]
    tail_ref, scr, stack, key_ref, value_ref, arrived = refs[7:]
    tokens = key_ref.shape[0]
    heads = full_ref.shape[0]
    copies = []
    for i in range(tokens // tile):
        span = pl.ds(i * tile, tile)
        for k, (source, target) in enumerate(((key_hbm, key_ref), (value_hbm, value_ref))):
            copies.append(pltpu.make_async_copy(source.at[span], target.at[span], arrived.at[k, i]))
            copies[-1].start()
    fill_table(tab, shard_ref, table_ref)
    fill_gates(len_ref, decay_ref, rows_ref, cols_ref, docs_ref, total_ref, tail_ref, scr, stack)
    for i in range(tokens // tile):
        copies[2 * i].wait()
        copies[2 * i + 1].wait()
        span = slice(i * tile, (i + 1) * tile)
        for h in range(heads):
            cols = slice(h * 128, (h + 1) * 128)
            scaled = (key_ref[span, cols].T.astype(F32) * tail_ref[h : h + 1, span]).astype(BF16)
            part = jnp.dot(scaled, value_ref[span, cols], preferred_element_type=F32)
            full_ref[h] = full_ref[h] + part if i else part
    low_ref[...] = full_ref[...].astype(BF16)


def prelude(tab, doc_lengths, block_shard, decay, key, value):
    heads, tokens = decay.shape
    hp = pad8(heads)
    tile = 2 * BLK
    smem = pl.BlockSpec(memory_space=pltpu.SMEM)
    vmem = pl.BlockSpec(memory_space=pltpu.VMEM)
    hbm = pl.BlockSpec(memory_space=pl.ANY)
    shapes = [(3 * hp, tokens), (tokens, 128), (8, tokens), (heads, 128)]
    return pl.pallas_call(
        functools.partial(prelude_kernel, tab, tile),
        in_specs=[smem, smem, vmem, hbm, hbm],
        out_specs=[vmem] * 4 + [smem] + [vmem] * 2,
        out_shape=[jax.ShapeDtypeStruct(shape, F32) for shape in shapes]
        + [jax.ShapeDtypeStruct((tab.size,), jnp.int32)]
        + [jax.ShapeDtypeStruct((heads, 128, 128), kind) for kind in (BF16, F32)],
        scratch_shapes=[
            pltpu.VMEM((hp, tokens), F32),
            pltpu.VMEM((128, tokens), F32),
            pltpu.VMEM((tokens // BLK * hp, BLK), F32),
            pltpu.VMEM(key.shape, BF16),
            pltpu.VMEM(value.shape, BF16),
            pltpu.SemaphoreType.DMA((2, tokens // tile)),
        ],
        compiler_params=params(32 * 2**20),
        name="prelude",
    )(doc_lengths, block_shard, in_hbm(decay), in_hbm(key), in_hbm(value))


def barred_pairs(hp, cols_ref, docs_ref):
    first = lax.broadcasted_iota(jnp.int32, (BLK, BLK), 0)
    second = lax.broadcasted_iota(jnp.int32, (BLK, BLK), 1)
    same = cols_ref[:, 2 * hp : 2 * hp + 1] == docs_ref[0:1, :]
    return jnp.where((first >= second) & same, 0.0, -1e30).astype(F32)


def chunk_of_head(h, head, hp, barred, query_ref, key_ref, value_ref, rows_ref, cols_ref, state):
    cols = slice(h * 128, (h + 1) * 128)
    query, value = query_ref[:, cols], value_ref[:, cols]
    key_t = key_ref[:, cols].T
    scores = jnp.dot(query, key_t, preferred_element_type=F32)
    gap = cols_ref[:, head : head + 1] - rows_ref[head : head + 1, :] + barred
    weights = (scores * jnp.exp(gap)).astype(BF16)
    intra = jnp.dot(weights, value, preferred_element_type=F32)
    reached = jnp.dot(query, state[h].astype(BF16), preferred_element_type=F32)
    scaled = (key_t.astype(F32) * rows_ref[hp + head : hp + head + 1, :]).astype(BF16)
    carry = rows_ref[2 * hp + head : 2 * hp + head + 1, :128]
    state[h] = carry * state[h] + jnp.dot(scaled, value, preferred_element_type=F32)
    return intra + cols_ref[:, hp + head : hp + head + 1] * reached


def gate_head(h, attended, square, gain_ref, gate_ref, gated):
    cols = slice(h * 128, (h + 1) * 128)
    attended = attended.astype(BF16).astype(F32)
    gated[:BLK, cols] = (
        attended * gain_ref[0:1, cols] * jax.nn.sigmoid(gate_ref[:, cols].astype(F32))
    ).astype(BF16)
    return square + attended * attended


def own_kernel(lo, hp, count, *refs):
    (_, query_ref, key_ref, value_ref, gate_ref, gain_ref, rows_ref, cols_ref, docs_ref) = refs[:9]
    own_ref, same_ref, factor_ref, state = refs[9:]

    @pl.when(pl.program_id(0) == 0)
    def _():
        state[...] = jnp.zeros_like(state)

    barred = barred_pairs(hp, cols_ref, docs_ref)
    for h in range(count):
        own_ref[:, h * 128 : (h + 1) * 128] = chunk_of_head(
            h, lo + h, hp, barred, query_ref, key_ref, value_ref, rows_ref, cols_ref, state
        )
    same_ref[...] = query_ref[...]
    factor_ref[...] = gain_ref[0:1, :] * jax.nn.sigmoid(gate_ref[...].astype(F32))


def attend_own(tab, table, query, key, value, gate, gain, rows, cols, docs, lo, count):
    tokens, local_width = query.shape
    hp = rows.shape[0] // 3
    width = count * 128
    at = lo * 128 // width
    wide = pl.BlockSpec((BLK, width), lambda c, tbl: (c, at))
    narrow = pl.BlockSpec((BLK, width), lambda c, tbl: (c, 0))
    return pl.pallas_call(
        functools.partial(own_kernel, lo, hp, count),
        grid_spec=pltpu.PrefetchScalarGridSpec(
            num_scalar_prefetch=1,
            grid=(tokens // BLK,),
            in_specs=[
                wide,
                wide,
                wide,
                wide,
                pl.BlockSpec((1, width), lambda c, tbl: (0, tbl[tab.half] * (local_width // width) + at)),
                pl.BlockSpec((rows.shape[0], BLK), lambda c, tbl: (0, c)),
                pl.BlockSpec((BLK, 128), lambda c, tbl: (c, 0)),
                pl.BlockSpec((8, BLK), lambda c, tbl: (0, c)),
            ],
            out_specs=[narrow] * 3,
            scratch_shapes=[pltpu.VMEM((count, 128, 128), F32)],
        ),
        out_shape=[jax.ShapeDtypeStruct((tokens, width), kind) for kind in (F32, BF16, F32)],
        compiler_params=params(24 * 2**20),
        cost_estimate=pl.CostEstimate(
            flops=8 * tokens * width * BLK, bytes_accessed=10 * tokens * width, transcendentals=0
        ),
        name="attend_own",
    )(table, *map(in_hbm, (query, key, value, gate)), gain, rows, cols, docs)


def enter_kernel(tab, lo, hp, count, table_ref, own_ref, query_ref, factor_ref, cols_ref, state_ref, out_ref, square_ref):
    for c in range(tab.chunks):
        span = slice(c * BLK, (c + 1) * BLK)
        place, slot = table_ref[tab.shard + c], table_ref[tab.slot + c]
        square = jnp.zeros((BLK, 128), F32)
        for h in range(count):
            cols = slice(h * 128, (h + 1) * 128)
            reached = jnp.dot(query_ref[span, cols], state_ref[h], preferred_element_type=F32)
            column = 2 * hp + 8 + lo + h
            attended = own_ref[span, cols] + cols_ref[span, column : column + 1] * reached
            attended = attended.astype(BF16).astype(F32)
            out_ref[place, :, cols] = (attended * factor_ref[span, cols]).astype(BF16)
            square = square + attended * attended
        square_ref[slot] = jnp.sum(square.T, axis=0, keepdims=True)


def attend_entered(tab, table, own, cols, entering, lo, count, hp):
    width = count * 128
    vmem = pl.BlockSpec(memory_space=pltpu.VMEM)
    return pl.pallas_call(
        functools.partial(enter_kernel, tab, lo, hp, count),
        in_specs=[pl.BlockSpec(memory_space=pltpu.SMEM)] + [vmem] * 5,
        out_specs=[vmem] * 2,
        out_shape=[
            jax.ShapeDtypeStruct((tab.chunks, BLK, width), BF16),
            jax.ShapeDtypeStruct((tab.chunks, 1, BLK), F32),
        ],
        compiler_params=params(24 * 2**20),
        cost_estimate=pl.CostEstimate(flops=width, bytes_accessed=width, transcendentals=0),
        name="attend_entered",
    )(table, *own, cols, entering)


def attend_kernel(tab, lo, hp, count, last, *refs):
    ops = tab.n
    (table_ref, query_ref, key_ref, value_ref, gate_ref, gain_ref, rows_ref, cols_ref, docs_ref, state_ref, squares_ref) = refs[:11]
    outs = refs[11 : 11 + ops]
    state, gated = refs[-2:]
    step = pl.program_id(0)

    @pl.when(step == 0)
    def _():
        state[...] = state_ref[...].astype(F32)
        if last:
            gated[BLK:, :] = jnp.zeros((16, gated.shape[1]), BF16)

    barred = barred_pairs(hp, cols_ref, docs_ref)
    square = jnp.zeros((BLK, 128), F32)
    for h in range(count):
        attended = chunk_of_head(
            h, lo + h, hp, barred, query_ref, key_ref, value_ref, rows_ref, cols_ref, state
        )
        square = gate_head(h, attended, square, gain_ref, gate_ref, gated)
    total = jnp.sum(square.T, axis=0, keepdims=True) + squares_ref[0]
    if last:
        lanes, lines = extra_rows(gated.shape[1])
        row = lax.broadcasted_iota(jnp.int32, (16, lanes), 0)
        extra, left = jnp.zeros((16, lanes), F32), total
        for term in range(3):
            part = left.astype(BF16).astype(F32)
            left = left - part
            for line in range(lines):
                piece = part[:, line * lanes : (line + 1) * lanes]
                extra = jnp.where(row == term * lines + line, piece, extra)
        gated[BLK:, :lanes] = extra.astype(BF16)
    else:
        refs[11 + ops][0] = total
    which = table_ref[tab.which + step]
    for op in range(ops):

        @pl.when(which == op)
        def _():
            outs[op][0] = gated[...]


def attend(tab, table, query, key, value, gate, gain, rows, cols, docs, entering, base, lo, count, squares, last):
    tokens, local_width = query.shape
    chunks, per = tab.chunks, tab.per
    ops = tab.n
    hp = rows.shape[0] // 3
    width = count * 128
    at = lo * 128 // width
    height = BLK + 16 * last
    wide = pl.BlockSpec((BLK, width), lambda c, tbl: (c, at))
    square_spec = pl.BlockSpec((1, 1, BLK), lambda c, tbl: (tbl[tab.slot + c], 0, 0))

    def out_map(op, c, tbl):
        return (tbl[tab.place + op * chunks + c], 0, 0)

    out = pl.pallas_call(
        functools.partial(attend_kernel, tab, lo, hp, count, last),
        grid_spec=pltpu.PrefetchScalarGridSpec(
            num_scalar_prefetch=1,
            grid=(chunks,),
            in_specs=[
                wide,
                wide,
                wide,
                wide,
                pl.BlockSpec((1, width), lambda c, tbl: (0, tbl[tab.half] * (local_width // width) + at)),
                pl.BlockSpec((rows.shape[0], BLK), lambda c, tbl: (0, c)),
                pl.BlockSpec((BLK, 128), lambda c, tbl: (c, 0)),
                pl.BlockSpec((8, BLK), lambda c, tbl: (0, c)),
                pl.BlockSpec((count, 128, 128), lambda c, tbl: ((lo - base) // count, 0, 0)),
            ]
            + [square_spec],
            out_specs=[
                pl.BlockSpec((1, height, width), functools.partial(out_map, op)) for op in range(ops)
            ]
            + [square_spec] * (not last),
            scratch_shapes=[
                pltpu.VMEM((count, 128, 128), F32),
                pltpu.VMEM((height, width), BF16),
            ],
        ),
        out_shape=[jax.ShapeDtypeStruct((chunks // ops, height, width), BF16)] * ops
        + [jax.ShapeDtypeStruct((chunks, 1, BLK), F32)] * (not last),
        compiler_params=params(),
        cost_estimate=pl.CostEstimate(flops=16 * tokens * width * BLK, bytes_accessed=10 * tokens * width, transcendentals=tokens * width),
        name="attend",
    )(table, query, key, value, gate, gain, rows, cols, docs, entering, squares)
    return out[:ops], None if last else out[ops]


def place_kernel(features, t, count, lanes, lines, table_ref, *refs):
    out_ref = refs[-1]
    square = []
    for line in range(lines):
        parts = [refs[k][0, term * lines + line : term * lines + line + 1, :] for k in range(t) for term in range(3)]
        square.append(sum(part.astype(F32) for part in parts))
    scale = [lax.rsqrt(row / features + norm_eps) for row in square]
    scale = jnp.concatenate([jnp.broadcast_to(row, (128, lanes)).T for row in scale], axis=0)
    done = 0
    for piece_ref in refs[t : t + count]:
        for c in range(piece_ref.shape[2] // 128):
            piece = piece_ref[0, :BLK, c * 128 : (c + 1) * 128].astype(F32)
            out_ref[:, done : done + 128] = (piece * scale).astype(BF16)
            done += 128


def place(tab, table, op, lo, pieces, extras, out, shape, local_width, features):
    def piece_map(all_blocks, c, tbl):
        block = tbl[tab.side + op] * tab.stride * tab.per + tbl[tab.row + op] if all_blocks else 0
        return (block + c, 0, 0)

    lanes, lines = extra_rows(extras[0].shape[2])
    unit = sum(piece.shape[2] for piece in pieces)

    def out_map(c, tbl):
        return (tbl[tab.row + op] + c, tbl[tab.side + op] * (local_width // unit) + lo * 128 // unit)

    in_specs = [pl.BlockSpec((1, 16, lanes), lambda c, tbl: (c, BLK // 16, 0))] * tab.t
    in_specs += [
        pl.BlockSpec((1, *piece.shape[1:]), functools.partial(piece_map, piece.shape[0] > tab.per))
        for piece in pieces
    ]
    operands = [table, *extras, *pieces]
    aliases = {}
    if out is not None:
        in_specs.append(pl.BlockSpec(memory_space=pl.ANY))
        operands.append(out)
        aliases = {len(operands) - 1: 0}
    return pl.pallas_call(
        functools.partial(place_kernel, features, tab.t, len(pieces), lanes, lines),
        grid_spec=pltpu.PrefetchScalarGridSpec(
            num_scalar_prefetch=1,
            grid=(tab.per,),
            in_specs=in_specs,
            out_specs=pl.BlockSpec((BLK, unit), out_map),
        ),
        out_shape=jax.ShapeDtypeStruct(shape, BF16),
        input_output_aliases=aliases,
        compiler_params=params(63 * 2**20),
        cost_estimate=pl.CostEstimate(flops=unit, bytes_accessed=unit, transcendentals=0),
        name="place",
    )(*operands)


def row_scale(extra_ref, features, t, lanes, lines):
    square = []
    for line in range(lines):
        at = [term * lines + line for term in range(3)]
        parts = [extra_ref[k, row : row + 1, :] for k in range(t) for row in at]
        square.append(sum(part.astype(F32) for part in parts))
    scale = [lax.rsqrt(row / features + norm_eps) for row in square]
    return jnp.concatenate([jnp.broadcast_to(row, (128, lanes)).T for row in scale], axis=0)


def place_last_kernel(tab, features, ops, lo, local_width, lanes, lines, table_ref, *refs):
    t, per, count = tab.t, tab.per, len(ops)
    extras, pieces = refs[: count * t], refs[count * t : count * (t + 1)]
    out_ref, extra, block, extra_in, block_in, block_out = refs[-6:]
    unit = block.shape[2]
    moves, fetched, stores = [], [], []
    for j in range(count):
        for c in range(per):
            for k in range(t):
                source = extras[j * t + k].at[c, pl.ds(BLK, 16), pl.ds(0, lanes)]
                moves.append(pltpu.make_async_copy(source, extra.at[j * per + c, k], extra_in.at[j * per + c, k]))
                moves[-1].start()
    for j in range(count):
        for c in range(per):
            b = j * per + c
            fetched.append(pltpu.make_async_copy(pieces[j].at[c], block.at[b], block_in.at[b]))
            fetched[-1].start()
    for j, op in enumerate(ops):
        row = table_ref[tab.row + op] * BLK
        left = pl.multiple_of(table_ref[tab.side + op] * local_width + lo * 128, 128)
        for c in range(per):
            b = j * per + c
            for k in range(t):
                moves[b * t + k].wait()
            scale = row_scale(extra.at[b], features, t, lanes, lines)
            fetched[b].wait()
            for col in range(0, unit, 128):
                cols = slice(col, col + 128)
                block[b, :, cols] = (block[b, :, cols].astype(F32) * scale).astype(BF16)
            top = pl.multiple_of(row + c * BLK, BLK)
            stores.append(
                pltpu.make_async_copy(
                    block.at[b], out_ref.at[pl.ds(top, BLK), pl.ds(left, unit)], block_out.at[b]
                )
            )
            stores[-1].start()
    for store in stores:
        store.wait()


def place_last(tab, table, ops, lo, pieces, extras, out, local_width, features):
    lanes, lines = extra_rows(extras[0].shape[2])
    blocks = len(ops) * tab.per
    hbm = pl.BlockSpec(memory_space=pl.ANY)
    operands = [table, *extras, *pieces, out]
    return pl.pallas_call(
        functools.partial(place_last_kernel, tab, features, ops, lo, local_width, lanes, lines),
        in_specs=[pl.BlockSpec(memory_space=pltpu.SMEM)] + [hbm] * (len(operands) - 1),
        out_specs=hbm,
        out_shape=jax.ShapeDtypeStruct(out.shape, BF16),
        scratch_shapes=[
            pltpu.VMEM((blocks, tab.t, 16, lanes), BF16),
            pltpu.VMEM((blocks, BLK, pieces[0].shape[2]), BF16),
            pltpu.SemaphoreType.DMA((blocks, tab.t)),
            pltpu.SemaphoreType.DMA((blocks,)),
            pltpu.SemaphoreType.DMA((blocks,)),
        ],
        input_output_aliases={len(operands) - 1: 0},
        compiler_params=params(63 * 2**20),
        cost_estimate=pl.CostEstimate(flops=lanes, bytes_accessed=lanes, transcendentals=0),
        name="place_last",
    )(*operands)


def local(query_rows, key_rows, value_rows, gate_rows, decay_log, norm_gain, doc_lengths, block_shard):
    tokens, width = query_rows.shape
    heads = decay_log.shape[0]
    features = norm_gain.shape[0]
    n, t = lax.axis_size("ctx"), lax.axis_size("tp")
    tab = Table(n, t, tokens // BLK)
    quarter = max(1, heads // 4)

    rest = heads - quarter
    rows, cols, docs, total_gate, table, low, full = prelude(
        tab, doc_lengths, block_shard, decay_log, key_rows, value_rows
    )
    gain = norm_gain.reshape(1, features)
    hop = [(i, i + 1) for i in range(n - 1)]

    def route(op):
        return [
            (d * t + k, (d + op + k * tab.stride) % n * t + d // tab.stride)
            for d in range(n)
            for k in range(t)
        ]

    carry = total_gate[:, :1, None]

    def merge(arrived, part):
        return (carry[part] * arrived[part].astype(F32) + full[part]).astype(BF16)

    first, others = slice(rest, heads), slice(0, rest)
    for _ in range(max(1, n // 2) - 2):
        low = merge(lax.ppermute(low, "ctx", hop), slice(0, heads))
    parts = [low[first], low[others]]
    if n // 2 > 1:
        arrived = lax.ppermute(low, "ctx", hop)
        parts = [merge(arrived, first), merge(arrived, others)]
    own = attend_own(
        tab, table, query_rows, key_rows, value_rows, gate_rows, gain, rows, cols, docs, rest, quarter
    )
    parts, own = lax.optimization_barrier((parts, own))
    early, entering = (lax.ppermute(part, "ctx", hop) for part in parts)
    ready, squares = attend_entered(tab, table, own, cols, early, rest, quarter, rows.shape[0] // 3)
    gated = [None]
    for lo, count in ((0, 2 * quarter), (2 * quarter, quarter)):
        outs, squares = attend(
            tab, table, query_rows, key_rows, value_rows, gate_rows, gain, rows, cols, docs,
            entering, 0, lo, count, squares, lo > 0,
        )
        gated.append(outs)
    head = lax.all_to_all(ready, "ctx", split_axis=0, concat_axis=0, tiled=True)
    head = lax.all_to_all(head, "tp", split_axis=0, concat_axis=0, tiled=True)
    tail = [lax.ppermute(gated[2][op], ("ctx", "tp"), route(op)) for op in range(n)]
    middle = []
    for op in range(n):
        ready = gated[1][op]
        for before in ([], [0, n - 1])[op] if op < 2 else [op - 1]:
            ready, tail[before] = lax.optimization_barrier((ready, tail[before]))
        middle.append(lax.ppermute(ready, ("ctx", "tp"), route(op)))

    shape = (tokens // t, features)
    out = None

    def extras(op):
        return [tail[(op + k * tab.stride) % n] for k in range(t)]

    for op in range(n):
        out = place(tab, table, op, 2 * quarter, [tail[op], head], extras(op), out, shape, width, features)
    for op in range(n - 2):
        out = place(tab, table, op, 0, [middle[op]], extras(op), out, shape, width, features)
    last = (n - 2, n - 1)
    return place_last(
        tab, table, last, 0, middle[n - 2 :], [extra for op in last for extra in extras(op)], out, width, features
    )


def solution(mesh):
    return jax.shard_map(
        local,
        mesh=mesh,
        in_specs=(
            P(("dp", "ctx"), "tp"),
            P(("dp", "ctx"), "tp"),
            P(("dp", "ctx"), "tp"),
            P(("dp", "ctx"), "tp"),
            P("tp", ("dp", "ctx")),
            P(),
            P("dp"),
            P("dp"),
        ),
        out_specs=P(("dp", "ctx", "tp"), None),
        check_vma=False,
    )
```

```python
import functools

import jax
import jax.numpy as jnp
from jax import lax
from jax.experimental import pallas as pl
from jax.experimental.pallas import tpu as pltpu
from jax.sharding import PartitionSpec as P

BLK = 256
norm_eps = 1e-05
VMEM_LIMIT = 56 * 2**20
F32 = jnp.float32
BF16 = jnp.bfloat16


def params(limit=VMEM_LIMIT):
    return pltpu.CompilerParams(vmem_limit_bytes=limit)


def in_hbm(array):
    return pltpu.with_memory_space_constraint(array, pltpu.HBM)


def whole(shape):
    return pl.BlockSpec(shape, lambda *_: (0,) * len(shape))


def extra_rows(width):
    lanes = min(width, BLK)
    return lanes, BLK // lanes


def pad8(count):
    return -(-count // 8) * 8


class Table:
    def __init__(self, n, t, chunks):
        self.n, self.t, self.chunks = n, t, chunks
        self.stride, self.per = n // t, chunks // n
        self.half = 0
        self.which = 1
        self.slot = self.which + chunks
        self.place = self.slot + chunks
        self.row = self.place + n * chunks
        self.side = self.row + n
        self.shard = self.side + n
        self.size = self.shard + chunks


def fill_table(tab, shard_ref, table_ref):
    n, per, chunks = tab.n, tab.per, tab.chunks
    ctx, tp = lax.axis_index("ctx"), lax.axis_index("tp")
    table_ref[tab.half] = tp
    seen = [jnp.int32(0)] * n
    for c in range(chunks):
        shard = shard_ref[ctx * chunks + c]
        op = lax.rem(shard - ctx - tp * tab.stride + 2 * n, n)
        table_ref[tab.which + c] = op
        rank = jnp.int32(0)
        for k in range(n):
            table_ref[tab.place + k * chunks + c] = jnp.minimum(seen[k], per - 1)
            here = (op == k).astype(jnp.int32)
            rank = rank + here * seen[k]
            seen[k] = seen[k] + here
        table_ref[tab.slot + c] = op * per + jnp.minimum(rank, per - 1)
        table_ref[tab.shard + c] = shard * per + jnp.minimum(rank, per - 1)
    for op in range(n):
        lane = lax.rem(ctx - op + n, tab.stride)
        source = tp * tab.stride + lane
        table_ref[tab.row + op] = lane * per
        table_ref[tab.side + op] = lax.rem(ctx - op - source + 2 * n, n) // tab.stride


def fill_gates(len_ref, decay_ref, rows_ref, cols_ref, docs_ref, total_ref, tail_ref, scr, stack):
    heads, tokens = decay_ref.shape
    hp = pad8(heads)
    chunks = tokens // BLK
    base = lax.axis_index("ctx") * tokens
    starts, run = [], jnp.int32(0)
    for i in range(len_ref.shape[0]):
        starts.append(run)
        run = run + len_ref[i]

    def doc_at(position):
        found = jnp.int32(0)
        for start in starts:
            found = found + (position >= start).astype(jnp.int32)
        return found - 1

    position = base + lax.broadcasted_iota(jnp.int32, (8, tokens), 1)
    doc = jnp.zeros((8, tokens), jnp.int32) - 1
    for start in starts:
        doc = doc + (position >= start).astype(jnp.int32)
    docs_ref[...] = doc.astype(F32)
    edges = [doc_at(base - 1)] + [doc_at(base + (c + 1) * BLK - 1) for c in range(chunks)]

    first = lax.broadcasted_iota(jnp.int32, (BLK, BLK), 0)
    second = lax.broadcasted_iota(jnp.int32, (BLK, BLK), 1)
    upto = jnp.where(first <= second, 1.0, 0.0).astype(BF16)
    stack[...] = jnp.zeros_like(stack)
    for c in range(chunks):
        stack[c * hp : c * hp + heads, :] = decay_ref[:, c * BLK : (c + 1) * BLK]
    left, terms = stack[...], []
    for _ in range(3):
        terms.append(left.astype(BF16))
        left = left - terms[-1].astype(F32)
    high, middle, low = (jnp.dot(term, upto, preferred_element_type=F32) for term in terms)
    stack[...] = high + (middle + low)
    scr[...] = jnp.zeros_like(scr)
    cums = [stack[c * hp : c * hp + heads, :] for c in range(chunks)]
    sums = [jnp.broadcast_to(cum[:, BLK - 1 :], cum.shape) for cum in cums]
    before, after = [], [None] * chunks
    run = jnp.zeros_like(sums[0])
    for c in range(chunks):
        before.append(run)
        run = run + sums[c]
    run = jnp.zeros_like(sums[0])
    for c in reversed(range(chunks)):
        after[c] = run
        run = run + sums[c]
    for c in range(chunks):
        span = slice(c * BLK, (c + 1) * BLK)
        doc_c = doc[:1, span]
        cum, total = cums[c], sums[c]
        rows_ref[0:heads, span] = cum
        rows_ref[hp : hp + heads, span] = jnp.where(doc_c == edges[c + 1], jnp.exp(total - cum), 0.0)
        tail_ref[0:heads, span] = jnp.where(doc_c == edges[-1], jnp.exp(total - cum + after[c]), 0.0)
        rows_ref[2 * hp : 2 * hp + heads, span] = jnp.where(
            edges[c + 1] == edges[c], jnp.exp(total), 0.0
        )
        scr[0:heads, span] = cum
        scr[hp : hp + heads, span] = jnp.where(doc_c == edges[c], jnp.exp(cum), 0.0)
        scr[2 * hp + 8 : 2 * hp + 8 + heads, span] = jnp.where(
            doc_c == edges[0], jnp.exp(before[c] + cum), 0.0
        )
    scr[2 * hp : 2 * hp + 8, :] = doc.astype(F32)
    cols_ref[...] = scr[...].T
    total_ref[...] = jnp.where(edges[-1] == edges[0], jnp.exp(run[:, :128]), 0.0)


def prelude_kernel(tab, tile, len_ref, shard_ref, decay_ref, key_hbm, value_hbm, *refs):
    rows_ref, cols_ref, docs_ref, total_ref, table_ref, low_ref, full_ref = refs[:7]
    tail_ref, scr, stack, key_ref, value_ref, arrived = refs[7:]
    tokens = key_ref.shape[0]
    heads = full_ref.shape[0]
    copies = []
    for i in range(tokens // tile):
        span = pl.ds(i * tile, tile)
        for k, (source, target) in enumerate(((key_hbm, key_ref), (value_hbm, value_ref))):
            copies.append(pltpu.make_async_copy(source.at[span], target.at[span], arrived.at[k, i]))
            copies[-1].start()
    fill_table(tab, shard_ref, table_ref)
    fill_gates(len_ref, decay_ref, rows_ref, cols_ref, docs_ref, total_ref, tail_ref, scr, stack)
    for i in range(tokens // tile):
        copies[2 * i].wait()
        copies[2 * i + 1].wait()
        span = slice(i * tile, (i + 1) * tile)
        for h in range(heads):
            cols = slice(h * 128, (h + 1) * 128)
            scaled = (key_ref[span, cols].T.astype(F32) * tail_ref[h : h + 1, span]).astype(BF16)
            part = jnp.dot(scaled, value_ref[span, cols], preferred_element_type=F32)
            full_ref[h] = full_ref[h] + part if i else part
    low_ref[...] = full_ref[...].astype(BF16)


def prelude(tab, doc_lengths, block_shard, decay, key, value):
    heads, tokens = decay.shape
    hp = pad8(heads)
    tile = 2 * BLK
    smem = pl.BlockSpec(memory_space=pltpu.SMEM)
    vmem = pl.BlockSpec(memory_space=pltpu.VMEM)
    hbm = pl.BlockSpec(memory_space=pl.ANY)
    shapes = [(3 * hp, tokens), (tokens, 128), (8, tokens), (heads, 128)]
    return pl.pallas_call(
        functools.partial(prelude_kernel, tab, tile),
        in_specs=[smem, smem, vmem, hbm, hbm],
        out_specs=[vmem] * 4 + [smem] + [vmem] * 2,
        out_shape=[jax.ShapeDtypeStruct(shape, F32) for shape in shapes]
        + [jax.ShapeDtypeStruct((tab.size,), jnp.int32)]
        + [jax.ShapeDtypeStruct((heads, 128, 128), kind) for kind in (BF16, F32)],
        scratch_shapes=[
            pltpu.VMEM((hp, tokens), F32),
            pltpu.VMEM((128, tokens), F32),
            pltpu.VMEM((tokens // BLK * hp, BLK), F32),
            pltpu.VMEM(key.shape, BF16),
            pltpu.VMEM(value.shape, BF16),
            pltpu.SemaphoreType.DMA((2, tokens // tile)),
        ],
        compiler_params=params(32 * 2**20),
        name="prelude",
    )(*map(in_hbm, (doc_lengths, block_shard, decay, key, value)))


def barred_pairs(hp, cols_ref, docs_ref):
    first = lax.broadcasted_iota(jnp.int32, (BLK, BLK), 0)
    second = lax.broadcasted_iota(jnp.int32, (BLK, BLK), 1)
    same = cols_ref[:, 2 * hp : 2 * hp + 1] == docs_ref[0:1, :]
    return jnp.where((first >= second) & same, 0.0, -1e30).astype(F32)


def chunk_of_head(h, head, hp, barred, query_ref, key_ref, value_ref, rows_ref, cols_ref, state):
    cols = slice(h * 128, (h + 1) * 128)
    query, value = query_ref[:, cols], value_ref[:, cols]
    key_t = key_ref[:, cols].T
    scores = jnp.dot(query, key_t, preferred_element_type=F32)
    gap = cols_ref[:, head : head + 1] - rows_ref[head : head + 1, :] + barred
    weights = (scores * jnp.exp(gap)).astype(BF16)
    intra = jnp.dot(weights, value, preferred_element_type=F32)
    reached = jnp.dot(query, state[h].astype(BF16), preferred_element_type=F32)
    scaled = (key_t.astype(F32) * rows_ref[hp + head : hp + head + 1, :]).astype(BF16)
    carry = rows_ref[2 * hp + head : 2 * hp + head + 1, :128]
    state[h] = carry * state[h] + jnp.dot(scaled, value, preferred_element_type=F32)
    return intra + cols_ref[:, hp + head : hp + head + 1] * reached


def gate_head(h, attended, square, gain_ref, gate_ref, gated):
    cols = slice(h * 128, (h + 1) * 128)
    attended = attended.astype(BF16).astype(F32)
    gated[:BLK, cols] = (
        attended * gain_ref[0:1, cols] * jax.nn.sigmoid(gate_ref[:, cols].astype(F32))
    ).astype(BF16)
    return square + attended * attended


def own_kernel(lo, hp, count, *refs):
    (_, query_ref, key_ref, value_ref, gate_ref, gain_ref, rows_ref, cols_ref, docs_ref) = refs[:9]
    own_ref, same_ref, factor_ref, state = refs[9:]

    @pl.when(pl.program_id(0) == 0)
    def _():
        state[...] = jnp.zeros_like(state)

    barred = barred_pairs(hp, cols_ref, docs_ref)
    for h in range(count):
        own_ref[:, h * 128 : (h + 1) * 128] = chunk_of_head(
            h, lo + h, hp, barred, query_ref, key_ref, value_ref, rows_ref, cols_ref, state
        )
    same_ref[...] = query_ref[...]
    factor_ref[...] = gain_ref[0:1, :] * jax.nn.sigmoid(gate_ref[...].astype(F32))


def attend_own(tab, table, query, key, value, gate, gain, rows, cols, docs, lo, count):
    tokens, local_width = query.shape
    hp = rows.shape[0] // 3
    width = count * 128
    at = lo * 128 // width
    wide = pl.BlockSpec((BLK, width), lambda c, tbl: (c, at))
    narrow = pl.BlockSpec((BLK, width), lambda c, tbl: (c, 0))
    return pl.pallas_call(
        functools.partial(own_kernel, lo, hp, count),
        grid_spec=pltpu.PrefetchScalarGridSpec(
            num_scalar_prefetch=1,
            grid=(tokens // BLK,),
            in_specs=[
                wide,
                wide,
                wide,
                wide,
                pl.BlockSpec((1, width), lambda c, tbl: (0, tbl[tab.half] * (local_width // width) + at)),
                pl.BlockSpec((rows.shape[0], BLK), lambda c, tbl: (0, c)),
                pl.BlockSpec((BLK, 128), lambda c, tbl: (c, 0)),
                pl.BlockSpec((8, BLK), lambda c, tbl: (0, c)),
            ],
            out_specs=[narrow] * 3,
            scratch_shapes=[pltpu.VMEM((count, 128, 128), F32)],
        ),
        out_shape=[jax.ShapeDtypeStruct((tokens, width), kind) for kind in (F32, BF16, F32)],
        compiler_params=params(24 * 2**20),
        cost_estimate=pl.CostEstimate(
            flops=8 * tokens * width * BLK, bytes_accessed=10 * tokens * width, transcendentals=0
        ),
        name="attend_own",
    )(table, *map(in_hbm, (query, key, value, gate)), gain, rows, cols, docs)


def enter_kernel(tab, lo, hp, count, table_ref, own_ref, query_ref, factor_ref, cols_ref, state_ref, out_ref, square_ref):
    for c in range(tab.chunks):
        span = slice(c * BLK, (c + 1) * BLK)
        place, slot = table_ref[tab.shard + c], table_ref[tab.slot + c]
        square = jnp.zeros((BLK, 128), F32)
        for h in range(count):
            cols = slice(h * 128, (h + 1) * 128)
            reached = jnp.dot(query_ref[span, cols], state_ref[h], preferred_element_type=F32)
            column = 2 * hp + 8 + lo + h
            attended = own_ref[span, cols] + cols_ref[span, column : column + 1] * reached
            attended = attended.astype(BF16).astype(F32)
            out_ref[place, :, cols] = (attended * factor_ref[span, cols]).astype(BF16)
            square = square + attended * attended
        square_ref[slot] = jnp.sum(square.T, axis=0, keepdims=True)


def attend_entered(tab, table, own, cols, entering, lo, count, hp):
    width = count * 128
    vmem = pl.BlockSpec(memory_space=pltpu.VMEM)
    return pl.pallas_call(
        functools.partial(enter_kernel, tab, lo, hp, count),
        in_specs=[pl.BlockSpec(memory_space=pltpu.SMEM)] + [vmem] * 5,
        out_specs=[vmem] * 2,
        out_shape=[
            jax.ShapeDtypeStruct((tab.chunks, BLK, width), BF16),
            jax.ShapeDtypeStruct((tab.chunks, 1, BLK), F32),
        ],
        compiler_params=params(24 * 2**20),
        cost_estimate=pl.CostEstimate(flops=width, bytes_accessed=width, transcendentals=0),
        name="attend_entered",
    )(table, *own, cols, entering)


def attend_kernel(tab, lo, hp, count, last, *refs):
    ops = tab.n
    (table_ref, query_ref, key_ref, value_ref, gate_ref, gain_ref, rows_ref, cols_ref, docs_ref, state_ref, squares_ref) = refs[:11]
    outs = refs[11 : 11 + ops]
    state, gated = refs[-2:]
    step = pl.program_id(0)

    @pl.when(step == 0)
    def _():
        state[...] = state_ref[...].astype(F32)

    barred = barred_pairs(hp, cols_ref, docs_ref)
    square = jnp.zeros((BLK, 128), F32)
    for h in range(count):
        attended = chunk_of_head(
            h, lo + h, hp, barred, query_ref, key_ref, value_ref, rows_ref, cols_ref, state
        )
        square = gate_head(h, attended, square, gain_ref, gate_ref, gated)
    total = jnp.sum(square.T, axis=0, keepdims=True) + squares_ref[0]
    if last:
        lanes, lines = extra_rows(gated.shape[1])
        row = lax.broadcasted_iota(jnp.int32, (16, lanes), 0)
        extra, left = jnp.zeros((16, lanes), F32), total
        for term in range(3):
            part = left.astype(BF16).astype(F32)
            left = left - part
            for line in range(lines):
                piece = part[:, line * lanes : (line + 1) * lanes]
                extra = jnp.where(row == term * lines + line, piece, extra)
    else:
        refs[11 + ops][0] = total
    which = table_ref[tab.which + step]
    for op in range(ops):

        @pl.when(which == op)
        def _():
            outs[op][...] = gated[...]
            if last:
                refs[11 + ops + op][...] = extra.astype(BF16)


def stitch_kernel(count, *refs):
    extras, outs, arrived = refs[:count], refs[2 * count : 3 * count], refs[-1]
    copies = []
    for k in range(count):
        target = outs[k].at[pl.ds(outs[k].shape[0] - 16, 16)]
        copies.append(pltpu.make_async_copy(extras[k], target, arrived.at[k]))
        copies[-1].start()
    for copy in copies:
        copy.wait()


def stitch(pieces, extras):
    count = len(pieces)
    hbm = pl.BlockSpec(memory_space=pl.ANY)
    return pl.pallas_call(
        functools.partial(stitch_kernel, count),
        in_specs=[hbm] * (2 * count),
        out_specs=[hbm] * count,
        out_shape=[jax.ShapeDtypeStruct(piece.shape, BF16) for piece in pieces],
        scratch_shapes=[pltpu.SemaphoreType.DMA((count,))],
        input_output_aliases={count + k: k for k in range(count)},
        compiler_params=params(63 * 2**20),
        cost_estimate=pl.CostEstimate(flops=128, bytes_accessed=128, transcendentals=0),
        name="stitch",
    )(*extras, *pieces)


def attend(tab, table, query, key, value, gate, gain, rows, cols, docs, entering, base, lo, count, squares, last):
    tokens, local_width = query.shape
    chunks, per = tab.chunks, tab.per
    ops = tab.n
    hp = rows.shape[0] // 3
    width = count * 128
    at = lo * 128 // width
    lanes, _ = extra_rows(width)
    wide = pl.BlockSpec((BLK, width), lambda c, tbl: (c, at))
    square_spec = pl.BlockSpec((1, 1, BLK), lambda c, tbl: (tbl[tab.slot + c], 0, 0))

    def out_map(op, c, tbl):
        return (tbl[tab.place + op * chunks + c], 0)

    def extra_map(op, c, tbl):
        return (0, tbl[tab.place + op * chunks + c])

    if last:
        square_specs = [pl.BlockSpec((16, lanes), functools.partial(extra_map, op)) for op in range(ops)]
        square_shapes = [jax.ShapeDtypeStruct((16, width), BF16)] * ops
    else:
        square_specs, square_shapes = [square_spec], [jax.ShapeDtypeStruct((chunks, 1, BLK), F32)]
    out = pl.pallas_call(
        functools.partial(attend_kernel, tab, lo, hp, count, last),
        grid_spec=pltpu.PrefetchScalarGridSpec(
            num_scalar_prefetch=1,
            grid=(chunks,),
            in_specs=[
                wide,
                wide,
                wide,
                wide,
                pl.BlockSpec((1, width), lambda c, tbl: (0, tbl[tab.half] * (local_width // width) + at)),
                pl.BlockSpec((rows.shape[0], BLK), lambda c, tbl: (0, c)),
                pl.BlockSpec((BLK, 128), lambda c, tbl: (c, 0)),
                pl.BlockSpec((8, BLK), lambda c, tbl: (0, c)),
                pl.BlockSpec((count, 128, 128), lambda c, tbl: ((lo - base) // count, 0, 0)),
            ]
            + [square_spec],
            out_specs=[
                pl.BlockSpec((BLK, width), functools.partial(out_map, op)) for op in range(ops)
            ]
            + square_specs,
            scratch_shapes=[
                pltpu.VMEM((count, 128, 128), F32),
                pltpu.VMEM((BLK, width), BF16),
            ],
        ),
        out_shape=[jax.ShapeDtypeStruct((per * BLK + 16 * last, width), BF16)] * ops + square_shapes,
        compiler_params=params(),
        cost_estimate=pl.CostEstimate(flops=16 * tokens * width * BLK, bytes_accessed=10 * tokens * width, transcendentals=tokens * width),
        name="attend",
    )(table, query, key, value, gate, gain, rows, cols, docs, entering, squares)
    if last:
        return stitch(out[:ops], out[ops:]), None
    return out[:ops], out[ops]


def row_scale(extras, features, lanes, lines):
    square = []
    for line in range(lines):
        at = [term * lines + line for term in range(3)]
        parts = [extra[row : row + 1, :] for extra in extras for row in at]
        square.append(sum(part.astype(F32) for part in parts))
    scale = [lax.rsqrt(row / features + norm_eps) for row in square]
    return jnp.concatenate([jnp.broadcast_to(row, (128, lanes)).T for row in scale], axis=0)


def place_kernel(features, t, count, lanes, lines, table_ref, *refs):
    out_ref = refs[-1]
    scale = row_scale(refs[:t], features, lanes, lines)
    done = 0
    for piece_ref in refs[t : t + count]:
        for c in range(piece_ref.shape[1] // 128):
            piece = piece_ref[:, c * 128 : (c + 1) * 128].astype(F32)
            out_ref[:, done : done + 128] = (piece * scale).astype(BF16)
            done += 128


def place(tab, table, op, lo, pieces, extras, out, shape, local_width, features):
    rows = tab.per * BLK

    def piece_map(all_blocks, c, tbl):
        block = tbl[tab.side + op] * tab.stride * tab.per + tbl[tab.row + op] if all_blocks else 0
        return (block + c, 0)

    lanes, lines = extra_rows(extras[0].shape[1])
    unit = sum(piece.shape[1] for piece in pieces)

    def out_map(c, tbl):
        return (tbl[tab.row + op] + c, tbl[tab.side + op] * (local_width // unit) + lo * 128 // unit)

    in_specs = [pl.BlockSpec((16, lanes), lambda c, tbl: (rows // 16, c))] * tab.t
    in_specs += [
        pl.BlockSpec((BLK, piece.shape[1]), functools.partial(piece_map, piece.shape[0] == tab.chunks * BLK))
        for piece in pieces
    ]
    operands = [table, *extras, *pieces]
    aliases = {}
    if out is not None:
        in_specs.append(pl.BlockSpec(memory_space=pl.ANY))
        operands.append(out)
        aliases = {len(operands) - 1: 0}
    return pl.pallas_call(
        functools.partial(place_kernel, features, tab.t, len(pieces), lanes, lines),
        grid_spec=pltpu.PrefetchScalarGridSpec(
            num_scalar_prefetch=1,
            grid=(tab.per,),
            in_specs=in_specs,
            out_specs=pl.BlockSpec((BLK, unit), out_map),
        ),
        out_shape=jax.ShapeDtypeStruct(shape, BF16),
        input_output_aliases=aliases,
        compiler_params=params(63 * 2**20),
        cost_estimate=pl.CostEstimate(flops=unit, bytes_accessed=unit, transcendentals=0),
        name="place",
    )(*operands)


def place_last_kernel(tab, features, ops, lo, local_width, lanes, lines, table_ref, *refs):
    t, per, count = tab.t, tab.per, len(ops)
    extras, pieces = refs[: count * t], refs[count * t : count * (t + 1)]
    out_ref, extra, block, extra_in, block_in, block_out = refs[-6:]
    unit, rows = block.shape[2], per * BLK
    moves, fetched, stores = [], [], []
    for j in range(count):
        for c in range(per):
            for k in range(t):
                source = extras[j * t + k].at[pl.ds(rows, 16), pl.ds(c * lanes, lanes)]
                moves.append(pltpu.make_async_copy(source, extra.at[j * per + c, k], extra_in.at[j * per + c, k]))
                moves[-1].start()
    for j in range(count):
        for c in range(per):
            b = j * per + c
            fetched.append(pltpu.make_async_copy(pieces[j].at[pl.ds(c * BLK, BLK)], block.at[b], block_in.at[b]))
            fetched[-1].start()
    for j, op in enumerate(ops):
        row = table_ref[tab.row + op] * BLK
        left = pl.multiple_of(table_ref[tab.side + op] * local_width + lo * 128, 128)
        for c in range(per):
            b = j * per + c
            for k in range(t):
                moves[b * t + k].wait()
            scale = row_scale([extra.at[b, k] for k in range(t)], features, lanes, lines)
            fetched[b].wait()
            for col in range(0, unit, 128):
                cols = slice(col, col + 128)
                block[b, :, cols] = (block[b, :, cols].astype(F32) * scale).astype(BF16)
            top = pl.multiple_of(row + c * BLK, BLK)
            stores.append(
                pltpu.make_async_copy(
                    block.at[b], out_ref.at[pl.ds(top, BLK), pl.ds(left, unit)], block_out.at[b]
                )
            )
            stores[-1].start()
    for store in stores:
        store.wait()


def place_last(tab, table, ops, lo, pieces, extras, out, local_width, features):
    lanes, lines = extra_rows(extras[0].shape[1])
    blocks = len(ops) * tab.per
    hbm = pl.BlockSpec(memory_space=pl.ANY)
    operands = [table, *extras, *pieces, out]
    return pl.pallas_call(
        functools.partial(place_last_kernel, tab, features, ops, lo, local_width, lanes, lines),
        in_specs=[pl.BlockSpec(memory_space=pltpu.SMEM)] + [hbm] * (len(operands) - 1),
        out_specs=hbm,
        out_shape=jax.ShapeDtypeStruct(out.shape, BF16),
        scratch_shapes=[
            pltpu.VMEM((blocks, tab.t, 16, lanes), BF16),
            pltpu.VMEM((blocks, BLK, pieces[0].shape[1]), BF16),
            pltpu.SemaphoreType.DMA((blocks, tab.t)),
            pltpu.SemaphoreType.DMA((blocks,)),
            pltpu.SemaphoreType.DMA((blocks,)),
        ],
        input_output_aliases={len(operands) - 1: 0},
        compiler_params=params(63 * 2**20),
        cost_estimate=pl.CostEstimate(flops=lanes, bytes_accessed=lanes, transcendentals=0),
        name="place_last",
    )(*operands)


def local(query_rows, key_rows, value_rows, gate_rows, decay_log, norm_gain, doc_lengths, block_shard):
    tokens, width = query_rows.shape
    heads = decay_log.shape[0]
    features = norm_gain.shape[0]
    n, t = lax.axis_size("ctx"), lax.axis_size("tp")
    tab = Table(n, t, tokens // BLK)
    quarter = max(1, heads // 4)

    rest = heads - quarter
    rows, cols, docs, total_gate, table, low, full = prelude(
        tab, doc_lengths, block_shard, decay_log, key_rows, value_rows
    )
    gain = norm_gain.reshape(1, features)
    hop = [(i, i + 1) for i in range(n - 1)]

    def route(op):
        return [
            (d * t + k, (d + op + k * tab.stride) % n * t + d // tab.stride)
            for d in range(n)
            for k in range(t)
        ]

    carry = total_gate[:, :1, None]

    def merge(arrived, part):
        return (carry[part] * arrived[part].astype(F32) + full[part]).astype(BF16)

    first, others = slice(rest, heads), slice(0, rest)
    for _ in range(max(1, n // 2) - 2):
        low = merge(lax.ppermute(low, "ctx", hop), slice(0, heads))
    parts = [low[first], low[others]]
    if n // 2 > 1:
        arrived = lax.ppermute(low, "ctx", hop)
        parts = [merge(arrived, first), merge(arrived, others)]
    own = attend_own(
        tab, table, query_rows, key_rows, value_rows, gate_rows, gain, rows, cols, docs, rest, quarter
    )
    parts, own = lax.optimization_barrier((parts, own))
    early, entering = (lax.ppermute(part, "ctx", hop) for part in parts)
    ready, squares = attend_entered(tab, table, own, cols, early, rest, quarter, rows.shape[0] // 3)
    gated = [None]
    for lo, count in ((0, 2 * quarter), (2 * quarter, quarter)):
        outs, squares = attend(
            tab, table, query_rows, key_rows, value_rows, gate_rows, gain, rows, cols, docs,
            entering, 0, lo, count, squares, lo > 0,
        )
        gated.append(outs)
    head = lax.all_to_all(ready, "ctx", split_axis=0, concat_axis=0, tiled=True)
    head = lax.all_to_all(head, "tp", split_axis=0, concat_axis=0, tiled=True).reshape(tokens, -1)
    tail = [lax.ppermute(gated[2][op], ("ctx", "tp"), route(op)) for op in range(n)]
    middle = []
    for op in range(n):
        ready = gated[1][op]
        for before in ([], [0, n - 1])[op] if op < 2 else [op - 1]:
            ready, tail[before] = lax.optimization_barrier((ready, tail[before]))
        middle.append(lax.ppermute(ready, ("ctx", "tp"), route(op)))

    shape = (tokens // t, features)
    out = None

    def extras(op):
        return [tail[(op + k * tab.stride) % n] for k in range(t)]

    for op in range(n):
        out = place(tab, table, op, 2 * quarter, [tail[op], head], extras(op), out, shape, width, features)
    for op in range(n - 2):
        out = place(tab, table, op, 0, [middle[op]], extras(op), out, shape, width, features)
    last = (n - 2, n - 1)
    return place_last(
        tab, table, last, 0, middle[n - 2 :], [extra for op in last for extra in extras(op)], out, width, features
    )


def solution(mesh):
    return jax.shard_map(
        local,
        mesh=mesh,
        in_specs=(
            P(("dp", "ctx"), "tp"),
            P(("dp", "ctx"), "tp"),
            P(("dp", "ctx"), "tp"),
            P(("dp", "ctx"), "tp"),
            P("tp", ("dp", "ctx")),
            P(),
            P("dp"),
            P("dp"),
        ),
        out_specs=P(("dp", "ctx", "tp"), None),
        check_vma=False,
    )
```

```python
import functools

import jax
import jax.numpy as jnp
from jax import lax
from jax.experimental import pallas as pl
from jax.experimental.pallas import tpu as pltpu
from jax.sharding import PartitionSpec as P

BLK = 256
norm_eps = 1e-05
VMEM_LIMIT = 56 * 2**20
F32 = jnp.float32
BF16 = jnp.bfloat16


def params(limit=VMEM_LIMIT):
    return pltpu.CompilerParams(vmem_limit_bytes=limit)


def in_hbm(array):
    return pltpu.with_memory_space_constraint(array, pltpu.HBM)


def whole(shape):
    return pl.BlockSpec(shape, lambda *_: (0,) * len(shape))


def extra_rows(width):
    lanes = min(width, BLK)
    return lanes, BLK // lanes


def pad8(count):
    return -(-count // 8) * 8


class Table:
    def __init__(self, n, t, chunks):
        self.n, self.t, self.chunks = n, t, chunks
        self.stride, self.per = n // t, chunks // n
        self.half = 0
        self.which = 1
        self.slot = self.which + chunks
        self.place = self.slot + chunks
        self.row = self.place + n * chunks
        self.side = self.row + n
        self.shard = self.side + n
        self.size = self.shard + chunks


def fill_table(tab, shard_ref, table_ref):
    n, per, chunks = tab.n, tab.per, tab.chunks
    ctx, tp = lax.axis_index("ctx"), lax.axis_index("tp")
    table_ref[tab.half] = tp
    seen = [jnp.int32(0)] * n
    for c in range(chunks):
        shard = shard_ref[ctx * chunks + c]
        op = lax.rem(shard - ctx - tp * tab.stride + 2 * n, n)
        table_ref[tab.which + c] = op
        rank = jnp.int32(0)
        for k in range(n):
            table_ref[tab.place + k * chunks + c] = jnp.minimum(seen[k], per - 1)
            here = (op == k).astype(jnp.int32)
            rank = rank + here * seen[k]
            seen[k] = seen[k] + here
        table_ref[tab.slot + c] = op * per + jnp.minimum(rank, per - 1)
        table_ref[tab.shard + c] = shard * per + jnp.minimum(rank, per - 1)
    for op in range(n):
        lane = lax.rem(ctx - op + n, tab.stride)
        source = tp * tab.stride + lane
        table_ref[tab.row + op] = lane * per
        table_ref[tab.side + op] = lax.rem(ctx - op - source + 2 * n, n) // tab.stride


def fill_gates(len_ref, decay_ref, rows_ref, cols_ref, docs_ref, total_ref, tail_ref, scr, stack):
    heads, tokens = decay_ref.shape
    hp = pad8(heads)
    chunks = tokens // BLK
    base = lax.axis_index("ctx") * tokens
    starts, run = [], jnp.int32(0)
    for i in range(len_ref.shape[0]):
        starts.append(run)
        run = run + len_ref[i]

    def doc_at(position):
        found = jnp.int32(0)
        for start in starts:
            found = found + (position >= start).astype(jnp.int32)
        return found - 1

    position = base + lax.broadcasted_iota(jnp.int32, (8, tokens), 1)
    doc = jnp.zeros((8, tokens), jnp.int32) - 1
    for start in starts:
        doc = doc + (position >= start).astype(jnp.int32)
    docs_ref[...] = doc.astype(F32)
    edges = [doc_at(base - 1)] + [doc_at(base + (c + 1) * BLK - 1) for c in range(chunks)]

    first = lax.broadcasted_iota(jnp.int32, (BLK, BLK), 0)
    second = lax.broadcasted_iota(jnp.int32, (BLK, BLK), 1)
    upto = jnp.where(first <= second, 1.0, 0.0).astype(BF16)
    stack[...] = jnp.zeros_like(stack)
    for c in range(chunks):
        stack[c * hp : c * hp + heads, :] = decay_ref[:, c * BLK : (c + 1) * BLK]
    left, terms = stack[...], []
    for _ in range(3):
        terms.append(left.astype(BF16))
        left = left - terms[-1].astype(F32)
    high, middle, low = (jnp.dot(term, upto, preferred_element_type=F32) for term in terms)
    stack[...] = high + (middle + low)
    scr[...] = jnp.zeros_like(scr)
    cums = [stack[c * hp : c * hp + heads, :] for c in range(chunks)]
    sums = [jnp.broadcast_to(cum[:, BLK - 1 :], cum.shape) for cum in cums]
    before, after = [], [None] * chunks
    run = jnp.zeros_like(sums[0])
    for c in range(chunks):
        before.append(run)
        run = run + sums[c]
    run = jnp.zeros_like(sums[0])
    for c in reversed(range(chunks)):
        after[c] = run
        run = run + sums[c]
    for c in range(chunks):
        span = slice(c * BLK, (c + 1) * BLK)
        doc_c = doc[:1, span]
        cum, total = cums[c], sums[c]
        rows_ref[0:heads, span] = cum
        rows_ref[hp : hp + heads, span] = jnp.where(doc_c == edges[c + 1], jnp.exp(total - cum), 0.0)
        tail_ref[0:heads, span] = jnp.where(doc_c == edges[-1], jnp.exp(total - cum + after[c]), 0.0)
        rows_ref[2 * hp : 2 * hp + heads, span] = jnp.where(
            edges[c + 1] == edges[c], jnp.exp(total), 0.0
        )
        scr[0:heads, span] = cum
        scr[hp : hp + heads, span] = jnp.where(doc_c == edges[c], jnp.exp(cum), 0.0)
        scr[2 * hp + 8 : 2 * hp + 8 + heads, span] = jnp.where(
            doc_c == edges[0], jnp.exp(before[c] + cum), 0.0
        )
    scr[2 * hp : 2 * hp + 8, :] = doc.astype(F32)
    cols_ref[...] = scr[...].T
    total_ref[...] = jnp.where(edges[-1] == edges[0], jnp.exp(run[:, :128]), 0.0)


def prelude_kernel(tab, tile, len_ref, shard_ref, decay_ref, key_hbm, value_hbm, *refs):
    rows_ref, cols_ref, docs_ref, total_ref, table_ref, low_ref, full_ref = refs[:7]
    tail_ref, scr, stack, key_ref, value_ref, arrived = refs[7:]
    tokens = key_ref.shape[0]
    heads = full_ref.shape[0]
    copies = []
    for i in range(tokens // tile):
        span = pl.ds(i * tile, tile)
        for k, (source, target) in enumerate(((key_hbm, key_ref), (value_hbm, value_ref))):
            copies.append(pltpu.make_async_copy(source.at[span], target.at[span], arrived.at[k, i]))
            copies[-1].start()
    fill_table(tab, shard_ref, table_ref)
    fill_gates(len_ref, decay_ref, rows_ref, cols_ref, docs_ref, total_ref, tail_ref, scr, stack)
    for i in range(tokens // tile):
        copies[2 * i].wait()
        copies[2 * i + 1].wait()
        span = slice(i * tile, (i + 1) * tile)
        for h in range(heads):
            cols = slice(h * 128, (h + 1) * 128)
            scaled = (key_ref[span, cols].T.astype(F32) * tail_ref[h : h + 1, span]).astype(BF16)
            part = jnp.dot(scaled, value_ref[span, cols], preferred_element_type=F32)
            full_ref[h] = full_ref[h] + part if i else part
    low_ref[...] = full_ref[...].astype(BF16)


def prelude(tab, doc_lengths, block_shard, decay, key, value):
    heads, tokens = decay.shape
    hp = pad8(heads)
    tile = BLK
    smem = pl.BlockSpec(memory_space=pltpu.SMEM)
    vmem = pl.BlockSpec(memory_space=pltpu.VMEM)
    hbm = pl.BlockSpec(memory_space=pl.ANY)
    shapes = [(3 * hp, tokens), (tokens, 128), (8, tokens), (heads, 128)]
    return pl.pallas_call(
        functools.partial(prelude_kernel, tab, tile),
        in_specs=[smem, smem, vmem, hbm, hbm],
        out_specs=[vmem] * 4 + [smem] + [vmem] * 2,
        out_shape=[jax.ShapeDtypeStruct(shape, F32) for shape in shapes]
        + [jax.ShapeDtypeStruct((tab.size,), jnp.int32)]
        + [jax.ShapeDtypeStruct((heads, 128, 128), kind) for kind in (BF16, F32)],
        scratch_shapes=[
            pltpu.VMEM((hp, tokens), F32),
            pltpu.VMEM((128, tokens), F32),
            pltpu.VMEM((tokens // BLK * hp, BLK), F32),
            pltpu.VMEM(key.shape, BF16),
            pltpu.VMEM(value.shape, BF16),
            pltpu.SemaphoreType.DMA((2, tokens // tile)),
        ],
        compiler_params=params(32 * 2**20),
        name="prelude",
    )(*map(in_hbm, (doc_lengths, block_shard, decay, key, value)))


def barred_pairs(hp, cols_ref, docs_ref):
    first = lax.broadcasted_iota(jnp.int32, (BLK, BLK), 0)
    second = lax.broadcasted_iota(jnp.int32, (BLK, BLK), 1)
    same = cols_ref[:, 2 * hp : 2 * hp + 1] == docs_ref[0:1, :]
    return jnp.where((first >= second) & same, 0.0, -1e30).astype(F32)


def chunk_of_head(h, head, hp, barred, query_ref, key_ref, value_ref, rows_ref, cols_ref, state):
    cols = slice(h * 128, (h + 1) * 128)
    query, value = query_ref[:, cols], value_ref[:, cols]
    key_t = key_ref[:, cols].T
    scores = jnp.dot(query, key_t, preferred_element_type=F32)
    gap = cols_ref[:, head : head + 1] - rows_ref[head : head + 1, :] + barred
    weights = (scores * jnp.exp(gap)).astype(BF16)
    intra = jnp.dot(weights, value, preferred_element_type=F32)
    reached = jnp.dot(query, state[h].astype(BF16), preferred_element_type=F32)
    scaled = (key_t.astype(F32) * rows_ref[hp + head : hp + head + 1, :]).astype(BF16)
    carry = rows_ref[2 * hp + head : 2 * hp + head + 1, :128]
    state[h] = carry * state[h] + jnp.dot(scaled, value, preferred_element_type=F32)
    return intra + cols_ref[:, hp + head : hp + head + 1] * reached


def gate_head(h, attended, square, gain_ref, gate_ref, gated):
    cols = slice(h * 128, (h + 1) * 128)
    attended = attended.astype(BF16).astype(F32)
    gated[:BLK, cols] = (
        attended * gain_ref[0:1, cols] * jax.nn.sigmoid(gate_ref[:, cols].astype(F32))
    ).astype(BF16)
    return square + attended * attended


def own_kernel(lo, hp, count, *refs):
    (_, query_ref, key_ref, value_ref, gate_ref, gain_ref, rows_ref, cols_ref, docs_ref) = refs[:9]
    own_ref, same_ref, factor_ref, state = refs[9:]

    @pl.when(pl.program_id(0) == 0)
    def _():
        state[...] = jnp.zeros_like(state)

    barred = barred_pairs(hp, cols_ref, docs_ref)
    for h in range(count):
        own_ref[:, h * 128 : (h + 1) * 128] = chunk_of_head(
            h, lo + h, hp, barred, query_ref, key_ref, value_ref, rows_ref, cols_ref, state
        )
    same_ref[...] = query_ref[...]
    factor_ref[...] = gain_ref[0:1, :] * jax.nn.sigmoid(gate_ref[...].astype(F32))


def attend_own(tab, table, query, key, value, gate, gain, rows, cols, docs, lo, count):
    tokens, local_width = query.shape
    hp = rows.shape[0] // 3
    width = count * 128
    at = lo * 128 // width
    wide = pl.BlockSpec((BLK, width), lambda c, tbl: (c, at))
    narrow = pl.BlockSpec((BLK, width), lambda c, tbl: (c, 0))
    return pl.pallas_call(
        functools.partial(own_kernel, lo, hp, count),
        grid_spec=pltpu.PrefetchScalarGridSpec(
            num_scalar_prefetch=1,
            grid=(tokens // BLK,),
            in_specs=[
                wide,
                wide,
                wide,
                wide,
                pl.BlockSpec((1, width), lambda c, tbl: (0, tbl[tab.half] * (local_width // width) + at)),
                pl.BlockSpec((rows.shape[0], BLK), lambda c, tbl: (0, c)),
                pl.BlockSpec((BLK, 128), lambda c, tbl: (c, 0)),
                pl.BlockSpec((8, BLK), lambda c, tbl: (0, c)),
            ],
            out_specs=[narrow] * 3,
            scratch_shapes=[pltpu.VMEM((count, 128, 128), F32)],
        ),
        out_shape=[jax.ShapeDtypeStruct((tokens, width), kind) for kind in (F32, BF16, F32)],
        compiler_params=params(24 * 2**20),
        cost_estimate=pl.CostEstimate(
            flops=8 * tokens * width * BLK, bytes_accessed=10 * tokens * width, transcendentals=0
        ),
        name="attend_own",
    )(table, *map(in_hbm, (query, key, value, gate)), gain, rows, cols, docs)


def enter_kernel(tab, lo, hp, count, table_ref, own_ref, query_ref, factor_ref, cols_ref, state_ref, out_ref, square_ref):
    for c in range(tab.chunks):
        span = slice(c * BLK, (c + 1) * BLK)
        place, slot = table_ref[tab.shard + c], table_ref[tab.slot + c]
        square = jnp.zeros((BLK, 128), F32)
        for h in range(count):
            cols = slice(h * 128, (h + 1) * 128)
            reached = jnp.dot(query_ref[span, cols], state_ref[h], preferred_element_type=F32)
            column = 2 * hp + 8 + lo + h
            attended = own_ref[span, cols] + cols_ref[span, column : column + 1] * reached
            attended = attended.astype(BF16).astype(F32)
            out_ref[place, :, cols] = (attended * factor_ref[span, cols]).astype(BF16)
            square = square + attended * attended
        square_ref[slot] = jnp.sum(square.T, axis=0, keepdims=True)


def attend_entered(tab, table, own, cols, entering, lo, count, hp):
    width = count * 128
    vmem = pl.BlockSpec(memory_space=pltpu.VMEM)
    return pl.pallas_call(
        functools.partial(enter_kernel, tab, lo, hp, count),
        in_specs=[pl.BlockSpec(memory_space=pltpu.SMEM)] + [vmem] * 5,
        out_specs=[vmem] * 2,
        out_shape=[
            jax.ShapeDtypeStruct((tab.chunks, BLK, width), BF16),
            jax.ShapeDtypeStruct((tab.chunks, 1, BLK), F32),
        ],
        compiler_params=params(24 * 2**20),
        cost_estimate=pl.CostEstimate(flops=width, bytes_accessed=width, transcendentals=0),
        name="attend_entered",
    )(table, *own, cols, entering)


def attend_kernel(tab, lo, hp, count, last, *refs):
    ops = tab.n
    (table_ref, query_ref, key_ref, value_ref, gate_ref, gain_ref, rows_ref, cols_ref, docs_ref, state_ref, squares_ref) = refs[:11]
    outs = refs[11 : 11 + ops]
    state, gated = refs[-2:]
    step = pl.program_id(0)

    @pl.when(step == 0)
    def _():
        state[...] = state_ref[...].astype(F32)

    barred = barred_pairs(hp, cols_ref, docs_ref)
    square = jnp.zeros((BLK, 128), F32)
    for h in range(count):
        attended = chunk_of_head(
            h, lo + h, hp, barred, query_ref, key_ref, value_ref, rows_ref, cols_ref, state
        )
        square = gate_head(h, attended, square, gain_ref, gate_ref, gated)
    total = jnp.sum(square.T, axis=0, keepdims=True) + squares_ref[0]
    if last:
        lanes, lines = extra_rows(gated.shape[1])
        row = lax.broadcasted_iota(jnp.int32, (16, lanes), 0)
        extra, left = jnp.zeros((16, lanes), F32), total
        for term in range(3):
            part = left.astype(BF16).astype(F32)
            left = left - part
            for line in range(lines):
                piece = part[:, line * lanes : (line + 1) * lanes]
                extra = jnp.where(row == term * lines + line, piece, extra)
    else:
        refs[11 + ops][0] = total
    which = table_ref[tab.which + step]
    for op in range(ops):

        @pl.when(which == op)
        def _():
            outs[op][...] = gated[...]
            if last:
                refs[11 + ops + op][...] = extra.astype(BF16)


def stitch_kernel(count, *refs):
    extras, outs, arrived = refs[:count], refs[2 * count : 3 * count], refs[-1]
    copies = []
    for k in range(count):
        target = outs[k].at[pl.ds(outs[k].shape[0] - 16, 16)]
        copies.append(pltpu.make_async_copy(extras[k], target, arrived.at[k]))
        copies[-1].start()
    for copy in copies:
        copy.wait()


def stitch(pieces, extras):
    count = len(pieces)
    hbm = pl.BlockSpec(memory_space=pl.ANY)
    return pl.pallas_call(
        functools.partial(stitch_kernel, count),
        in_specs=[hbm] * (2 * count),
        out_specs=[hbm] * count,
        out_shape=[jax.ShapeDtypeStruct(piece.shape, BF16) for piece in pieces],
        scratch_shapes=[pltpu.SemaphoreType.DMA((count,))],
        input_output_aliases={count + k: k for k in range(count)},
        compiler_params=params(63 * 2**20),
        cost_estimate=pl.CostEstimate(flops=128, bytes_accessed=128, transcendentals=0),
        name="stitch",
    )(*extras, *pieces)


def attend(tab, table, query, key, value, gate, gain, rows, cols, docs, entering, base, lo, count, squares, last):
    tokens, local_width = query.shape
    chunks, per = tab.chunks, tab.per
    ops = tab.n
    hp = rows.shape[0] // 3
    width = count * 128
    at = lo * 128 // width
    lanes, _ = extra_rows(width)
    wide = pl.BlockSpec((BLK, width), lambda c, tbl: (c, at))
    square_spec = pl.BlockSpec((1, 1, BLK), lambda c, tbl: (tbl[tab.slot + c], 0, 0))

    def out_map(op, c, tbl):
        return (tbl[tab.place + op * chunks + c], 0)

    def extra_map(op, c, tbl):
        return (0, tbl[tab.place + op * chunks + c])

    if last:
        square_specs = [pl.BlockSpec((16, lanes), functools.partial(extra_map, op)) for op in range(ops)]
        square_shapes = [jax.ShapeDtypeStruct((16, width), BF16)] * ops
    else:
        square_specs, square_shapes = [square_spec], [jax.ShapeDtypeStruct((chunks, 1, BLK), F32)]
    out = pl.pallas_call(
        functools.partial(attend_kernel, tab, lo, hp, count, last),
        grid_spec=pltpu.PrefetchScalarGridSpec(
            num_scalar_prefetch=1,
            grid=(chunks,),
            in_specs=[
                wide,
                wide,
                wide,
                wide,
                pl.BlockSpec((1, width), lambda c, tbl: (0, tbl[tab.half] * (local_width // width) + at)),
                pl.BlockSpec((rows.shape[0], BLK), lambda c, tbl: (0, c)),
                pl.BlockSpec((BLK, 128), lambda c, tbl: (c, 0)),
                pl.BlockSpec((8, BLK), lambda c, tbl: (0, c)),
                pl.BlockSpec((count, 128, 128), lambda c, tbl: ((lo - base) // count, 0, 0)),
            ]
            + [square_spec],
            out_specs=[
                pl.BlockSpec((BLK, width), functools.partial(out_map, op)) for op in range(ops)
            ]
            + square_specs,
            scratch_shapes=[
                pltpu.VMEM((count, 128, 128), F32),
                pltpu.VMEM((BLK, width), BF16),
            ],
        ),
        out_shape=[jax.ShapeDtypeStruct((per * BLK + 16 * last, width), BF16)] * ops + square_shapes,
        compiler_params=params(),
        cost_estimate=pl.CostEstimate(flops=16 * tokens * width * BLK, bytes_accessed=10 * tokens * width, transcendentals=tokens * width),
        name="attend",
    )(table, query, key, value, gate, gain, rows, cols, docs, entering, squares)
    if last:
        return stitch(out[:ops], out[ops:]), None
    return out[:ops], out[ops]


def row_scale(extras, features, lanes, lines):
    square = []
    for line in range(lines):
        at = [term * lines + line for term in range(3)]
        parts = [extra[row : row + 1, :] for extra in extras for row in at]
        square.append(sum(part.astype(F32) for part in parts))
    scale = [lax.rsqrt(row / features + norm_eps) for row in square]
    return jnp.concatenate([jnp.broadcast_to(row, (128, lanes)).T for row in scale], axis=0)


def place_kernel(features, t, count, lanes, lines, table_ref, *refs):
    out_ref = refs[-1]
    scale = row_scale(refs[:t], features, lanes, lines)
    done = 0
    for piece_ref in refs[t : t + count]:
        for c in range(piece_ref.shape[1] // 128):
            piece = piece_ref[:, c * 128 : (c + 1) * 128].astype(F32)
            out_ref[:, done : done + 128] = (piece * scale).astype(BF16)
            done += 128


def place(tab, table, op, lo, pieces, extras, out, shape, local_width, features):
    rows = tab.per * BLK

    def piece_map(all_blocks, c, tbl):
        block = tbl[tab.side + op] * tab.stride * tab.per + tbl[tab.row + op] if all_blocks else 0
        return (block + c, 0)

    lanes, lines = extra_rows(extras[0].shape[1])
    unit = sum(piece.shape[1] for piece in pieces)

    def out_map(c, tbl):
        return (tbl[tab.row + op] + c, tbl[tab.side + op] * (local_width // unit) + lo * 128 // unit)

    in_specs = [pl.BlockSpec((16, lanes), lambda c, tbl: (rows // 16, c))] * tab.t
    in_specs += [
        pl.BlockSpec((BLK, piece.shape[1]), functools.partial(piece_map, piece.shape[0] == tab.chunks * BLK))
        for piece in pieces
    ]
    operands = [table, *extras, *pieces]
    aliases = {}
    if out is not None:
        in_specs.append(pl.BlockSpec(memory_space=pl.ANY))
        operands.append(out)
        aliases = {len(operands) - 1: 0}
    return pl.pallas_call(
        functools.partial(place_kernel, features, tab.t, len(pieces), lanes, lines),
        grid_spec=pltpu.PrefetchScalarGridSpec(
            num_scalar_prefetch=1,
            grid=(tab.per,),
            in_specs=in_specs,
            out_specs=pl.BlockSpec((BLK, unit), out_map),
        ),
        out_shape=jax.ShapeDtypeStruct(shape, BF16),
        input_output_aliases=aliases,
        compiler_params=params(63 * 2**20),
        cost_estimate=pl.CostEstimate(flops=unit, bytes_accessed=unit, transcendentals=0),
        name="place",
    )(*operands)


def place_last_kernel(tab, features, ops, lo, local_width, lanes, lines, table_ref, *refs):
    t, per, count = tab.t, tab.per, len(ops)
    extras, pieces = refs[: count * t], refs[count * t : count * (t + 1)]
    out_ref, extra, block, extra_in, block_in, block_out = refs[-6:]
    unit, rows = block.shape[2], per * BLK
    part = BLK // 2
    moves, fetched, stores = [], [], []
    for j in range(count):
        for c in range(per):
            b = j * per + c
            for k in range(t):
                source = extras[j * t + k].at[pl.ds(rows, 16), pl.ds(c * lanes, lanes)]
                moves.append(pltpu.make_async_copy(source, extra.at[b, k], extra_in.at[b, k]))
                moves[-1].start()
            for half in range(2):
                source = pieces[j].at[pl.ds(c * BLK + half * part, part)]
                target = block.at[b, pl.ds(half * part, part)]
                fetched.append(pltpu.make_async_copy(source, target, block_in.at[b, half]))
                fetched[-1].start()
    for j, op in enumerate(ops):
        row = table_ref[tab.row + op] * BLK
        left = pl.multiple_of(table_ref[tab.side + op] * local_width + lo * 128, 128)
        for c in range(per):
            b = j * per + c
            for k in range(t):
                moves[b * t + k].wait()
            scale = row_scale([extra.at[b, k] for k in range(t)], features, lanes, lines)
            for half in range(2):
                fetched[2 * b + half].wait()
                span = slice(half * part, (half + 1) * part)
                for col in range(0, unit, 128):
                    cols = slice(col, col + 128)
                    block[b, span, cols] = (block[b, span, cols].astype(F32) * scale[span]).astype(BF16)
                top = pl.multiple_of(row + c * BLK + half * part, part)
                target = out_ref.at[pl.ds(top, part), pl.ds(left, unit)]
                source = block.at[b, pl.ds(half * part, part)]
                stores.append(pltpu.make_async_copy(source, target, block_out.at[b, half]))
                stores[-1].start()
    for store in stores:
        store.wait()


def place_last(tab, table, ops, lo, pieces, extras, out, local_width, features):
    lanes, lines = extra_rows(extras[0].shape[1])
    blocks = len(ops) * tab.per
    hbm = pl.BlockSpec(memory_space=pl.ANY)
    operands = [table, *extras, *pieces, out]
    return pl.pallas_call(
        functools.partial(place_last_kernel, tab, features, ops, lo, local_width, lanes, lines),
        in_specs=[pl.BlockSpec(memory_space=pltpu.SMEM)] + [hbm] * (len(operands) - 1),
        out_specs=hbm,
        out_shape=jax.ShapeDtypeStruct(out.shape, BF16),
        scratch_shapes=[
            pltpu.VMEM((blocks, tab.t, 16, lanes), BF16),
            pltpu.VMEM((blocks, BLK, pieces[0].shape[1]), BF16),
            pltpu.SemaphoreType.DMA((blocks, tab.t)),
            pltpu.SemaphoreType.DMA((blocks, 2)),
            pltpu.SemaphoreType.DMA((blocks, 2)),
        ],
        input_output_aliases={len(operands) - 1: 0},
        compiler_params=params(63 * 2**20),
        cost_estimate=pl.CostEstimate(flops=lanes, bytes_accessed=lanes, transcendentals=0),
        name="place_last",
    )(*operands)


def local(query_rows, key_rows, value_rows, gate_rows, decay_log, norm_gain, doc_lengths, block_shard):
    tokens, width = query_rows.shape
    heads = decay_log.shape[0]
    features = norm_gain.shape[0]
    n, t = lax.axis_size("ctx"), lax.axis_size("tp")
    tab = Table(n, t, tokens // BLK)
    quarter = max(1, heads // 4)

    rest = heads - quarter
    rows, cols, docs, total_gate, table, low, full = prelude(
        tab, doc_lengths, block_shard, decay_log, key_rows, value_rows
    )
    gain = norm_gain.reshape(1, features)
    hop = [(i, i + 1) for i in range(n - 1)]

    def route(op):
        return [
            (d * t + k, (d + op + k * tab.stride) % n * t + d // tab.stride)
            for d in range(n)
            for k in range(t)
        ]

    carry = total_gate[:, :1, None]

    def merge(arrived, part):
        return (carry[part] * arrived[part].astype(F32) + full[part]).astype(BF16)

    first, others = slice(rest, heads), slice(0, rest)
    for _ in range(max(1, n // 2) - 2):
        low = merge(lax.ppermute(low, "ctx", hop), slice(0, heads))
    parts = [low[first], low[others]]
    if n // 2 > 1:
        arrived = lax.ppermute(low, "ctx", hop)
        parts = [merge(arrived, first), merge(arrived, others)]
    own = attend_own(
        tab, table, query_rows, key_rows, value_rows, gate_rows, gain, rows, cols, docs, rest, quarter
    )
    parts, own = lax.optimization_barrier((parts, own))
    early, entering = (lax.ppermute(part, "ctx", hop) for part in parts)
    ready, squares = attend_entered(tab, table, own, cols, early, rest, quarter, rows.shape[0] // 3)
    gated = [None]
    for lo, count in ((0, 2 * quarter), (2 * quarter, quarter)):
        outs, squares = attend(
            tab, table, query_rows, key_rows, value_rows, gate_rows, gain, rows, cols, docs,
            entering, 0, lo, count, squares, lo > 0,
        )
        gated.append(outs)
    head = lax.all_to_all(ready, "ctx", split_axis=0, concat_axis=0, tiled=True)
    head = lax.all_to_all(head, "tp", split_axis=0, concat_axis=0, tiled=True).reshape(tokens, -1)
    tail = [lax.ppermute(gated[2][op], ("ctx", "tp"), route(op)) for op in range(n)]
    middle = []
    for op in range(n):
        ready = gated[1][op]
        for before in ([], [0, n - 1])[op] if op < 2 else [op - 1]:
            ready, tail[before] = lax.optimization_barrier((ready, tail[before]))
        middle.append(lax.ppermute(ready, ("ctx", "tp"), route(op)))

    shape = (tokens // t, features)
    out = None

    def extras(op):
        return [tail[(op + k * tab.stride) % n] for k in range(t)]

    for op in range(n):
        out = place(tab, table, op, 2 * quarter, [tail[op], head], extras(op), out, shape, width, features)
    for op in range(n - 2):
        out = place(tab, table, op, 0, [middle[op]], extras(op), out, shape, width, features)
    last = (n - 2, n - 1)
    return place_last(
        tab, table, last, 0, middle[n - 2 :], [extra for op in last for extra in extras(op)], out, width, features
    )


def solution(mesh):
    return jax.shard_map(
        local,
        mesh=mesh,
        in_specs=(
            P(("dp", "ctx"), "tp"),
            P(("dp", "ctx"), "tp"),
            P(("dp", "ctx"), "tp"),
            P(("dp", "ctx"), "tp"),
            P("tp", ("dp", "ctx")),
            P(),
            P("dp"),
            P("dp"),
        ),
        out_specs=P(("dp", "ctx", "tp"), None),
        check_vma=False,
    )
```

```python
import functools

import jax
import jax.numpy as jnp
from jax import lax
from jax.experimental import pallas as pl
from jax.experimental.pallas import tpu as pltpu
from jax.sharding import PartitionSpec as P

BLK = 256
norm_eps = 1e-05
VMEM_LIMIT = 56 * 2**20
F32 = jnp.float32
BF16 = jnp.bfloat16


def params(limit=VMEM_LIMIT):
    return pltpu.CompilerParams(vmem_limit_bytes=limit)


def in_hbm(array):
    return pltpu.with_memory_space_constraint(array, pltpu.HBM)


def whole(shape):
    return pl.BlockSpec(shape, lambda *_: (0,) * len(shape))


def extra_rows(width):
    lanes = min(width, BLK)
    return lanes, BLK // lanes


def pad8(count):
    return -(-count // 8) * 8


class Table:
    def __init__(self, n, t, chunks):
        self.n, self.t, self.chunks = n, t, chunks
        self.stride, self.per = n // t, chunks // n
        self.half = 0
        self.which = 1
        self.slot = self.which + chunks
        self.place = self.slot + chunks
        self.row = self.place + n * chunks
        self.side = self.row + n
        self.shard = self.side + n
        self.size = self.shard + chunks


def fill_table(tab, shard_ref, table_ref):
    n, per, chunks = tab.n, tab.per, tab.chunks
    ctx, tp = lax.axis_index("ctx"), lax.axis_index("tp")
    table_ref[tab.half] = tp
    seen = [jnp.int32(0)] * n
    for c in range(chunks):
        shard = shard_ref[ctx * chunks + c]
        op = lax.rem(shard - ctx - tp * tab.stride + 2 * n, n)
        table_ref[tab.which + c] = op
        rank = jnp.int32(0)
        for k in range(n):
            table_ref[tab.place + k * chunks + c] = jnp.minimum(seen[k], per - 1)
            here = (op == k).astype(jnp.int32)
            rank = rank + here * seen[k]
            seen[k] = seen[k] + here
        table_ref[tab.slot + c] = op * per + jnp.minimum(rank, per - 1)
        table_ref[tab.shard + c] = shard * per + jnp.minimum(rank, per - 1)
    for op in range(n):
        lane = lax.rem(ctx - op + n, tab.stride)
        source = tp * tab.stride + lane
        table_ref[tab.row + op] = lane * per
        table_ref[tab.side + op] = lax.rem(ctx - op - source + 2 * n, n) // tab.stride


def fill_gates(len_ref, decay_ref, rows_ref, cols_ref, docs_ref, total_ref, tail_ref, scr, stack):
    heads, tokens = decay_ref.shape
    hp = pad8(heads)
    chunks = tokens // BLK
    base = lax.axis_index("ctx") * tokens
    starts, run = [], jnp.int32(0)
    for i in range(len_ref.shape[0]):
        starts.append(run)
        run = run + len_ref[i]

    def doc_at(position):
        found = jnp.int32(0)
        for start in starts:
            found = found + (position >= start).astype(jnp.int32)
        return found - 1

    position = base + lax.broadcasted_iota(jnp.int32, (8, tokens), 1)
    doc = jnp.zeros((8, tokens), jnp.int32) - 1
    for start in starts:
        doc = doc + (position >= start).astype(jnp.int32)
    docs_ref[...] = doc.astype(F32)
    edges = [doc_at(base - 1)] + [doc_at(base + (c + 1) * BLK - 1) for c in range(chunks)]

    first = lax.broadcasted_iota(jnp.int32, (BLK, BLK), 0)
    second = lax.broadcasted_iota(jnp.int32, (BLK, BLK), 1)
    upto = jnp.where(first <= second, 1.0, 0.0).astype(BF16)
    stack[...] = jnp.zeros_like(stack)
    for c in range(chunks):
        stack[c * hp : c * hp + heads, :] = decay_ref[:, c * BLK : (c + 1) * BLK]
    left, terms = stack[...], []
    for _ in range(3):
        terms.append(left.astype(BF16))
        left = left - terms[-1].astype(F32)
    high, middle, low = (jnp.dot(term, upto, preferred_element_type=F32) for term in terms)
    stack[...] = high + (middle + low)
    scr[...] = jnp.zeros_like(scr)
    cums = [stack[c * hp : c * hp + heads, :] for c in range(chunks)]
    sums = [jnp.broadcast_to(cum[:, BLK - 1 :], cum.shape) for cum in cums]
    before, after = [], [None] * chunks
    run = jnp.zeros_like(sums[0])
    for c in range(chunks):
        before.append(run)
        run = run + sums[c]
    run = jnp.zeros_like(sums[0])
    for c in reversed(range(chunks)):
        after[c] = run
        run = run + sums[c]
    for c in range(chunks):
        span = slice(c * BLK, (c + 1) * BLK)
        doc_c = doc[:1, span]
        cum, total = cums[c], sums[c]
        rows_ref[0:heads, span] = cum
        rows_ref[hp : hp + heads, span] = jnp.where(doc_c == edges[c + 1], jnp.exp(total - cum), 0.0)
        tail_ref[0:heads, span] = jnp.where(doc_c == edges[-1], jnp.exp(total - cum + after[c]), 0.0)
        rows_ref[2 * hp : 2 * hp + heads, span] = jnp.where(
            edges[c + 1] == edges[c], jnp.exp(total), 0.0
        )
        scr[0:heads, span] = cum
        scr[hp : hp + heads, span] = jnp.where(doc_c == edges[c], jnp.exp(cum), 0.0)
        scr[2 * hp + 8 : 2 * hp + 8 + heads, span] = jnp.where(
            doc_c == edges[0], jnp.exp(before[c] + cum), 0.0
        )
    scr[2 * hp : 2 * hp + 8, :] = doc.astype(F32)
    cols_ref[...] = scr[...].T
    total_ref[...] = jnp.where(edges[-1] == edges[0], jnp.exp(run[:, :128]), 0.0)


def prelude_kernel(tab, tile, len_ref, shard_ref, decay_ref, key_hbm, value_hbm, *refs):
    rows_ref, cols_ref, docs_ref, total_ref, table_ref, low_ref, full_ref = refs[:7]
    tail_ref, scr, stack, key_ref, value_ref, arrived = refs[7:]
    tokens = key_ref.shape[0]
    heads = full_ref.shape[0]
    copies = []
    for i in range(tokens // tile):
        span = pl.ds(i * tile, tile)
        for k, (source, target) in enumerate(((key_hbm, key_ref), (value_hbm, value_ref))):
            copies.append(pltpu.make_async_copy(source.at[span], target.at[span], arrived.at[k, i]))
            copies[-1].start()
    fill_table(tab, shard_ref, table_ref)
    fill_gates(len_ref, decay_ref, rows_ref, cols_ref, docs_ref, total_ref, tail_ref, scr, stack)
    for i in range(tokens // tile):
        copies[2 * i].wait()
        copies[2 * i + 1].wait()
        span = slice(i * tile, (i + 1) * tile)
        for h in range(heads):
            cols = slice(h * 128, (h + 1) * 128)
            scaled = (key_ref[span, cols].T.astype(F32) * tail_ref[h : h + 1, span]).astype(BF16)
            part = jnp.dot(scaled, value_ref[span, cols], preferred_element_type=F32)
            full_ref[h] = full_ref[h] + part if i else part
    low_ref[...] = full_ref[...].astype(BF16)


def prelude(tab, doc_lengths, block_shard, decay, key, value):
    heads, tokens = decay.shape
    hp = pad8(heads)
    tile = BLK
    smem = pl.BlockSpec(memory_space=pltpu.SMEM)
    vmem = pl.BlockSpec(memory_space=pltpu.VMEM)
    hbm = pl.BlockSpec(memory_space=pl.ANY)
    shapes = [(3 * hp, tokens), (tokens, 128), (8, tokens), (heads, 128)]
    return pl.pallas_call(
        functools.partial(prelude_kernel, tab, tile),
        in_specs=[smem, smem, vmem, hbm, hbm],
        out_specs=[vmem] * 4 + [smem] + [vmem] * 2,
        out_shape=[jax.ShapeDtypeStruct(shape, F32) for shape in shapes]
        + [jax.ShapeDtypeStruct((tab.size,), jnp.int32)]
        + [jax.ShapeDtypeStruct((heads, 128, 128), kind) for kind in (BF16, F32)],
        scratch_shapes=[
            pltpu.VMEM((hp, tokens), F32),
            pltpu.VMEM((128, tokens), F32),
            pltpu.VMEM((tokens // BLK * hp, BLK), F32),
            pltpu.VMEM(key.shape, BF16),
            pltpu.VMEM(value.shape, BF16),
            pltpu.SemaphoreType.DMA((2, tokens // tile)),
        ],
        compiler_params=params(32 * 2**20),
        name="prelude",
    )(*map(in_hbm, (doc_lengths, block_shard, decay, key, value)))


def barred_pairs(hp, cols_ref, docs_ref):
    first = lax.broadcasted_iota(jnp.int32, (BLK, BLK), 0)
    second = lax.broadcasted_iota(jnp.int32, (BLK, BLK), 1)
    same = cols_ref[:, 2 * hp : 2 * hp + 1] == docs_ref[0:1, :]
    return jnp.where((first >= second) & same, 0.0, -1e30).astype(F32)


def chunk_of_head(h, head, hp, barred, query_ref, key_ref, value_ref, rows_ref, cols_ref, state):
    cols = slice(h * 128, (h + 1) * 128)
    query, value = query_ref[:, cols], value_ref[:, cols]
    key_t = key_ref[:, cols].T
    scores = jnp.dot(query, key_t, preferred_element_type=F32)
    gap = cols_ref[:, head : head + 1] - rows_ref[head : head + 1, :] + barred
    weights = (scores * jnp.exp(gap)).astype(BF16)
    intra = jnp.dot(weights, value, preferred_element_type=F32)
    reached = jnp.dot(query, state[h].astype(BF16), preferred_element_type=F32)
    scaled = (key_t.astype(F32) * rows_ref[hp + head : hp + head + 1, :]).astype(BF16)
    carry = rows_ref[2 * hp + head : 2 * hp + head + 1, :128]
    state[h] = carry * state[h] + jnp.dot(scaled, value, preferred_element_type=F32)
    return intra + cols_ref[:, hp + head : hp + head + 1] * reached


def gate_head(h, attended, square, gain_ref, gate_ref, gated):
    cols = slice(h * 128, (h + 1) * 128)
    attended = attended.astype(BF16).astype(F32)
    gated[:BLK, cols] = (
        attended * gain_ref[0:1, cols] * jax.nn.sigmoid(gate_ref[:, cols].astype(F32))
    ).astype(BF16)
    return square + attended * attended


def own_kernel(lo, hp, count, *refs):
    (_, query_ref, key_ref, value_ref, gate_ref, gain_ref, rows_ref, cols_ref, docs_ref) = refs[:9]
    own_ref, same_ref, factor_ref, state = refs[9:]

    @pl.when(pl.program_id(0) == 0)
    def _():
        state[...] = jnp.zeros_like(state)

    barred = barred_pairs(hp, cols_ref, docs_ref)
    for h in range(count):
        own_ref[:, h * 128 : (h + 1) * 128] = chunk_of_head(
            h, lo + h, hp, barred, query_ref, key_ref, value_ref, rows_ref, cols_ref, state
        )
    same_ref[...] = query_ref[...]
    factor_ref[...] = gain_ref[0:1, :] * jax.nn.sigmoid(gate_ref[...].astype(F32))


def attend_own(tab, table, query, key, value, gate, gain, rows, cols, docs, lo, count):
    tokens, local_width = query.shape
    hp = rows.shape[0] // 3
    width = count * 128
    at = lo * 128 // width
    wide = pl.BlockSpec((BLK, width), lambda c, tbl: (c, at))
    narrow = pl.BlockSpec((BLK, width), lambda c, tbl: (c, 0))
    return pl.pallas_call(
        functools.partial(own_kernel, lo, hp, count),
        grid_spec=pltpu.PrefetchScalarGridSpec(
            num_scalar_prefetch=1,
            grid=(tokens // BLK,),
            in_specs=[
                wide,
                wide,
                wide,
                wide,
                pl.BlockSpec((1, width), lambda c, tbl: (0, tbl[tab.half] * (local_width // width) + at)),
                pl.BlockSpec((rows.shape[0], BLK), lambda c, tbl: (0, c)),
                pl.BlockSpec((BLK, 128), lambda c, tbl: (c, 0)),
                pl.BlockSpec((8, BLK), lambda c, tbl: (0, c)),
            ],
            out_specs=[narrow] * 3,
            scratch_shapes=[pltpu.VMEM((count, 128, 128), F32)],
        ),
        out_shape=[jax.ShapeDtypeStruct((tokens, width), kind) for kind in (F32, BF16, F32)],
        compiler_params=params(24 * 2**20),
        cost_estimate=pl.CostEstimate(
            flops=8 * tokens * width * BLK, bytes_accessed=10 * tokens * width, transcendentals=0
        ),
        name="attend_own",
    )(table, *map(in_hbm, (query, key, value, gate)), gain, rows, cols, docs)


def enter_kernel(tab, lo, hp, count, table_ref, own_ref, query_ref, factor_ref, cols_ref, state_ref, out_ref, square_ref, gated, stored):
    stores = []
    for c in range(tab.chunks):
        span = slice(c * BLK, (c + 1) * BLK)
        place, slot = table_ref[tab.shard + c], table_ref[tab.slot + c]
        square = jnp.zeros((BLK, 128), F32)
        for h in range(count):
            cols = slice(h * 128, (h + 1) * 128)
            reached = jnp.dot(query_ref[span, cols], state_ref[h], preferred_element_type=F32)
            column = 2 * hp + 8 + lo + h
            attended = own_ref[span, cols] + cols_ref[span, column : column + 1] * reached
            attended = attended.astype(BF16).astype(F32)
            gated[span, cols] = (attended * factor_ref[span, cols]).astype(BF16)
            square = square + attended * attended
        square_ref[slot] = jnp.sum(square.T, axis=0, keepdims=True)
        stores.append(pltpu.make_async_copy(gated.at[pl.ds(c * BLK, BLK)], out_ref.at[place], stored.at[c]))
        stores[-1].start()
    for store in stores:
        store.wait()


def attend_entered(tab, table, own, cols, entering, lo, count, hp):
    width = count * 128
    vmem = pl.BlockSpec(memory_space=pltpu.VMEM)
    return pl.pallas_call(
        functools.partial(enter_kernel, tab, lo, hp, count),
        in_specs=[pl.BlockSpec(memory_space=pltpu.SMEM)] + [vmem] * 5,
        out_specs=[pl.BlockSpec(memory_space=pl.ANY), vmem],
        out_shape=[
            jax.ShapeDtypeStruct((tab.chunks, BLK, width), BF16),
            jax.ShapeDtypeStruct((tab.chunks, 1, BLK), F32),
        ],
        scratch_shapes=[
            pltpu.VMEM((tab.chunks * BLK, width), BF16),
            pltpu.SemaphoreType.DMA((tab.chunks,)),
        ],
        compiler_params=params(24 * 2**20),
        cost_estimate=pl.CostEstimate(flops=width, bytes_accessed=width, transcendentals=0),
        name="attend_entered",
    )(table, *own, cols, entering)


def attend_kernel(tab, lo, hp, count, last, *refs):
    ops = tab.n
    (table_ref, query_ref, key_ref, value_ref, gate_ref, gain_ref, rows_ref, cols_ref, docs_ref, state_ref, squares_ref) = refs[:11]
    outs = refs[11 : 11 + ops]
    state, gated = refs[-2:]
    step = pl.program_id(0)

    @pl.when(step == 0)
    def _():
        state[...] = state_ref[...].astype(F32)

    barred = barred_pairs(hp, cols_ref, docs_ref)
    square = jnp.zeros((BLK, 128), F32)
    for h in range(count):
        attended = chunk_of_head(
            h, lo + h, hp, barred, query_ref, key_ref, value_ref, rows_ref, cols_ref, state
        )
        square = gate_head(h, attended, square, gain_ref, gate_ref, gated)
    total = jnp.sum(square.T, axis=0, keepdims=True) + squares_ref[0]
    if last:
        lanes, lines = extra_rows(gated.shape[1])
        row = lax.broadcasted_iota(jnp.int32, (16, lanes), 0)
        extra, left = jnp.zeros((16, lanes), F32), total
        for term in range(3):
            part = left.astype(BF16).astype(F32)
            left = left - part
            for line in range(lines):
                piece = part[:, line * lanes : (line + 1) * lanes]
                extra = jnp.where(row == term * lines + line, piece, extra)
    else:
        refs[11 + ops][0] = total
    which = table_ref[tab.which + step]
    for op in range(ops):

        @pl.when(which == op)
        def _():
            outs[op][...] = gated[...]
            if last:
                refs[11 + ops + op][...] = extra.astype(BF16)


def stitch_kernel(count, *refs):
    extras, outs, arrived = refs[:count], refs[2 * count : 3 * count], refs[-1]
    copies = []
    for k in range(count):
        target = outs[k].at[pl.ds(outs[k].shape[0] - 16, 16)]
        copies.append(pltpu.make_async_copy(extras[k], target, arrived.at[k]))
        copies[-1].start()
    for copy in copies:
        copy.wait()


def stitch(pieces, extras):
    count = len(pieces)
    hbm = pl.BlockSpec(memory_space=pl.ANY)
    return pl.pallas_call(
        functools.partial(stitch_kernel, count),
        in_specs=[hbm] * (2 * count),
        out_specs=[hbm] * count,
        out_shape=[jax.ShapeDtypeStruct(piece.shape, BF16) for piece in pieces],
        scratch_shapes=[pltpu.SemaphoreType.DMA((count,))],
        input_output_aliases={count + k: k for k in range(count)},
        compiler_params=params(63 * 2**20),
        cost_estimate=pl.CostEstimate(flops=128, bytes_accessed=128, transcendentals=0),
        name="stitch",
    )(*extras, *pieces)


def attend(tab, table, query, key, value, gate, gain, rows, cols, docs, entering, base, lo, count, squares, last):
    tokens, local_width = query.shape
    chunks, per = tab.chunks, tab.per
    ops = tab.n
    hp = rows.shape[0] // 3
    width = count * 128
    at = lo * 128 // width
    lanes, _ = extra_rows(width)
    wide = pl.BlockSpec((BLK, width), lambda c, tbl: (c, at))
    square_spec = pl.BlockSpec((1, 1, BLK), lambda c, tbl: (tbl[tab.slot + c], 0, 0))

    def out_map(op, c, tbl):
        return (tbl[tab.place + op * chunks + c], 0)

    def extra_map(op, c, tbl):
        return (0, tbl[tab.place + op * chunks + c])

    if last:
        square_specs = [pl.BlockSpec((16, lanes), functools.partial(extra_map, op)) for op in range(ops)]
        square_shapes = [jax.ShapeDtypeStruct((16, width), BF16)] * ops
    else:
        square_specs, square_shapes = [square_spec], [jax.ShapeDtypeStruct((chunks, 1, BLK), F32)]
    out = pl.pallas_call(
        functools.partial(attend_kernel, tab, lo, hp, count, last),
        grid_spec=pltpu.PrefetchScalarGridSpec(
            num_scalar_prefetch=1,
            grid=(chunks,),
            in_specs=[
                wide,
                wide,
                wide,
                wide,
                pl.BlockSpec((1, width), lambda c, tbl: (0, tbl[tab.half] * (local_width // width) + at)),
                pl.BlockSpec((rows.shape[0], BLK), lambda c, tbl: (0, c)),
                pl.BlockSpec((BLK, 128), lambda c, tbl: (c, 0)),
                pl.BlockSpec((8, BLK), lambda c, tbl: (0, c)),
                pl.BlockSpec((count, 128, 128), lambda c, tbl: ((lo - base) // count, 0, 0)),
            ]
            + [square_spec],
            out_specs=[
                pl.BlockSpec((BLK, width), functools.partial(out_map, op)) for op in range(ops)
            ]
            + square_specs,
            scratch_shapes=[
                pltpu.VMEM((count, 128, 128), F32),
                pltpu.VMEM((BLK, width), BF16),
            ],
        ),
        out_shape=[jax.ShapeDtypeStruct((per * BLK + 16 * last, width), BF16)] * ops + square_shapes,
        compiler_params=params(),
        cost_estimate=pl.CostEstimate(flops=16 * tokens * width * BLK, bytes_accessed=10 * tokens * width, transcendentals=tokens * width),
        name="attend",
    )(table, query, key, value, gate, gain, rows, cols, docs, entering, squares)
    if last:
        return stitch(out[:ops], out[ops:]), None
    return out[:ops], out[ops]


def row_scale(extras, features, lanes, lines):
    square = []
    for line in range(lines):
        at = [term * lines + line for term in range(3)]
        parts = [extra[row : row + 1, :] for extra in extras for row in at]
        square.append(sum(part.astype(F32) for part in parts))
    scale = [lax.rsqrt(row / features + norm_eps) for row in square]
    return jnp.concatenate([jnp.broadcast_to(row, (128, lanes)).T for row in scale], axis=0)


def place_kernel(features, t, count, lanes, lines, table_ref, *refs):
    out_ref = refs[-1]
    scale = row_scale(refs[:t], features, lanes, lines)
    done = 0
    for piece_ref in refs[t : t + count]:
        for c in range(piece_ref.shape[1] // 128):
            piece = piece_ref[:, c * 128 : (c + 1) * 128].astype(F32)
            out_ref[:, done : done + 128] = (piece * scale).astype(BF16)
            done += 128


def place(tab, table, op, lo, pieces, extras, out, shape, local_width, features):
    rows = tab.per * BLK

    def piece_map(all_blocks, c, tbl):
        block = tbl[tab.side + op] * tab.stride * tab.per + tbl[tab.row + op] if all_blocks else 0
        return (block + c, 0)

    lanes, lines = extra_rows(extras[0].shape[1])
    unit = sum(piece.shape[1] for piece in pieces)

    def out_map(c, tbl):
        return (tbl[tab.row + op] + c, tbl[tab.side + op] * (local_width // unit) + lo * 128 // unit)

    in_specs = [pl.BlockSpec((16, lanes), lambda c, tbl: (rows // 16, c))] * tab.t
    in_specs += [
        pl.BlockSpec((BLK, piece.shape[1]), functools.partial(piece_map, piece.shape[0] == tab.chunks * BLK))
        for piece in pieces
    ]
    operands = [table, *extras, *pieces]
    aliases = {}
    if out is not None:
        in_specs.append(pl.BlockSpec(memory_space=pl.ANY))
        operands.append(out)
        aliases = {len(operands) - 1: 0}
    return pl.pallas_call(
        functools.partial(place_kernel, features, tab.t, len(pieces), lanes, lines),
        grid_spec=pltpu.PrefetchScalarGridSpec(
            num_scalar_prefetch=1,
            grid=(tab.per,),
            in_specs=in_specs,
            out_specs=pl.BlockSpec((BLK, unit), out_map),
        ),
        out_shape=jax.ShapeDtypeStruct(shape, BF16),
        input_output_aliases=aliases,
        compiler_params=params(63 * 2**20),
        cost_estimate=pl.CostEstimate(flops=unit, bytes_accessed=unit, transcendentals=0),
        name="place",
    )(*operands)


def place_last_kernel(tab, features, ops, lo, local_width, lanes, lines, table_ref, *refs):
    t, per, count = tab.t, tab.per, len(ops)
    extras, pieces = refs[: count * t], refs[count * t : count * (t + 1)]
    out_ref, extra, block, extra_in, block_in, block_out = refs[-6:]
    unit, rows = block.shape[2], per * BLK
    part = BLK // 2
    moves, fetched, stores = [], [], []
    for j in range(count):
        for c in range(per):
            b = j * per + c
            for k in range(t):
                source = extras[j * t + k].at[pl.ds(rows, 16), pl.ds(c * lanes, lanes)]
                moves.append(pltpu.make_async_copy(source, extra.at[b, k], extra_in.at[b, k]))
                moves[-1].start()
            for half in range(2):
                source = pieces[j].at[pl.ds(c * BLK + half * part, part)]
                target = block.at[b, pl.ds(half * part, part)]
                fetched.append(pltpu.make_async_copy(source, target, block_in.at[b, half]))
                fetched[-1].start()
    for j, op in enumerate(ops):
        row = table_ref[tab.row + op] * BLK
        left = pl.multiple_of(table_ref[tab.side + op] * local_width + lo * 128, 128)
        for c in range(per):
            b = j * per + c
            for k in range(t):
                moves[b * t + k].wait()
            scale = row_scale([extra.at[b, k] for k in range(t)], features, lanes, lines)
            for half in range(2):
                fetched[2 * b + half].wait()
                span = slice(half * part, (half + 1) * part)
                for col in range(0, unit, 128):
                    cols = slice(col, col + 128)
                    block[b, span, cols] = (block[b, span, cols].astype(F32) * scale[span]).astype(BF16)
                top = pl.multiple_of(row + c * BLK + half * part, part)
                target = out_ref.at[pl.ds(top, part), pl.ds(left, unit)]
                source = block.at[b, pl.ds(half * part, part)]
                stores.append(pltpu.make_async_copy(source, target, block_out.at[b, half]))
                stores[-1].start()
    for store in stores:
        store.wait()


def place_last(tab, table, ops, lo, pieces, extras, out, local_width, features):
    lanes, lines = extra_rows(extras[0].shape[1])
    blocks = len(ops) * tab.per
    hbm = pl.BlockSpec(memory_space=pl.ANY)
    operands = [table, *extras, *pieces, out]
    return pl.pallas_call(
        functools.partial(place_last_kernel, tab, features, ops, lo, local_width, lanes, lines),
        in_specs=[pl.BlockSpec(memory_space=pltpu.SMEM)] + [hbm] * (len(operands) - 1),
        out_specs=hbm,
        out_shape=jax.ShapeDtypeStruct(out.shape, BF16),
        scratch_shapes=[
            pltpu.VMEM((blocks, tab.t, 16, lanes), BF16),
            pltpu.VMEM((blocks, BLK, pieces[0].shape[1]), BF16),
            pltpu.SemaphoreType.DMA((blocks, tab.t)),
            pltpu.SemaphoreType.DMA((blocks, 2)),
            pltpu.SemaphoreType.DMA((blocks, 2)),
        ],
        input_output_aliases={len(operands) - 1: 0},
        compiler_params=params(63 * 2**20),
        cost_estimate=pl.CostEstimate(flops=lanes, bytes_accessed=lanes, transcendentals=0),
        name="place_last",
    )(*operands)


def local(query_rows, key_rows, value_rows, gate_rows, decay_log, norm_gain, doc_lengths, block_shard):
    tokens, width = query_rows.shape
    heads = decay_log.shape[0]
    features = norm_gain.shape[0]
    n, t = lax.axis_size("ctx"), lax.axis_size("tp")
    tab = Table(n, t, tokens // BLK)
    quarter = max(1, heads // 4)

    rest = heads - quarter
    rows, cols, docs, total_gate, table, low, full = prelude(
        tab, doc_lengths, block_shard, decay_log, key_rows, value_rows
    )
    gain = norm_gain.reshape(1, features)
    hop = [(i, i + 1) for i in range(n - 1)]

    def route(op):
        return [
            (d * t + k, (d + op + k * tab.stride) % n * t + d // tab.stride)
            for d in range(n)
            for k in range(t)
        ]

    carry = total_gate[:, :1, None]

    def merge(arrived, part):
        return (carry[part] * arrived[part].astype(F32) + full[part]).astype(BF16)

    first, others = slice(rest, heads), slice(0, rest)
    for _ in range(max(1, n // 2) - 2):
        low = merge(lax.ppermute(low, "ctx", hop), slice(0, heads))
    parts = [low[first], low[others]]
    if n // 2 > 1:
        arrived = lax.ppermute(low, "ctx", hop)
        parts = [merge(arrived, first), merge(arrived, others)]
    own = attend_own(
        tab, table, query_rows, key_rows, value_rows, gate_rows, gain, rows, cols, docs, rest, quarter
    )
    parts, own = lax.optimization_barrier((parts, own))
    early, entering = (lax.ppermute(part, "ctx", hop) for part in parts)
    ready, squares = attend_entered(tab, table, own, cols, early, rest, quarter, rows.shape[0] // 3)
    gated = [None]
    for lo, count in ((0, 2 * quarter), (2 * quarter, quarter)):
        outs, squares = attend(
            tab, table, query_rows, key_rows, value_rows, gate_rows, gain, rows, cols, docs,
            entering, 0, lo, count, squares, lo > 0,
        )
        gated.append(outs)
    head = lax.all_to_all(ready, "ctx", split_axis=0, concat_axis=0, tiled=True)
    head = lax.all_to_all(head, "tp", split_axis=0, concat_axis=0, tiled=True).reshape(tokens, -1)
    tail = [lax.ppermute(gated[2][op], ("ctx", "tp"), route(op)) for op in range(n)]
    middle = []
    for op in range(n):
        ready = gated[1][op]
        for before in ([], [0, n - 1])[op] if op < 2 else [op - 1]:
            ready, tail[before] = lax.optimization_barrier((ready, tail[before]))
        middle.append(lax.ppermute(ready, ("ctx", "tp"), route(op)))

    shape = (tokens // t, features)
    out = None

    def extras(op):
        return [tail[(op + k * tab.stride) % n] for k in range(t)]

    for op in range(n):
        out = place(tab, table, op, 2 * quarter, [tail[op], head], extras(op), out, shape, width, features)
    for op in range(n - 2):
        out = place(tab, table, op, 0, [middle[op]], extras(op), out, shape, width, features)
    last = (n - 2, n - 1)
    return place_last(
        tab, table, last, 0, middle[n - 2 :], [extra for op in last for extra in extras(op)], out, width, features
    )


def solution(mesh):
    return jax.shard_map(
        local,
        mesh=mesh,
        in_specs=(
            P(("dp", "ctx"), "tp"),
            P(("dp", "ctx"), "tp"),
            P(("dp", "ctx"), "tp"),
            P(("dp", "ctx"), "tp"),
            P("tp", ("dp", "ctx")),
            P(),
            P("dp"),
            P("dp"),
        ),
        out_specs=P(("dp", "ctx", "tp"), None),
        check_vma=False,
    )
```
